256 devices in a mesh: seq: 128 (over z, x, y_hi, core), rep: 2 (over y_lo).
Axes of the slice: x: 4, y: 4 (y_hi: 2, y_lo: 2; y = y_hi * 2 + y_lo), z: 8, core: 2. Of those that a mesh axis runs over, the one named last changes fastest.
Arguments:
- hidden_in: bfloat16 [2, 16384, 1536], P('rep', 'seq'), may hold values from -24 to 24
- upstream: bfloat16 [2, 16384, 1536], P('rep', 'seq'), may hold values from -6 to 6
- out_weight: bfloat16 [1536, 1536], P(('seq', 'rep')), may hold values from -0.15625 to 0.15625
- conv_kernel: bfloat16 [31, 1536], replicated, may hold values from -1 to 1
- durations: int32 [2, 1024], P('rep', 'seq'), may hold values from 1 to 31, as said below
Outputs:
- frame_grad: bfloat16 [2, 16384, 1536], P('rep', 'seq')
- gloss_grad: float32 [2, 1024, 1536], P('rep', 'seq')
- weight_grad: float32 [1536, 1536], P(('seq', 'rep'))
- kernel_grad: float32 [31, 1536], replicated
The draws below stay inside these ranges and needn't reach their ends.
Inputs may be any that keep to these rules, and one draw needn't show every extreme that they name: In each broadcast the durations sum to 16384. The first frame of a gloss block of 8 rows lies at or after the first frame of the same index's frames and less than 16 frames after it.
All inputs are finite; a program needn't handle non-finite values.
Results may differ from the reference program's by a relative error of at most 0.005.
Values may be sent and summed in bfloat16 or wider, within the bound.
No kernel may reach another device: no remote copies, remote signals or barrier semaphores. Data moves between devices by JAX's collectives and lax.ppermute only.
A program may use at most 64 MiB of HBM per device.

```python
import math
import jax
import jax.numpy as jnp
from jax import lax

D = 1536
KERNEL = 31
TOK_DEV = 128
G_DEV = 8
FRAMES = 16384
GLOSSES = 1024
BROADCASTS = 2


def draw_durations(key, part):
    key = jax.random.fold_in(key, 7)
    mean_len = TOK_DEV // G_DEV
    carry = jax.random.randint(key, (BROADCASTS, GLOSSES), 0, mean_len)
    column = jnp.arange(GLOSSES, dtype=jnp.int32)[None, :]
    carry = jnp.where(column == 0, mean_len - 1, carry)
    carry = jnp.where(column == 1, 0, carry)
    carry = jnp.where(column == GLOSSES - 1, 0, carry)
    previous = jnp.concatenate((jnp.zeros((BROADCASTS, 1), jnp.int32), carry[:, :-1]), axis=1)
    lengths = mean_len + carry - previous
    return lengths.astype(jnp.int32)


def spiked(array, key, source, target, parts, factor):
    def block_of(position):
        return (jnp.arange(array.shape[position]) // (array.shape[position] // parts)).reshape((-1,) + (1,) * (array.ndim - 1 - position))

    one_side = jax.random.permutation(key, parts)[block_of(target)]
    far = (block_of(target) + parts // 2) % parts
    return jnp.where((block_of(source) == one_side) | (block_of(source) == far), factor * array, array)


def level_of(rng, shape, split, least, high):
    factor_of = 1.0
    for position, shards_of in split:
        heights = jax.random.uniform(jax.random.fold_in(jax.random.fold_in(rng, 6), position), (shards_of,), jnp.float32, least / len(split), high / len(split))
        factor_of = factor_of * jnp.repeat(jnp.exp(heights), shape[position] // shards_of).reshape((-1,) + (1,) * (len(shape) - 1 - position))
    return factor_of


def noise(stream_key, shape, width, reach, cuts=(), kind=jnp.bfloat16):
    entries = jax.random.normal(stream_key, shape, jnp.float32) * width
    if len(cuts) > 0:
        entries = level_of(stream_key, shape, cuts, -0.22, 0.18) * entries
    return jnp.clip(entries, min=-reach, max=reach).astype(kind)


def gaussian_with(rng, shape, scale, reach, split, heavy, kind=jnp.bfloat16):
    result = scale * jax.random.normal(rng, shape, jnp.float32)
    if split:
        result = result * level_of(rng, shape, split, -0.22, 0.18)
    return jnp.clip(spiked(result, jax.random.fold_in(rng, 3), *heavy), -reach, reach).astype(kind)


def setup_inputs(seed: int = 0) -> dict:
    splits = jax.random.split(jax.random.key(seed), 6)
    return {
        "hidden_in": gaussian_with(splits[0], (BROADCASTS, FRAMES, D), 1.0, 24.0, ((0, 2), (1, 128)), (1, 2, 128, 5.5)),
        "upstream": noise(splits[1], (BROADCASTS, FRAMES, D), 1.0, 6.0, ((0, 2), (1, 128))),
        "out_weight": noise(splits[2], (D, D), D ** -0.5, 0.15625, ((0, 256),)),
        "conv_kernel": noise(splits[3], (KERNEL, D), 0.2, 1.0),
        "durations": draw_durations(jax.random.fold_in(splits[5], 71), 0),
    }


def reference(hidden_in, upstream, out_weight, conv_kernel, durations):
    half_width = KERNEL // 2
    kernel_f = conv_kernel.astype(jnp.float32)
    scaling = 1.0 / math.sqrt(BROADCASTS * FRAMES)
    weight_total = jnp.zeros((D, D), jnp.float32)
    kernel_total = jnp.zeros((KERNEL, D), jnp.float32)
    input_grads = []
    gloss_grads = []
    for member in range(BROADCASTS):
        frames_in = hidden_in[member]
        grad_out = upstream[member]
        padded = jnp.pad(frames_in, ((half_width, half_width), (0, 0)))
        conv_out = jnp.zeros((FRAMES, D), jnp.float32)
        for kernel_tap in range(KERNEL):
            conv_out = conv_out + kernel_f[kernel_tap] * padded[kernel_tap:kernel_tap + FRAMES].astype(jnp.float32)
        activated = jax.nn.silu(conv_out).astype(jnp.bfloat16)
        grad_act = jnp.dot(grad_out, out_weight.T, preferred_element_type=jnp.float32)
        sigmoid_a = jax.nn.sigmoid(conv_out)
        grad_conv = (grad_act * sigmoid_a * (1.0 + conv_out * (1.0 - sigmoid_a))).astype(jnp.bfloat16)
        weight_total = weight_total + jnp.dot(activated.T, grad_out, preferred_element_type=jnp.float32)
        conv_grad_f = grad_conv.astype(jnp.float32)
        tap_rows = [lax.optimization_barrier(jnp.sum(conv_grad_f * padded[kernel_tap:kernel_tap + FRAMES].astype(jnp.float32), axis=0)) for kernel_tap in range(KERNEL)]
        kernel_total = kernel_total + jnp.stack(tap_rows)
        padded_grad = jnp.pad(grad_conv, ((half_width, half_width), (0, 0)))
        frame_sum = jnp.zeros((FRAMES, D), jnp.float32)
        for kernel_tap in range(KERNEL):
            begin = 2 * half_width - kernel_tap
            frame_sum = frame_sum + kernel_f[kernel_tap] * padded_grad[begin:begin + FRAMES].astype(jnp.float32)
        frame_grad = frame_sum.astype(jnp.bfloat16)
        input_grads.append(frame_grad)
        gloss_ids = jnp.repeat(jnp.arange(GLOSSES, dtype=jnp.int32), durations[member], total_repeat_length=FRAMES)
        gloss_grads.append(jax.ops.segment_sum(frame_grad.astype(jnp.float32), gloss_ids, num_segments=GLOSSES))
    return (jnp.stack(input_grads), jnp.stack(gloss_grads), weight_total * scaling, kernel_total * scaling)
```

```python
import math

import jax
import jax.numpy as jnp
import numpy as np
from jax import lax
from jax.sharding import Mesh
from jax.sharding import PartitionSpec as P

AXES = ("z", "x", "yh", "core", "rep")
SIZES = (8, 4, 2, 2, 2)
GROUP = ("yh", "core")
PLANE = ("x", "rep")
QUARTERS = 4
BLOCK = 6
PAD = 56
LEFT_H, RIGHT_H = 32, 48
LEFT_U, RIGHT_U = 16, 32
SWAP = [(0, 1), (1, 0)]
BF = jnp.bfloat16
F32 = jnp.float32


def placement():
    out = np.zeros((384, 8 * PAD), np.float32)
    for zl in range(2):
        for x in range(4):
            for q in range(4):
                for rep in range(2):
                    for r in range(BLOCK):
                        row = (((zl * 4 + x) * 4 + q) * 2 + rep) * BLOCK + r
                        out[row, (x * 2 + rep) * PAD + (q * 2 + zl) * BLOCK + r] = 1
    return out


def turned():
    pairs = []
    for zq in range(4):
        for zl in range(2):
            for q in range(4):
                pairs.append(((zq * 2 + zl) * 4 + q, (q * 2 + zl) * 4 + zq))
    return pairs


def ordered(mine, other, first):
    return jnp.where(first, jnp.stack((mine, other)), jnp.stack((other, mine)))


def half(value, index, axis):
    size = value.shape[axis] // 2
    return lax.dynamic_slice_in_dim(value, index * size, size, axis)


def split_out(value, axis, dim, index):
    got = lax.ppermute(half(value, 1 - index, dim), axis, SWAP)
    return ordered(half(value, index, dim), got, index == 0)


def body(hidden_in, upstream, out_weight, conv_kernel, durations):
    taps = conv_kernel.shape[0]
    width = taps // 2
    yh, core = lax.axis_index("yh"), lax.axis_index("core")
    rep = lax.axis_index("rep")
    quarter = yh * 2 + core
    place = lax.axis_index("z") * 4 + lax.axis_index("x")
    frames = 4 * hidden_in.shape[1]
    scaling = 1.0 / math.sqrt(2 * 128 * hidden_in.shape[1])
    channels = 384

    lengths = ordered(durations[0], lax.ppermute(durations[0], "yh", SWAP), yh == 0)
    lengths = jnp.swapaxes(
        ordered(lengths, lax.ppermute(lengths, "core", SWAP), core == 0), 0, 1
    ).reshape(4, -1)
    totals = jnp.sum(lengths, axis=1)

    rows = lax.ppermute(out_weight, ("z", "yh", "core"), turned())
    note = jnp.zeros((2, 1536), BF).at[0, :4].set(totals.astype(BF))
    rows = jnp.concatenate((rows, note), axis=0)
    rows = lax.all_to_all(
        jnp.broadcast_to(rows[None], (8,) + rows.shape), "z", 0, 0, tiled=True
    )
    note = jnp.zeros((PAD - 48, 1536), BF).at[0, :32].set(rows[:, 6, :4].reshape(32))
    rows = jnp.concatenate((rows[:, :BLOCK].reshape(48, 1536), note), axis=0)
    rows = lax.all_to_all(
        jnp.broadcast_to(rows[None], (8,) + rows.shape), PLANE, 0, 0, tiled=True
    )
    notes = rows[:, 48, :32].reshape(4, 2, 8, 4).astype(F32)
    notes = jnp.where(rep == 0, notes[:, 0], notes[:, 1])
    spread = jnp.asarray(placement(), BF)
    weights = jnp.dot(
        spread, rows.reshape(8 * PAD, 1536), preferred_element_type=F32
    ).astype(BF)

    hidden = split_out(hidden_in[0], "yh", 1, yh)
    hidden = split_out(hidden, "core", 2, core)
    hidden = jnp.swapaxes(hidden, 0, 1).reshape(frames, channels)
    grads = ordered(upstream[0], lax.ppermute(upstream[0], "yh", SWAP), yh == 0)
    grads = ordered(grads, lax.ppermute(grads, "core", SWAP), core == 0)
    grads = jnp.swapaxes(grads, 0, 1).reshape(frames, 1536)
    forward = [(i, i + 1) for i in range(31)]
    backward = [(i + 1, i) for i in range(31)]
    ring = ("z", "x")
    hidden_ext = jnp.concatenate(
        (
            lax.ppermute(hidden[-LEFT_H:], ring, forward),
            hidden,
            lax.ppermute(hidden[:RIGHT_H], ring, backward),
        )
    ).astype(F32)
    grads_ext = jnp.concatenate(
        (
            lax.ppermute(grads[-LEFT_U:], ring, forward),
            grads,
            lax.ppermute(grads[:RIGHT_U], ring, backward),
        )
    )
    kernel_f = lax.dynamic_slice_in_dim(
        conv_kernel, quarter * channels, channels, 1
    ).astype(F32)

    wide = frames + LEFT_U + RIGHT_U
    conv_out = jnp.zeros((wide, channels), F32)
    for k in range(taps):
        begin = LEFT_H - LEFT_U + k - width
        conv_out = conv_out + kernel_f[k] * hidden_ext[begin : begin + wide]
    sig = jax.nn.sigmoid(conv_out)
    activated = (conv_out * sig)[LEFT_U : LEFT_U + frames].astype(BF)
    slope = sig * (1.0 + conv_out * (1.0 - sig))
    activated = jnp.dot(activated, spread, preferred_element_type=F32).astype(BF)
    weight_part = lax.dot_general(
        activated, grads, (((0,), (0,)), ((), ())), preferred_element_type=F32
    ).astype(BF)

    grad_act = lax.dot_general(
        grads_ext, weights, (((1,), (1,)), ((), ())), preferred_element_type=F32
    )
    grad_conv = (grad_act * slope).astype(BF).astype(F32)
    longer = frames + 16
    frame_sum = jnp.zeros((longer, channels), F32)
    for k in range(taps):
        begin = LEFT_U + width - k
        frame_sum = frame_sum + kernel_f[k] * grad_conv[begin : begin + longer]
    frame_grad = frame_sum.astype(BF)
    own_grad = grad_conv[LEFT_U : LEFT_U + frames]
    tap_rows = [
        jnp.sum(
            own_grad * hidden_ext[LEFT_H + k - width : LEFT_H + k - width + frames],
            axis=0,
        )
        for k in range(taps)
    ]
    tap_rows = jnp.stack(tap_rows + [jnp.zeros_like(tap_rows[0])]).reshape(8, 1536)

    high = tap_rows.astype(BF)
    low = (tap_rows - high.astype(F32)).astype(BF)
    parts = weight_part.reshape(8, PAD, 1536)
    parts = jnp.concatenate(
        (parts[:, :48], high[:, None], low[:, None], parts[:, 50:]), axis=1
    )
    parts = lax.all_to_all(parts, PLANE, 0, 0, tiled=True)
    parts = jnp.sum(parts.astype(F32), axis=0)
    taps_part = parts[48] + parts[49]
    high = taps_part.astype(BF)
    low = (taps_part - high.astype(F32)).astype(BF)
    parts = jnp.concatenate(
        (
            parts[:48].astype(BF).reshape(8, BLOCK, 1536),
            jnp.broadcast_to(high, (8, 1, 1536)),
            jnp.broadcast_to(low, (8, 1, 1536)),
        ),
        axis=1,
    )
    parts = lax.all_to_all(parts, "z", 0, 0, tiled=True)
    parts = jnp.sum(parts.astype(F32), axis=0) * scaling
    weight_grad = lax.ppermute(
        parts[:BLOCK], ("z", "yh", "core"), [(b, a) for a, b in turned()]
    )
    taps_sum = (parts[6] + parts[7])[None]
    taps_all = lax.all_to_all(
        jnp.broadcast_to(taps_sum, (32, 1536)), ("x", "yh", "core", "rep"), 0, 0, tiled=True
    )
    taps_all = taps_all.reshape(4, 4, 2, 4, channels)
    kernel_grad = taps_all.transpose(0, 2, 3, 1, 4).reshape(32, 1536)[:taps]

    order = lax.iota(jnp.int32, 8)[None, :] * 4 + lax.iota(jnp.int32, 4)[:, None]
    before = jnp.sum(jnp.where(order < place, jnp.sum(notes, axis=2), 0.0))
    start = before.astype(jnp.int32) - place * frames
    ends = start + jnp.cumsum(lengths.reshape(-1))
    starts = ends - lengths.reshape(-1)
    at = lax.iota(jnp.int32, longer)
    covers = (at[None] >= starts[:, None]) & (at[None] < ends[:, None])
    gloss = jnp.dot(covers.astype(BF), frame_grad, preferred_element_type=F32)

    def back(value):
        value = value.reshape(2, 2, -1, channels)
        kept = lax.dynamic_index_in_dim(value, core, 1, False)
        got = lax.ppermute(
            lax.dynamic_index_in_dim(value, 1 - core, 1, False), "core", SWAP
        )
        value = jnp.where(
            core == 0,
            jnp.concatenate((kept, got), axis=2),
            jnp.concatenate((got, kept), axis=2),
        )
        kept = lax.dynamic_index_in_dim(value, yh, 0, False)
        got = lax.ppermute(
            lax.dynamic_index_in_dim(value, 1 - yh, 0, False), "yh", SWAP
        )
        return jnp.where(
            yh == 0,
            jnp.concatenate((kept, got), axis=1),
            jnp.concatenate((got, kept), axis=1),
        )

    return (
        back(frame_grad[:frames])[None],
        back(gloss)[None],
        weight_grad,
        kernel_grad,
    )


def solution(mesh):
    fine = Mesh(mesh.devices.reshape(SIZES), AXES)
    seq = ("z", "x", "yh", "core")
    rows = P(seq + ("rep",), None)
    in_specs = (P("rep", seq, None), P("rep", seq, None), rows, P(), P("rep", seq))
    out_specs = (P("rep", seq, None), P("rep", seq, None), rows, P())
    return jax.shard_map(
        body, mesh=fine, in_specs=in_specs, out_specs=out_specs, check_vma=False
    )
```

```python
import math

import jax
import jax.numpy as jnp
import numpy as np
from jax import lax
from jax.experimental import pallas as pl
from jax.experimental.pallas import tpu as pltpu
from jax.sharding import Mesh
from jax.sharding import PartitionSpec as P

AXES = ("z", "x", "yh", "core", "rep")
SIZES = (8, 4, 2, 2, 2)
GROUP = ("yh", "core")
PLANE = ("x", "rep")
QUARTERS = 4
BLOCK = 6
PAD = 56
LEFT_H, RIGHT_H = 32, 48
LEFT_U, RIGHT_U = 16, 32
FRAMES, CHANNELS, TAPS = 512, 384, 31
WIDE = FRAMES + LEFT_U + RIGHT_U
LONG = FRAMES + 16
SWAP = [(0, 1), (1, 0)]
BF = jnp.bfloat16
F32 = jnp.float32


def placement(pad):
    out = np.zeros((CHANNELS, 8 * pad), np.float32)
    for zl in range(2):
        for x in range(4):
            for q in range(4):
                for rep in range(2):
                    for r in range(BLOCK):
                        row = (((zl * 4 + x) * 4 + q) * 2 + rep) * BLOCK + r
                        out[row, (x * 2 + rep) * pad + (q * 2 + zl) * BLOCK + r] = 1
    return jnp.asarray(out, BF)


def turned():
    pairs = []
    for zq in range(4):
        for zl in range(2):
            for q in range(4):
                pairs.append(((zq * 2 + zl) * 4 + q, (q * 2 + zl) * 4 + zq))
    return pairs


def ordered(mine, other, first):
    return jnp.where(first, jnp.stack((mine, other)), jnp.stack((other, mine)))


def half(value, index, axis):
    size = value.shape[axis] // 2
    return lax.dynamic_slice_in_dim(value, index * size, size, axis)


def lanes(tile):
    return slice(tile * 128, tile * 128 + 128)


def assemble(hidden, upstream, across, beside, out):
    yh, core = lax.axis_index("yh"), lax.axis_index("core")
    quarter = pl.ds(pl.multiple_of((yh * 2 + core) * CHANNELS, 128), CHANNELS)
    part = pl.ds(pl.multiple_of(core * CHANNELS, 128), CHANNELS)
    own = yh * 2 + core
    out[own, :, :CHANNELS] = hidden[:, quarter]
    out[own, :, CHANNELS:] = upstream[...]
    far = (1 - yh) * 2 + core
    out[far, :, :CHANNELS] = across[:, part]
    out[far, :, CHANNELS:] = across[:, 2 * CHANNELS :]
    out[yh * 2 + 1 - core] = beside[0]
    out[(1 - yh) * 2 + 1 - core] = beside[1]


def convolve(frames, left, right, kernel, order, slope, hidden, parts, active):
    hidden[:LEFT_H] = left[:, :CHANNELS].astype(F32)
    hidden[LEFT_H : LEFT_H + FRAMES] = frames[:, :CHANNELS].astype(F32)
    hidden[LEFT_H + FRAMES :] = right[:, :CHANNELS].astype(F32)
    rows = 80
    for tile in range(CHANNELS // 128):

        def chunk(c, _, tile=tile):
            base = pl.multiple_of(c * rows, 8)
            total = jnp.zeros((rows, 128), F32)
            window = hidden[pl.ds(base, rows + 32), lanes(tile)]
            for b in range(8):
                slab = window[b : b + rows + 24]
                for a in range(4):
                    k = 8 * a + b - 1
                    if 0 <= k < TAPS:
                        total += kernel[k : k + 1, lanes(tile)] * slab[8 * a : 8 * a + rows]
            sig = jax.nn.sigmoid(total)
            slope[pl.ds(base, rows), lanes(tile)] = sig * (1.0 + total * (1.0 - sig))
            active[pl.ds(base, rows), lanes(tile)] = total * sig
            return 0

        lax.fori_loop(0, WIDE // rows, chunk, 0)
    acts = active[LEFT_U : LEFT_U + FRAMES].astype(BF)
    acts = jnp.dot(acts, order[...], preferred_element_type=F32).astype(BF)
    product = lax.dot_general(
        acts,
        frames[:, CHANNELS:],
        (((0,), (0,)), ((), ())),
        preferred_element_type=F32,
    ).astype(BF)
    for s in range(8):
        parts[s] = product[48 * s : 48 * s + 48]


def backward(
    gathered, spread, frames, left, right, slope, hidden, kernel,
    frame_grad, taps, grad_conv, frame_sum, sums,
):
    weights = jnp.dot(spread[...], gathered[...], preferred_element_type=F32).astype(BF)

    def gradient(upstream, begin, count):
        value = lax.dot_general(
            upstream, weights, (((1,), (1,)), ((), ())), preferred_element_type=F32
        )
        value = (value * slope[begin : begin + count]).astype(BF)
        grad_conv[begin : begin + count] = value.astype(F32)

    gradient(left[LEFT_H - LEFT_U :, CHANNELS:], 0, LEFT_U)
    gradient(frames[:, CHANNELS:], LEFT_U, FRAMES)
    gradient(right[:RIGHT_U, CHANNELS:], LEFT_U + FRAMES, RIGHT_U)
    rows, span = 88, 128
    sums[...] = jnp.zeros_like(sums)
    for tile in range(CHANNELS // 128):

        def chunk(c, _, tile=tile):
            base = pl.multiple_of(c * rows, 8)
            total = jnp.zeros((rows, 128), F32)
            window = grad_conv[pl.ds(base, rows + 32), lanes(tile)]
            for b in range(8):
                slab = window[b : b + rows + 24]
                for a in range(4):
                    k = TAPS - 8 * a - b
                    if 0 <= k < TAPS:
                        total += kernel[k : k + 1, lanes(tile)] * slab[8 * a : 8 * a + rows]
            frame_sum[pl.ds(base, rows), lanes(tile)] = total
            return 0

        lax.fori_loop(0, LONG // rows, chunk, 0)

        def piece(c, _, tile=tile):
            base = pl.multiple_of(c * span, 8)
            grads = grad_conv[pl.ds(base + LEFT_U, span), lanes(tile)]
            window = hidden[pl.ds(base + LEFT_U, span + 32), lanes(tile)]
            for b in range(8):
                slab = window[b : b + span + 24]
                for a in range(4):
                    k = 8 * a + b - 1
                    if 0 <= k < TAPS:
                        terms = grads * slab[8 * a : 8 * a + span]
                        sums[k, :, lanes(tile)] += jnp.sum(
                            terms.reshape(span // 8, 8, 128), axis=0
                        )
            return 0

        lax.fori_loop(0, FRAMES // span, piece, 0)
    frame_grad[...] = frame_sum[...].astype(BF)
    for k in range(TAPS + 1):
        at = (k % 4) * CHANNELS
        taps[k // 4 : k // 4 + 1, at : at + CHANNELS] = jnp.sum(sums[k], axis=0, keepdims=True)


def call(kernel, outs, scratch, flops, *args):
    shapes = [jax.ShapeDtypeStruct(shape, dtype) for shape, dtype in outs]
    size = sum(math.prod(s.shape) * s.dtype.itemsize for s in list(args) + shapes)
    return pl.pallas_call(
        kernel,
        out_shape=shapes,
        scratch_shapes=[pltpu.VMEM(shape, dtype) for shape, dtype in scratch],
        compiler_params=pltpu.CompilerParams(vmem_limit_bytes=40 * 2**20),
        cost_estimate=pl.CostEstimate(
            flops=flops, bytes_accessed=size, transcendentals=0
        ),
    )(*args)


def body(hidden_in, upstream, out_weight, conv_kernel, durations):
    yh, core = lax.axis_index("yh"), lax.axis_index("core")
    rep = lax.axis_index("rep")
    quarter = yh * 2 + core
    place = lax.axis_index("z") * 4 + lax.axis_index("x")
    scaling = 1.0 / math.sqrt(2 * 128 * hidden_in.shape[1])

    lengths = ordered(durations[0], lax.ppermute(durations[0], "yh", SWAP), yh == 0)
    lengths = jnp.swapaxes(
        ordered(lengths, lax.ppermute(lengths, "core", SWAP), core == 0), 0, 1
    ).reshape(4, -1)
    totals = jnp.sum(lengths, axis=1)

    rows = lax.ppermute(out_weight, ("z", "yh", "core"), turned())
    note = jnp.zeros((2, 1536), BF).at[0, :4].set(totals.astype(BF))
    rows = jnp.concatenate((rows, note), axis=0)
    rows = lax.all_to_all(
        jnp.broadcast_to(rows[None], (8,) + rows.shape), "z", 0, 0, tiled=True
    )
    note = jnp.zeros((PAD - 48, 1536), BF).at[0, :32].set(rows[:, 6, :4].reshape(32))
    rows = jnp.concatenate((rows[:, :BLOCK].reshape(48, 1536), note), axis=0)
    rows = lax.all_to_all(
        jnp.broadcast_to(rows[None], (8,) + rows.shape), PLANE, 0, 0, tiled=True
    )
    notes = rows[:, 48, :32].reshape(4, 2, 8, 4).astype(F32)
    notes = jnp.where(rep == 0, notes[:, 0], notes[:, 1])

    hidden, grads = hidden_in[0], upstream[0]
    across = jnp.concatenate((half(hidden, 1 - yh, 1), grads), axis=1)
    across = lax.ppermute(across, "yh", SWAP)
    beside = jnp.stack(
        (
            jnp.concatenate((half(half(hidden, yh, 1), 1 - core, 1), grads), axis=1),
            jnp.concatenate(
                (half(across[:, : 2 * CHANNELS], 1 - core, 1), across[:, 2 * CHANNELS :]),
                axis=1,
            ),
        )
    )
    beside = lax.ppermute(beside, "core", SWAP)
    [frames] = call(
        assemble, [((4, 128, CHANNELS + 1536), BF)], [], 0, hidden, grads, across, beside
    )
    frames = frames.reshape(FRAMES, CHANNELS + 1536)
    ring = ("z", "x")
    left = lax.ppermute(frames[-LEFT_H:], ring, [(i, i + 1) for i in range(31)])
    right = lax.ppermute(frames[:RIGHT_H], ring, [(i + 1, i) for i in range(31)])
    kernel_f = lax.dynamic_slice_in_dim(
        jnp.pad(conv_kernel, ((0, 1), (0, 0))), quarter * CHANNELS, CHANNELS, 1
    ).astype(F32)

    slope, hidden_f, parts = call(
        convolve,
        [((WIDE, CHANNELS), F32), ((LEFT_H + FRAMES + RIGHT_H, CHANNELS), F32), ((8, 48, 1536), BF)],
        [((WIDE, CHANNELS), F32)],
        800_000_000,
        frames, left, right, kernel_f, placement(48),
    )
    parts = lax.all_to_all(parts, PLANE, 0, 0, tiled=True)
    parts = jnp.sum(parts.astype(F32), axis=0).astype(BF)

    frame_grad, tap_rows = call(
        backward,
        [((LONG, CHANNELS), BF), ((8, 1536), F32)],
        [((WIDE, CHANNELS), F32), ((LONG, CHANNELS), F32), ((TAPS + 1, 8, CHANNELS), F32)],
        1_400_000_000,
        rows.reshape(8 * PAD, 1536), placement(PAD), frames, left, right, slope, hidden_f, kernel_f,
    )

    taps_part = lax.all_to_all(tap_rows, PLANE, 0, 0, tiled=True)
    taps_part = jnp.sum(taps_part, axis=0)
    high = taps_part.astype(BF)
    low = (taps_part - high.astype(F32)).astype(BF)
    parts = jnp.concatenate(
        (
            parts.reshape(8, BLOCK, 1536),
            jnp.broadcast_to(high, (8, 1, 1536)),
            jnp.broadcast_to(low, (8, 1, 1536)),
        ),
        axis=1,
    )
    parts = lax.all_to_all(parts, "z", 0, 0, tiled=True)
    parts = jnp.sum(parts.astype(F32), axis=0) * scaling
    weight_grad = lax.ppermute(
        parts[:BLOCK], ("z", "yh", "core"), [(b, a) for a, b in turned()]
    )
    taps_sum = (parts[6] + parts[7])[None]
    taps_all = lax.all_to_all(
        jnp.broadcast_to(taps_sum, (32, 1536)), ("x", "yh", "core", "rep"), 0, 0, tiled=True
    )
    taps_all = taps_all.reshape(4, 4, 2, 4, CHANNELS)
    kernel_grad = taps_all.transpose(0, 2, 3, 1, 4).reshape(32, 1536)[:TAPS]

    order = lax.iota(jnp.int32, 8)[None, :] * 4 + lax.iota(jnp.int32, 4)[:, None]
    before = jnp.sum(jnp.where(order < place, jnp.sum(notes, axis=2), 0.0))
    start = before.astype(jnp.int32) - place * FRAMES
    ends = start + jnp.cumsum(lengths.reshape(-1))
    starts = ends - lengths.reshape(-1)
    at = lax.iota(jnp.int32, LONG)
    covers = (at[None] >= starts[:, None]) & (at[None] < ends[:, None])
    gloss = jnp.dot(covers.astype(BF), frame_grad, preferred_element_type=F32)

    def back(value):
        value = value.reshape(2, 2, -1, CHANNELS)
        kept = lax.dynamic_index_in_dim(value, core, 1, False)
        got = lax.ppermute(
            lax.dynamic_index_in_dim(value, 1 - core, 1, False), "core", SWAP
        )
        value = jnp.where(
            core == 0,
            jnp.concatenate((kept, got), axis=2),
            jnp.concatenate((got, kept), axis=2),
        )
        kept = lax.dynamic_index_in_dim(value, yh, 0, False)
        got = lax.ppermute(
            lax.dynamic_index_in_dim(value, 1 - yh, 0, False), "yh", SWAP
        )
        return jnp.where(
            yh == 0,
            jnp.concatenate((kept, got), axis=1),
            jnp.concatenate((got, kept), axis=1),
        )

    return (
        back(frame_grad[:FRAMES])[None],
        back(gloss)[None],
        weight_grad,
        kernel_grad,
    )


def solution(mesh):
    fine = Mesh(mesh.devices.reshape(SIZES), AXES)
    seq = ("z", "x", "yh", "core")
    rows = P(seq + ("rep",), None)
    in_specs = (P("rep", seq, None), P("rep", seq, None), rows, P(), P("rep", seq))
    out_specs = (P("rep", seq, None), P("rep", seq, None), rows, P())
    return jax.shard_map(
        body, mesh=fine, in_specs=in_specs, out_specs=out_specs, check_vma=False
    )
```

```python
import math

import jax
import jax.numpy as jnp
import numpy as np
from jax import lax
from jax.experimental import pallas as pl
from jax.experimental.pallas import tpu as pltpu
from jax.sharding import Mesh
from jax.sharding import PartitionSpec as P

AXES = ("z", "x", "yh", "core", "rep")
SIZES = (8, 4, 2, 2, 2)
GROUP = ("yh", "core")
PLANE = ("x", "rep")
QUARTERS = 4
BLOCK = 6
PLANE_ROWS = 48
EXTRA = 128
EDGE, AFTER = 16, 32
FRAMES, CHANNELS, TAPS = 512, 384, 31
LONG = FRAMES + EDGE
SWAP = [(0, 1), (1, 0)]
BF = jnp.bfloat16
F32 = jnp.float32


def placement():
    out = np.zeros((CHANNELS, CHANNELS), np.float32)
    for zl in range(2):
        for x in range(4):
            for q in range(4):
                for rep in range(2):
                    for r in range(BLOCK):
                        row = (((zl * 4 + x) * 4 + q) * 2 + rep) * BLOCK + r
                        out[row, (x * 2 + rep) * PLANE_ROWS + (q * 2 + zl) * BLOCK + r] = 1
    return jnp.asarray(out, BF)


def turned():
    pairs = []
    for zq in range(4):
        for zl in range(2):
            for q in range(4):
                pairs.append(((zq * 2 + zl) * 4 + q, (q * 2 + zl) * 4 + zq))
    return pairs


def ordered(mine, other, first):
    return jnp.where(first, jnp.stack((mine, other)), jnp.stack((other, mine)))


def half(value, index, axis):
    size = value.shape[axis] // 2
    return lax.dynamic_slice_in_dim(value, index * size, size, axis)


def lanes(tile):
    return slice(tile * 128, tile * 128 + 128)


def begin(pairs, sems):
    copies = [pltpu.make_async_copy(a, b, sems.at[i]) for i, (a, b) in enumerate(pairs)]
    for copy in copies:
        copy.start()
    return copies


def finish(copies):
    for copy in copies:
        copy.wait()


def spread(weights, durations, slot, out, got, lengths, block, sems):
    finish(begin([(weights, got), (durations, lengths)], sems))
    lane = lax.broadcasted_iota(jnp.int32, (1, 1536), 1)
    total = jnp.sum(lengths[...].astype(F32), axis=1, keepdims=True)
    note = jnp.where(lane == lax.axis_index("z"), jnp.broadcast_to(total, (1, 1536)), 0.0)
    rows = [got[...].astype(F32), note, jnp.zeros((1, 1536), F32)]
    block[...] = jnp.concatenate(rows, axis=0).astype(BF)
    finish(begin([(block, out.at[peer]) for peer in range(8)], sems))


def pack(gathered, slot, across, upstream, plane, rows, got, block, sems):
    finish(begin([(gathered, got)], sems))
    note = jnp.zeros((8, EXTRA), F32)
    for z in range(8):
        block_z = got[z].astype(F32)
        rows[BLOCK * z : BLOCK * z + BLOCK] = block_z[:BLOCK]
        note += jnp.broadcast_to(block_z[BLOCK : BLOCK + 1, :EXTRA], (8, EXTRA))
    block[:, :1536] = rows[...].astype(BF)
    block[:, 1536:] = jnp.concatenate([note] * (PLANE_ROWS // 8), axis=0).astype(BF)
    finish(begin([(block, plane.at[peer]) for peer in range(8)], sems))


def group_grads(sources, grads):
    yh, core = lax.axis_index("yh"), lax.axis_index("core")
    places = [yh * 2 + core, 2 - 2 * yh + core, yh * 2 + 1 - core, 3 - 2 * yh - core]
    return [(source, grads.at[place]) for source, place in zip(sources, places)]


def convolve(
    own, slot, across, slot_across, beside, up_0, up_1, up_2, up_3, kernel, order, slope, hidden, parts,
    grads, frames, weights, turn, v_slope, v_hidden, v_parts, active, sems,
):
    yh, core = lax.axis_index("yh"), lax.axis_index("core")
    part = pl.ds(pl.multiple_of(core * CHANNELS, 128), CHANNELS)
    mine = pl.ds(pl.multiple_of((yh * 2 + core) * CHANNELS, 128), CHANNELS)
    needed = begin(
        [
            (own.at[:, mine], frames.at[yh * 2 + core, pl.ds(0, 128)]),
            (slot.at[:, mine], frames.at[yh * 2 + core, pl.ds(128, EDGE)]),
            (across.at[:, part], frames.at[(1 - yh) * 2 + core, pl.ds(0, 128)]),
            (slot_across.at[:, part], frames.at[(1 - yh) * 2 + core, pl.ds(128, EDGE)]),
            (beside.at[0], frames.at[yh * 2 + 1 - core]),
            (beside.at[1], frames.at[(1 - yh) * 2 + 1 - core]),
            (kernel, weights),
        ],
        sems,
    )
    later = begin(
        group_grads((up_0, up_1, up_2, up_3), grads) + [(order, turn)], sems.at[pl.ds(8, 5)]
    )
    finish(needed)
    v_hidden[:EDGE] = frames[0, 128:].astype(F32)
    for b in range(4):
        v_hidden[EDGE + 128 * b : EDGE + 128 * b + 128] = frames[b, :128].astype(F32)
    v_hidden[EDGE + FRAMES :] = frames[3, 128:].astype(F32)
    rows = 128
    for tile in range(CHANNELS // 128):

        def chunk(c, _, tile=tile):
            base = pl.multiple_of(c * rows, 8)
            total = jnp.zeros((rows, 128), F32)
            window = v_hidden[pl.ds(base, rows + 32), lanes(tile)]
            for b in range(8):
                slab = window[b : b + rows + 24]
                for a in range(4):
                    k = 8 * a + b - 1
                    if 0 <= k < TAPS:
                        total += weights[k : k + 1, lanes(tile)] * slab[8 * a : 8 * a + rows]
            sig = jax.nn.sigmoid(total)
            v_slope[pl.ds(base, rows), lanes(tile)] = sig * (1.0 + total * (1.0 - sig))
            active[pl.ds(base, rows), lanes(tile)] = total * sig
            return 0

        lax.fori_loop(0, FRAMES // rows, chunk, 0)
    out = begin([(v_slope, slope), (v_hidden, hidden)], sems)
    finish(later)
    acts = active[...].astype(BF)
    acts = jnp.dot(acts, turn[...], preferred_element_type=F32).astype(BF)
    product = lax.dot_general(
        acts,
        grads[...].reshape(FRAMES, 1536),
        (((0,), (0,)), ((), ())),
        preferred_element_type=F32,
    ).astype(BF)
    for s in range(8):
        v_parts[s] = product[PLANE_ROWS * s : PLANE_ROWS * (s + 1)]
    finish(begin([(v_parts, parts.at[:, :, pl.ds(0, 1536)])], sems.at[pl.ds(2, 1)]))
    finish(out)


def backward(
    gathered, spread, up_0, up_1, up_2, up_3, slope, hidden, parts,
    grad_conv, head, tail, message,
    got, turn, grads, v_slope, v_hidden, v_grad, v_grad_f, v_taps, sums, sems,
):
    needed = begin(
        [(gathered.at[s, :, pl.ds(0, 1536)], got.at[s]) for s in range(8)]
        + [(spread, turn)],
        sems,
    )
    later = begin(group_grads((up_0, up_1, up_2, up_3), grads), sems.at[pl.ds(9, 4)])
    last = begin([(slope, v_slope), (hidden, v_hidden)], sems.at[pl.ds(13, 2)])
    finish(needed)
    weights = jnp.dot(
        turn[...], got[...].reshape(CHANNELS, 1536), preferred_element_type=F32
    ).astype(BF)
    finish(later)
    value = lax.dot_general(
        grads[...].reshape(FRAMES, 1536),
        weights,
        (((1,), (1,)), ((), ())),
        preferred_element_type=F32,
    )
    finish(last)
    value = (value * v_slope[...]).astype(BF)
    v_grad[...] = value
    v_grad_f[...] = value.astype(F32)
    out = begin(
        [
            (v_grad, grad_conv),
            (v_grad.at[pl.ds(0, AFTER)], head),
            (v_grad.at[pl.ds(FRAMES - EDGE, EDGE)], tail),
        ],
        sems,
    )
    span = 128
    sums[...] = jnp.zeros_like(sums)
    for tile in range(CHANNELS // 128):

        def piece(c, _, tile=tile):
            base = pl.multiple_of(c * span, 8)
            terms = v_grad_f[pl.ds(base, span), lanes(tile)]
            window = v_hidden[pl.ds(base, span + 32), lanes(tile)]
            for b in range(8):
                slab = window[b : b + span + 24]
                for a in range(4):
                    k = 8 * a + b - 1
                    if 0 <= k < TAPS:
                        sums[k, :, lanes(tile)] += jnp.sum(
                            (terms * slab[8 * a : 8 * a + span]).reshape(span // 8, 8, 128),
                            axis=0,
                        )
            return 0

        lax.fori_loop(0, FRAMES // span, piece, 0)
    for s in range(8):
        rows = [
            jnp.sum(sums[4 * s + t, :, lanes(tile)], axis=0, keepdims=True)
            for t in range(4)
            for tile in range(CHANNELS // 128)
        ]
        rows = jnp.concatenate(rows, axis=0)
        high = rows.astype(BF).astype(F32)
        rows = [high, rows - high, jnp.zeros((PLANE_ROWS - 24, 128), F32)]
        v_taps[s] = jnp.concatenate(rows, axis=0).astype(BF)
    finish(begin([(v_taps, message.at[:, :, pl.ds(1536, EXTRA)])], sems.at[pl.ds(3, 1)]))
    finish(out)


def transposed(
    grad_conv, before, after, kernel, frame_grad, v_grad, edge, rest, weights, wide, total_f, v_out, sems,
):
    finish(
        begin([(grad_conv, v_grad), (before, edge), (after, rest), (kernel, weights)], sems)
    )
    wide[:EDGE] = edge[...].astype(F32)
    wide[EDGE : EDGE + FRAMES] = v_grad[...].astype(F32)
    wide[EDGE + FRAMES :] = rest[...].astype(F32)
    rows = 88
    for tile in range(CHANNELS // 128):

        def chunk(c, _, tile=tile):
            base = pl.multiple_of(c * rows, 8)
            total = jnp.zeros((rows, 128), F32)
            window = wide[pl.ds(base, rows + 32), lanes(tile)]
            for b in range(8):
                slab = window[b : b + rows + 24]
                for a in range(4):
                    k = TAPS - 8 * a - b
                    if 0 <= k < TAPS:
                        total += weights[k : k + 1, lanes(tile)] * slab[8 * a : 8 * a + rows]
            total_f[pl.ds(base, rows), lanes(tile)] = total
            return 0

        lax.fori_loop(0, LONG // rows, chunk, 0)
    v_out[...] = total_f[...].astype(BF)
    finish(begin([(v_out, frame_grad)], sems))


def pack_z(parts, out, v_parts, v_sum, v_out, sems):
    finish(begin([(parts, v_parts)], sems))
    v_sum[...] = jnp.sum(v_parts[...].astype(F32), axis=0)
    taps = v_sum[:12, 1536:] + v_sum[12:24, 1536:]
    taps = jnp.concatenate([taps[j : j + 1] for j in range(12)], axis=1)
    high = taps.astype(BF).astype(F32)
    for z in range(8):
        rows = [v_sum[BLOCK * z : BLOCK * z + BLOCK, :1536], high, taps - high]
        v_out[z] = jnp.concatenate(rows, axis=0).astype(BF)
    finish(begin([(v_out, out)], sems))


def unpack_z(got, weights, taps, v_got, v_weights, v_taps, sems):
    finish(begin([(got, v_got)], sems))
    total = v_got[0].astype(F32)
    for z in range(1, 8):
        total += v_got[z].astype(F32)
    total = total * (1.0 / math.sqrt(2 * 16384))
    v_weights[...] = total[:BLOCK]
    for peer in range(32):
        v_taps[peer] = total[6:7] + total[7:8]
    finish(begin([(v_taps, taps), (v_weights, weights)], sems))


def arrange(got, out, v_got, v_out, sems):
    finish(begin([(got, v_got)], sems))
    for x in range(4):
        for q in range(4):
            for rep in range(2):
                for t in range(4):
                    k = (x * 2 + rep) * 4 + t
                    if k < TAPS:
                        v_out[k : k + 1, q * CHANNELS : q * CHANNELS + CHANNELS] = v_got[
                            (x * 4 + q) * 2 + rep, :, t * CHANNELS : t * CHANNELS + CHANNELS
                        ]
    finish(begin([(v_out, out)], sems))


def call(kernel, outs, scratch, flops, *args, alias=None):
    shapes = [jax.ShapeDtypeStruct(shape, dtype) for shape, dtype in outs]
    size = sum(math.prod(s.shape) * s.dtype.itemsize for s in list(args) + shapes)
    return pl.pallas_call(
        kernel,
        out_shape=shapes,
        in_specs=[pl.BlockSpec(memory_space=pltpu.HBM)] * len(args),
        out_specs=[pl.BlockSpec(memory_space=pltpu.HBM)] * len(shapes),
        scratch_shapes=[pltpu.VMEM(shape, dtype) for shape, dtype in scratch]
        + [pltpu.SemaphoreType.DMA((16,))],
        input_output_aliases=alias or {},
        compiler_params=pltpu.CompilerParams(vmem_limit_bytes=(56 if flops else 12) * 2**20),
        cost_estimate=pl.CostEstimate(
            flops=flops, bytes_accessed=size, transcendentals=0
        ),
    )(*args)


def body(hidden_in, upstream, out_weight, conv_kernel, durations):
    yh, core = lax.axis_index("yh"), lax.axis_index("core")
    rep = lax.axis_index("rep")
    z, x = lax.axis_index("z"), lax.axis_index("x")
    quarter = yh * 2 + core
    place = z * 4 + x
    hidden, grads = hidden_in[0], upstream[0]

    rows = lax.ppermute(out_weight, ("z", "yh", "core"), turned())
    ends = [(4 * i + 3, 4 * i + 4) for i in range(31)]
    slot = lax.ppermute(
        jnp.where(quarter == 0, hidden[:EDGE], hidden[128 - EDGE :]),
        ("z", "x", "yh", "core"),
        ends + [(b, a) for a, b in ends],
    )
    [rows] = call(
        spread,
        [((8, 8, 1536), BF)],
        [((BLOCK, 1536), BF), ((1, 8), jnp.int32), ((8, 1536), BF)],
        0,
        rows, durations, slot,
    )
    rows = lax.all_to_all(rows, "z", 0, 0, tiled=True)
    across = lax.ppermute(half(hidden, 1 - yh, 1), "yh", SWAP)
    up_1 = lax.ppermute(grads, "yh", SWAP)
    up_2 = lax.ppermute(grads, "core", SWAP)
    slot_across = lax.ppermute(half(slot, 1 - yh, 1), "yh", SWAP)
    up_3 = lax.ppermute(up_1, "core", SWAP)
    ups = (grads, up_1, up_2, up_3)
    near = jnp.concatenate((half(hidden, yh, 1), half(slot, yh, 1)), axis=0)
    far = jnp.concatenate((across, slot_across), axis=0)
    beside = half(jnp.stack((near, far)), 1 - core, 2)
    beside = lax.ppermute(beside, "core", SWAP)
    [plane] = call(
        pack,
        [((8, PLANE_ROWS, 1536 + EXTRA), BF)],
        [((PLANE_ROWS, 1536), F32), ((8, 8, 1536), BF), ((PLANE_ROWS, 1536 + EXTRA), BF)],
        0,
        rows, slot_across, across, up_1,
    )
    rows = lax.all_to_all(plane, PLANE, 0, 0, tiled=True)
    ring = ("z", "x")
    up, down = [(i, i + 1) for i in range(31)], [(i + 1, i) for i in range(31)]
    kernel_f = lax.dynamic_slice_in_dim(
        jnp.pad(conv_kernel, ((0, 1), (0, 0))), quarter * CHANNELS, CHANNELS, 1
    ).astype(F32)
    square = ((CHANNELS, CHANNELS), BF)
    frames_f = ((FRAMES, CHANNELS), F32)
    wide_f = ((FRAMES + 2 * EDGE, CHANNELS), F32)
    all_grads = ((4, 128, 1536), BF)
    sent = ((8, PLANE_ROWS, 1536), BF)
    message = ((8, PLANE_ROWS, 1536 + EXTRA), BF)
    kernel_shape = ((TAPS + 1, CHANNELS), F32)
    slope, hidden_f, parts = call(
        convolve,
        [frames_f, wide_f, message],
        [
            all_grads, ((4, 128 + EDGE, CHANNELS), BF), kernel_shape, square, frames_f, wide_f, sent, frames_f,
        ],
        800_000_000,
        hidden, slot, across, slot_across, beside, *ups, kernel_f, placement(),
    )
    grad_conv, head, tail, parts = call(
        backward,
        [
            ((FRAMES, CHANNELS), BF), ((AFTER, CHANNELS), BF), ((EDGE, CHANNELS), BF), message,
        ],
        [
            sent, square, all_grads, frames_f, wide_f, ((FRAMES, CHANNELS), BF), frames_f,
            ((8, PLANE_ROWS, EXTRA), BF), ((TAPS + 1, 8, CHANNELS), F32),
        ],
        1_400_000_000,
        rows, placement(), *ups, slope, hidden_f, parts,
        alias={8: 3},
    )

    parts = lax.all_to_all(parts, PLANE, 0, 0, tiled=True)
    [parts] = call(
        pack_z,
        [((8, 8, 1536), BF)],
        [message, ((PLANE_ROWS, 1536 + EXTRA), F32), ((8, 8, 1536), BF)],
        0,
        parts,
    )
    parts = lax.all_to_all(parts, "z", 0, 0, tiled=True)
    weight_grad, taps_all = call(
        unpack_z,
        [((BLOCK, 1536), F32), ((32, 1, 1536), F32)],
        [((8, 8, 1536), BF), ((BLOCK, 1536), F32), ((32, 1, 1536), F32)],
        0,
        parts,
    )
    taps_all = lax.all_to_all(
        taps_all, ("x", "yh", "core", "rep"), 0, 0, tiled=True
    )
    weight_grad = lax.ppermute(
        weight_grad, ("z", "yh", "core"), [(b, a) for a, b in turned()]
    )
    [kernel_grad] = call(
        arrange,
        [((TAPS, 1536), F32)],
        [((32, 1, 1536), F32), ((TAPS, 1536), F32)],
        0,
        taps_all,
    )

    [frame_grad] = call(
        transposed,
        [((LONG, CHANNELS), BF)],
        [
            ((FRAMES, CHANNELS), BF), ((EDGE, CHANNELS), BF), ((AFTER, CHANNELS), BF),
            kernel_shape, ((FRAMES + EDGE + AFTER, CHANNELS), F32), ((LONG, CHANNELS), F32),
            ((LONG, CHANNELS), BF),
        ],
        200_000_000,
        grad_conv, lax.ppermute(tail, ring, up), lax.ppermute(head, ring, down), kernel_f,
    )
    notes = rows[:, 0, 1536:1544].reshape(4, 2, 8).astype(F32)
    notes = jnp.where(rep == 0, notes[:, 0], notes[:, 1])
    order = lax.iota(jnp.int32, 8)[None, :] * 4 + lax.iota(jnp.int32, 4)[:, None]
    earlier = jnp.sum(jnp.where(order < place, notes, 0.0)).astype(jnp.int32)
    known = jnp.concatenate((durations[0], jnp.full((8,), earlier)))
    known = jnp.stack(
        [known]
        + [lax.ppermute(known, GROUP, [(i, i ^ k) for i in range(4)]) for k in (1, 2, 3)]
    )
    start = jnp.sum(known[:, 8]) - place * FRAMES
    blocks = quarter ^ lax.iota(jnp.int32, 4)
    lengths = jnp.sum(
        jnp.where(blocks[None] == lax.iota(jnp.int32, 4)[:, None], 1, 0)[:, :, None]
        * known[None, :, :8],
        axis=1,
    ).reshape(-1)
    ends = start + jnp.cumsum(lengths)
    starts = ends - lengths
    at = lax.iota(jnp.int32, LONG)
    covers = (at[None] >= starts[:, None]) & (at[None] < ends[:, None])
    gloss = jnp.dot(covers.astype(BF), frame_grad, preferred_element_type=F32)

    def back(value):
        value = value.reshape(2, 2, -1, CHANNELS)
        kept = lax.dynamic_index_in_dim(value, core, 1, False)
        got = lax.ppermute(
            lax.dynamic_index_in_dim(value, 1 - core, 1, False), "core", SWAP
        )
        value = jnp.where(
            core == 0,
            jnp.concatenate((kept, got), axis=2),
            jnp.concatenate((got, kept), axis=2),
        )
        kept = lax.dynamic_index_in_dim(value, yh, 0, False)
        got = lax.ppermute(
            lax.dynamic_index_in_dim(value, 1 - yh, 0, False), "yh", SWAP
        )
        return jnp.where(
            yh == 0,
            jnp.concatenate((kept, got), axis=1),
            jnp.concatenate((got, kept), axis=1),
        )

    return (
        back(frame_grad[:FRAMES])[None],
        back(gloss)[None],
        weight_grad,
        kernel_grad,
    )


def solution(mesh):
    fine = Mesh(mesh.devices.reshape(SIZES), AXES)
    seq = ("z", "x", "yh", "core")
    rows = P(seq + ("rep",), None)
    in_specs = (P("rep", seq, None), P("rep", seq, None), rows, P(), P("rep", seq))
    out_specs = (P("rep", seq, None), P("rep", seq, None), rows, P())
    return jax.shard_map(
        body, mesh=fine, in_specs=in_specs, out_specs=out_specs, check_vma=False
    )
```

```python
import math

import jax
import jax.numpy as jnp
import numpy as np
from jax import lax
from jax.experimental import pallas as pl
from jax.experimental.pallas import tpu as pltpu
from jax.sharding import Mesh
from jax.sharding import PartitionSpec as P

AXES = ("z", "x", "yh", "core", "rep")
SIZES = (8, 4, 2, 2, 2)
GROUP = ("yh", "core")
PLANE = ("x", "rep")
QUARTERS = 4
BLOCK = 6
PLANE_ROWS = 48
EXTRA = 128
FRAMES, CHANNELS, TAPS = 512, 384, 31
EDGE_H, EDGE_U, SPILL = 48, 32, 16
LEFT_H, LEFT_U = 32, 16
WIDE = FRAMES + LEFT_U + EDGE_U
LONG = FRAMES + SPILL
SHARE = 128 + EDGE_H + 2 * EDGE_U
HANDED = 128 + EDGE_H + 4 * EDGE_U
BACK = 128 + SPILL + 16
SWAP = [(0, 1), (1, 0)]
BF = jnp.bfloat16
F32 = jnp.float32


def placement():
    out = np.zeros((CHANNELS, CHANNELS), np.float32)
    for zl in range(2):
        for x in range(4):
            for q in range(4):
                for rep in range(2):
                    for r in range(BLOCK):
                        row = (((zl * 4 + x) * 4 + q) * 2 + rep) * BLOCK + r
                        out[row, (x * 2 + rep) * PLANE_ROWS + (q * 2 + zl) * BLOCK + r] = 1
    return jnp.asarray(out, BF)


def turned():
    pairs = []
    for zq in range(4):
        for zl in range(2):
            for q in range(4):
                pairs.append(((zq * 2 + zl) * 4 + q, (q * 2 + zl) * 4 + zq))
    return pairs


def lanes(tile):
    return slice(tile * 128, tile * 128 + 128)


def begin(pairs, sems):
    copies = [pltpu.make_async_copy(a, b, sems.at[i]) for i, (a, b) in enumerate(pairs)]
    for copy in copies:
        copy.start()
    return copies


def finish(copies):
    for copy in copies:
        copy.wait()


def spread(weights, durations, slot, hidden, out, share, got, lengths, block, v_share, sems):
    yh = lax.axis_index("yh")
    other = pl.ds(pl.multiple_of((1 - yh) * 2 * CHANNELS, 128), 2 * CHANNELS)
    up = pl.ds(EDGE_H, EDGE_U)
    taken = begin(
        [
            (hidden.at[:, other], v_share.at[pl.ds(0, 128)]),
            (slot.at[pl.ds(0, EDGE_H), other], v_share.at[pl.ds(128, EDGE_H)]),
            (slot.at[up, pl.ds(0, 768)], v_share.at[pl.ds(128 + EDGE_H, EDGE_U)]),
            (slot.at[up, pl.ds(768, 768)], v_share.at[pl.ds(128 + EDGE_H + EDGE_U, EDGE_U)]),
        ],
        sems.at[pl.ds(9, 4)],
    )
    finish(begin([(weights, got), (durations, lengths)], sems))
    lane = lax.broadcasted_iota(jnp.int32, (1, 1536), 1)
    total = jnp.sum(lengths[...].astype(F32), axis=1, keepdims=True)
    note = jnp.where(lane == lax.axis_index("z"), jnp.broadcast_to(total, (1, 1536)), 0.0)
    rows = [got[...].astype(F32), note, jnp.zeros((1, 1536), F32)]
    block[...] = jnp.concatenate(rows, axis=0).astype(BF)
    finish(taken)
    given = begin([(v_share, share)], sems.at[pl.ds(9, 1)])
    finish(begin([(block, out.at[peer]) for peer in range(8)], sems))
    finish(given)


def pack(
    gathered, hidden, slot, across, upstream, plane, beside, rows, got, block, v_beside, sems
):
    yh, core = lax.axis_index("yh"), lax.axis_index("core")
    other = pl.ds(pl.multiple_of((yh * 2 + 1 - core) * CHANNELS, 128), CHANNELS)
    part = pl.ds(pl.multiple_of((1 - core) * CHANNELS, 128), CHANNELS)
    first = begin([(gathered, got)], sems)
    ups = 128 + EDGE_H
    moves = [
        (hidden.at[:, other], v_beside.at[0, pl.ds(0, 128)]),
        (slot.at[pl.ds(0, EDGE_H), other], v_beside.at[0, pl.ds(128, EDGE_H)]),
        (across.at[pl.ds(0, ups), part], v_beside.at[1, pl.ds(0, ups)]),
    ]
    for i in range(4):
        cut = pl.ds((i % 2) * CHANNELS, CHANNELS)
        row = pl.ds(ups + EDGE_U * i, EDGE_U)
        wide = pl.ds(i * CHANNELS, CHANNELS)
        moves.append((slot.at[pl.ds(EDGE_H, EDGE_U), wide], v_beside.at[0, row]))
        moves.append((across.at[pl.ds(ups + EDGE_U * (i // 2), EDGE_U), cut], v_beside.at[1, row]))
    moves = begin(moves, sems.at[pl.ds(1, 11)])
    finish(first)
    note = jnp.zeros((8, EXTRA), F32)
    for z in range(8):
        block_z = got[z].astype(F32)
        rows[BLOCK * z : BLOCK * z + BLOCK] = block_z[:BLOCK]
        note += jnp.broadcast_to(block_z[BLOCK : BLOCK + 1, :EXTRA], (8, EXTRA))
    block[:, :1536] = rows[...].astype(BF)
    block[:, 1536:] = jnp.concatenate([note] * (PLANE_ROWS // 8), axis=0).astype(BF)
    sent = begin([(block, plane.at[peer]) for peer in range(8)], sems.at[pl.ds(12, 8)])
    finish(moves)
    handed = begin([(v_beside, beside)], sems)
    finish(sent)
    finish(handed)


def group_grads(sources, grads):
    yh, core = lax.axis_index("yh"), lax.axis_index("core")
    places = [yh * 2 + core, 2 - 2 * yh + core, yh * 2 + 1 - core, 3 - 2 * yh - core]
    return [(source, grads.at[place]) for source, place in zip(sources, places)]


def convolve(
    own, slot, across, beside, up_0, up_1, up_2, up_3, kernel, order, slope, hidden, parts,
    grads, frames, weights, turn, v_slope, v_hidden, v_parts, active, sems,
):
    yh, core = lax.axis_index("yh"), lax.axis_index("core")
    part = pl.ds(pl.multiple_of(core * CHANNELS, 128), CHANNELS)
    mine = pl.ds(pl.multiple_of((yh * 2 + core) * CHANNELS, 128), CHANNELS)
    block = pl.ds(0, 128 + EDGE_H)
    needed = begin(
        [
            (own.at[:, mine], frames.at[yh * 2 + core, pl.ds(0, 128)]),
            (slot.at[pl.ds(0, EDGE_H), mine], frames.at[yh * 2 + core, pl.ds(128, EDGE_H)]),
            (across.at[block, part], frames.at[(1 - yh) * 2 + core]),
            (beside.at[0, block], frames.at[yh * 2 + 1 - core]),
            (beside.at[1, block], frames.at[(1 - yh) * 2 + 1 - core]),
            (kernel, weights),
        ],
        sems,
    )
    later = begin(
        group_grads((up_0, up_1, up_2, up_3), grads) + [(order, turn)], sems.at[pl.ds(8, 5)]
    )
    finish(needed)
    v_hidden[:LEFT_H] = frames[0, 128 + EDGE_H - LEFT_H :].astype(F32)
    for b in range(4):
        v_hidden[LEFT_H + 128 * b : LEFT_H + 128 * b + 128] = frames[b, :128].astype(F32)
    v_hidden[LEFT_H + FRAMES :] = frames[3, 128:].astype(F32)
    rows = 112
    for tile in range(CHANNELS // 128):

        def chunk(c, _, tile=tile):
            base = pl.multiple_of(c * rows, 8)
            total = jnp.zeros((rows, 128), F32)
            window = v_hidden[pl.ds(base, rows + 32), lanes(tile)]
            for b in range(8):
                slab = window[b : b + rows + 24]
                for a in range(4):
                    k = 8 * a + b - 1
                    if 0 <= k < TAPS:
                        total += weights[k : k + 1, lanes(tile)] * slab[8 * a : 8 * a + rows]
            sig = jax.nn.sigmoid(total)
            v_slope[pl.ds(base, rows), lanes(tile)] = sig * (1.0 + total * (1.0 - sig))
            active[pl.ds(base, rows), lanes(tile)] = total * sig
            return 0

        lax.fori_loop(0, WIDE // rows, chunk, 0)
    out = begin([(v_slope, slope), (v_hidden, hidden)], sems)
    finish(later)
    acts = active[LEFT_U : LEFT_U + FRAMES].astype(BF)
    acts = jnp.dot(acts, turn[...], preferred_element_type=F32).astype(BF)
    product = lax.dot_general(
        acts,
        grads[...].reshape(FRAMES, 1536),
        (((0,), (0,)), ((), ())),
        preferred_element_type=F32,
    ).astype(BF)
    for s in range(8):
        v_parts[s] = product[PLANE_ROWS * s : PLANE_ROWS * (s + 1)]
    finish(begin([(v_parts, parts.at[:, :, pl.ds(0, 1536)])], sems.at[pl.ds(2, 1)]))
    finish(out)


def backward(
    gathered, spread, up_0, up_1, up_2, up_3, slope, hidden, parts,
    grad_conv, projection, message,
    got, turn, grads, v_slope, v_hidden, v_grad, v_grad_f, v_taps, sums, v_weights, sems,
):
    needed = begin(
        [(gathered.at[s, :, pl.ds(0, 1536)], got.at[s]) for s in range(8)]
        + [(spread, turn)],
        sems,
    )
    later = begin(group_grads((up_0, up_1, up_2, up_3), grads), sems.at[pl.ds(9, 4)])
    last = begin(
        [(slope.at[pl.ds(LEFT_U, FRAMES)], v_slope), (hidden, v_hidden)], sems.at[pl.ds(13, 2)]
    )
    finish(needed)
    weights = jnp.dot(
        turn[...], got[...].reshape(CHANNELS, 1536), preferred_element_type=F32
    ).astype(BF)
    v_weights[...] = weights
    finish(later)
    value = lax.dot_general(
        grads[...].reshape(FRAMES, 1536),
        weights,
        (((1,), (1,)), ((), ())),
        preferred_element_type=F32,
    )
    finish(last)
    value = (value * v_slope[...]).astype(BF)
    v_grad[...] = value
    v_grad_f[...] = value.astype(F32)
    out = begin([(v_grad, grad_conv), (v_weights, projection)], sems)
    span = 128
    sums[...] = jnp.zeros_like(sums)
    for tile in range(CHANNELS // 128):

        def piece(c, _, tile=tile):
            base = pl.multiple_of(c * span, 8)
            terms = v_grad_f[pl.ds(base, span), lanes(tile)]
            window = v_hidden[pl.ds(base + LEFT_U, span + 32), lanes(tile)]
            for b in range(8):
                slab = window[b : b + span + 24]
                for a in range(4):
                    k = 8 * a + b - 1
                    if 0 <= k < TAPS:
                        sums[k, :, lanes(tile)] += jnp.sum(
                            (terms * slab[8 * a : 8 * a + span]).reshape(span // 8, 8, 128),
                            axis=0,
                        )
            return 0

        lax.fori_loop(0, FRAMES // span, piece, 0)
    for s in range(8):
        rows = [
            jnp.sum(sums[4 * s + t, :, lanes(tile)], axis=0, keepdims=True)
            for t in range(4)
            for tile in range(CHANNELS // 128)
        ]
        rows = jnp.concatenate(rows, axis=0)
        high = rows.astype(BF).astype(F32)
        rows = [high, rows - high, jnp.zeros((PLANE_ROWS - 24, 128), F32)]
        v_taps[s] = jnp.concatenate(rows, axis=0).astype(BF)
    finish(begin([(v_taps, message.at[:, :, pl.ds(1536, EXTRA)])], sems.at[pl.ds(3, 1)]))
    finish(out)


def transposed(
    grad_conv, projection, slope, slot, across, beside, kernel, gathered, lengths,
    kept, given, v_grad, v_weights, v_slope, ups, weights, notes, v_lengths, wide, total_f,
    v_kept, v_given, sems,
):
    yh, core = lax.axis_index("yh"), lax.axis_index("core")
    far = 128 + EDGE_H
    edges = [(slot.at[pl.ds(EDGE_H, EDGE_U)], ups.at[yh * 2 + core])]
    for i in range(2):
        edges.append(
            (
                across.at[pl.ds(far + EDGE_U * i, EDGE_U)],
                ups.at[(1 - yh) * 2 + core, :, pl.ds(768 * i, 768)],
            )
        )
    for i in range(4):
        row, cut = pl.ds(far + EDGE_U * i, EDGE_U), pl.ds(CHANNELS * i, CHANNELS)
        edges.append((beside.at[0, row], ups.at[yh * 2 + 1 - core, :, cut]))
        edges.append((beside.at[1, row], ups.at[(1 - yh) * 2 + 1 - core, :, cut]))
    edges += [
        (projection, v_weights),
        (slope.at[pl.ds(0, LEFT_U)], v_slope.at[pl.ds(0, LEFT_U)]),
        (slope.at[pl.ds(LEFT_U + FRAMES, EDGE_U)], v_slope.at[pl.ds(LEFT_U, EDGE_U)]),
        (grad_conv, v_grad),
        (kernel, weights),
        (gathered.at[:, pl.ds(0, 16), pl.ds(1536, EXTRA)], notes),
        (lengths, v_lengths),
    ]
    finish(begin(edges, sems))
    rows = jnp.concatenate([ups[0, EDGE_U - LEFT_U :], ups[3]], axis=0)
    value = lax.dot_general(
        rows, v_weights[...], (((1,), (1,)), ((), ())), preferred_element_type=F32
    )
    value = (value * v_slope[...]).astype(BF).astype(F32)
    wide[:LEFT_U] = value[:LEFT_U]
    wide[LEFT_U : LEFT_U + FRAMES] = v_grad[...].astype(F32)
    wide[LEFT_U + FRAMES :] = value[LEFT_U:]
    rows = 88
    for tile in range(CHANNELS // 128):

        def chunk(c, _, tile=tile):
            base = pl.multiple_of(c * rows, 8)
            total = jnp.zeros((rows, 128), F32)
            window = wide[pl.ds(base, rows + 32), lanes(tile)]
            for b in range(8):
                slab = window[b : b + rows + 24]
                for a in range(4):
                    k = TAPS - 8 * a - b
                    if 0 <= k < TAPS:
                        total += weights[k : k + 1, lanes(tile)] * slab[8 * a : 8 * a + rows]
            total_f[pl.ds(base, rows), lanes(tile)] = total
            return 0

        lax.fori_loop(0, LONG // rows, chunk, 0)
    place = lax.axis_index("z") * 4 + lax.axis_index("x")
    lane = lax.broadcasted_iota(jnp.int32, (8, EXTRA), 1)
    before = jnp.zeros((8, EXTRA), F32)
    for peer in range(8):
        earlier = (lane * 4 + peer // 2 < place) & (lax.axis_index("rep") == peer % 2) & (lane < 8)
        before += jnp.where(earlier, notes[peer, :8].astype(F32), 0.0)
    before = jnp.broadcast_to(jnp.sum(before, axis=1, keepdims=True), (8, CHANNELS))
    high = before.astype(BF).astype(F32)
    block = jnp.broadcast_to(jnp.sum(v_lengths[...], axis=1, keepdims=True), (8, CHANNELS))
    note = jnp.concatenate([high[:1], before[:1] - high[:1], block[:1], block[:5], block], axis=0)
    for row in range(2):
        for out, side in ((v_kept, core), (v_given, 1 - core)):
            begin_row = pl.multiple_of((row * 2 + side) * 128, 128)
            out[row, : 128 + SPILL] = total_f[pl.ds(begin_row, 128 + SPILL)].astype(BF)
            out[row, 128 + SPILL :] = note.astype(BF)
    finish(begin([(v_kept, kept), (v_given, given)], sems))


def settle(kept, got, far, lengths, frame_grad, gloss, frames, notes, v_lengths, v_gloss, sems):
    yh, core = lax.axis_index("yh"), lax.axis_index("core")
    sources = [(kept.at[yh], yh, core), (got.at[yh], yh, 1 - core)]
    sources += [(far.at[0], 1 - yh, core), (far.at[1], 1 - yh, 1 - core)]
    moves = [(lengths, v_lengths)]
    for source, a, b in sources:
        cut = pl.ds(pl.multiple_of((a * 2 + b) * CHANNELS, 128), CHANNELS)
        moves.append((source.at[pl.ds(0, 128 + SPILL)], frames.at[:, cut]))
        moves.append((source.at[pl.ds(128 + SPILL, 16)], notes.at[a * 2 + b]))
    finish(begin(moves, sems))
    out = begin([(frames.at[pl.ds(0, 128)], frame_grad)], sems)
    mine = yh * 2 + core
    place = lax.axis_index("z") * 4 + lax.axis_index("x")
    start = jnp.zeros((1, EXTRA), F32)
    for q in range(4):
        note = notes[q, :, :EXTRA].astype(F32)
        start += note[0:1] + note[1:2] + jnp.where(q < mine, note[2:3], 0.0)
    start = start[:, :1] - (place * FRAMES + mine * 128).astype(F32)
    gloss_id = lax.broadcasted_iota(jnp.int32, (8, EXTRA), 0)
    lane = lax.broadcasted_iota(jnp.int32, (8, EXTRA), 1)
    length = v_lengths[...]
    first = jnp.sum(jnp.where(lane < gloss_id, length, 0.0), axis=1, keepdims=True) + start
    last = first + jnp.sum(jnp.where(lane == gloss_id, length, 0.0), axis=1, keepdims=True)
    at = lax.broadcasted_iota(jnp.int32, (8, 128 + SPILL), 1).astype(F32)
    covers = jnp.where((at >= first) & (at < last), 1.0, 0.0).astype(BF)
    v_gloss[...] = jnp.dot(covers, frames[...], preferred_element_type=F32)
    finish(begin([(v_gloss, gloss)], sems.at[pl.ds(1, 1)]))
    finish(out)


def pack_z(parts, out, v_parts, v_sum, v_out, sems):
    finish(begin([(parts, v_parts)], sems))
    v_sum[...] = jnp.sum(v_parts[...].astype(F32), axis=0)
    taps = v_sum[:12, 1536:] + v_sum[12:24, 1536:]
    taps = jnp.concatenate([taps[j : j + 1] for j in range(12)], axis=1)
    high = taps.astype(BF).astype(F32)
    for z in range(8):
        rows = [v_sum[BLOCK * z : BLOCK * z + BLOCK, :1536], high, taps - high]
        v_out[z] = jnp.concatenate(rows, axis=0).astype(BF)
    finish(begin([(v_out, out)], sems))


def unpack_z(got, weights, taps, v_got, v_weights, v_taps, sems):
    finish(begin([(got, v_got)], sems))
    total = v_got[0].astype(F32)
    for z in range(1, 8):
        total += v_got[z].astype(F32)
    total = total * (1.0 / math.sqrt(2 * 16384))
    v_weights[...] = total[:BLOCK]
    for peer in range(32):
        v_taps[peer] = total[6:7] + total[7:8]
    finish(begin([(v_taps, taps), (v_weights, weights)], sems))


def arrange(got, out, v_got, v_out, sems):
    finish(begin([(got, v_got)], sems))
    for x in range(4):
        for q in range(4):
            for rep in range(2):
                for t in range(4):
                    k = (x * 2 + rep) * 4 + t
                    if k < TAPS:
                        v_out[k : k + 1, q * CHANNELS : q * CHANNELS + CHANNELS] = v_got[
                            (x * 4 + q) * 2 + rep, :, t * CHANNELS : t * CHANNELS + CHANNELS
                        ]
    finish(begin([(v_out, out)], sems))


def call(kernel, outs, scratch, flops, *args, alias=None):
    shapes = [jax.ShapeDtypeStruct(shape, dtype) for shape, dtype in outs]
    size = sum(math.prod(s.shape) * s.dtype.itemsize for s in list(args) + shapes)
    return pl.pallas_call(
        kernel,
        out_shape=shapes,
        in_specs=[pl.BlockSpec(memory_space=pltpu.HBM)] * len(args),
        out_specs=[pl.BlockSpec(memory_space=pltpu.HBM)] * len(shapes),
        scratch_shapes=[pltpu.VMEM(shape, dtype) for shape, dtype in scratch]
        + [pltpu.SemaphoreType.DMA((20,))],
        input_output_aliases=alias or {},
        compiler_params=pltpu.CompilerParams(vmem_limit_bytes=(56 if flops else 16) * 2**20),
        cost_estimate=pl.CostEstimate(
            flops=flops, bytes_accessed=size, transcendentals=0
        ),
    )(*args)


def body(hidden_in, upstream, out_weight, conv_kernel, durations):
    yh, core = lax.axis_index("yh"), lax.axis_index("core")
    quarter = yh * 2 + core
    hidden, grads = hidden_in[0], upstream[0]
    lengths = jnp.broadcast_to(
        jnp.pad(durations.astype(F32), ((0, 0), (0, EXTRA - durations.shape[1]))), (8, EXTRA)
    )

    ends = [(4 * i + 3, 4 * i + 4) for i in range(31)]
    slot = lax.ppermute(
        jnp.where(
            quarter == 0,
            jnp.concatenate((hidden[:EDGE_H], grads[:EDGE_U])),
            jnp.concatenate((hidden[128 - EDGE_H :], grads[128 - EDGE_U :])),
        ),
        ("z", "x", "yh", "core"),
        ends + [(b, a) for a, b in ends],
    )
    rows = lax.ppermute(out_weight, ("z", "yh", "core"), turned())
    rows, share = call(
        spread,
        [((8, 8, 1536), BF), ((SHARE, 768), BF)],
        [((BLOCK, 1536), BF), ((1, 8), jnp.int32), ((8, 1536), BF), ((SHARE, 768), BF)],
        0,
        rows, durations, slot, hidden,
    )
    rows = lax.all_to_all(rows, "z", 0, 0, tiled=True)
    across = lax.ppermute(share, "yh", SWAP)
    up_1 = lax.ppermute(grads, "yh", SWAP)
    up_2 = lax.ppermute(grads, "core", SWAP)
    up_3 = lax.ppermute(up_1, "core", SWAP)
    ups = (grads, up_1, up_2, up_3)
    plane, beside = call(
        pack,
        [((8, PLANE_ROWS, 1536 + EXTRA), BF), ((2, HANDED, CHANNELS), BF)],
        [
            ((PLANE_ROWS, 1536), F32), ((8, 8, 1536), BF), ((PLANE_ROWS, 1536 + EXTRA), BF),
            ((2, HANDED, CHANNELS), BF),
        ],
        0,
        rows, hidden, slot, across, up_1,
    )
    rows = lax.all_to_all(plane, PLANE, 0, 0, tiled=True)
    beside = lax.ppermute(beside, "core", SWAP)
    kernel_f = lax.dynamic_slice_in_dim(
        jnp.pad(conv_kernel, ((0, 1), (0, 0))), quarter * CHANNELS, CHANNELS, 1
    ).astype(F32)
    square = ((CHANNELS, CHANNELS), BF)
    frames_f = ((FRAMES, CHANNELS), F32)
    wide_f = ((LEFT_H + FRAMES + EDGE_H, CHANNELS), F32)
    slope_f = ((WIDE, CHANNELS), F32)
    all_grads = ((4, 128, 1536), BF)
    sent = ((8, PLANE_ROWS, 1536), BF)
    message = ((8, PLANE_ROWS, 1536 + EXTRA), BF)
    kernel_shape = ((TAPS + 1, CHANNELS), F32)
    slope, hidden_f, parts = call(
        convolve,
        [slope_f, wide_f, message],
        [
            all_grads, ((4, 128 + EDGE_H, CHANNELS), BF), kernel_shape, square, slope_f, wide_f,
            sent, slope_f,
        ],
        800_000_000,
        hidden, slot, across, beside, *ups, kernel_f, placement(),
    )
    grad_conv, projection, parts = call(
        backward,
        [
            ((FRAMES, CHANNELS), BF), ((CHANNELS, 1536), BF), message,
        ],
        [
            sent, square, all_grads, frames_f, wide_f, ((FRAMES, CHANNELS), BF), frames_f,
            ((8, PLANE_ROWS, EXTRA), BF), ((TAPS + 1, 8, CHANNELS), F32),
            ((CHANNELS, 1536), BF),
        ],
        1_400_000_000,
        rows, placement(), *ups, slope, hidden_f, parts,
        alias={8: 2},
    )

    parts = lax.all_to_all(parts, PLANE, 0, 0, tiled=True)
    [parts] = call(
        pack_z,
        [((8, 8, 1536), BF)],
        [message, ((PLANE_ROWS, 1536 + EXTRA), F32), ((8, 8, 1536), BF)],
        0,
        parts,
    )
    parts = lax.all_to_all(parts, "z", 0, 0, tiled=True)
    weight_grad, taps_all = call(
        unpack_z,
        [((BLOCK, 1536), F32), ((32, 1, 1536), F32)],
        [((8, 8, 1536), BF), ((BLOCK, 1536), F32), ((32, 1, 1536), F32)],
        0,
        parts,
    )
    taps_all = lax.all_to_all(
        taps_all, ("x", "yh", "core", "rep"), 0, 0, tiled=True
    )
    weight_grad = lax.ppermute(
        weight_grad, ("z", "yh", "core"), [(b, a) for a, b in turned()]
    )
    [kernel_grad] = call(
        arrange,
        [((TAPS, 1536), F32)],
        [((32, 1, 1536), F32), ((TAPS, 1536), F32)],
        0,
        taps_all,
    )

    back = ((2, BACK, CHANNELS), BF)
    kept, given = call(
        transposed,
        [back, back],
        [
            ((FRAMES, CHANNELS), BF), ((CHANNELS, 1536), BF), ((LEFT_U + EDGE_U, CHANNELS), F32),
            ((4, EDGE_U, 1536), BF), kernel_shape, ((8, 16, EXTRA), BF), ((8, EXTRA), F32),
            slope_f, ((LONG, CHANNELS), F32), back, back,
        ],
        200_000_000,
        grad_conv, projection, slope, slot, across, beside, kernel_f, rows, lengths,
    )
    got = lax.ppermute(given, "core", SWAP)
    far = jnp.stack(
        [lax.dynamic_index_in_dim(part, 1 - yh, 0, False) for part in (kept, got)]
    )
    far = lax.ppermute(far, "yh", SWAP)
    frame_grad, gloss = call(
        settle,
        [((128, 1536), BF), ((8, 1536), F32)],
        [
            ((128 + SPILL, 1536), BF), ((4, 16, CHANNELS), BF), ((8, EXTRA), F32),
            ((8, 1536), F32),
        ],
        0,
        kept, got, far, lengths,
    )
    return (frame_grad[None], gloss[None], weight_grad, kernel_grad)


def solution(mesh):
    fine = Mesh(mesh.devices.reshape(SIZES), AXES)
    seq = ("z", "x", "yh", "core")
    rows = P(seq + ("rep",), None)
    in_specs = (P("rep", seq, None), P("rep", seq, None), rows, P(), P("rep", seq))
    out_specs = (P("rep", seq, None), P("rep", seq, None), rows, P())
    return jax.shard_map(
        body, mesh=fine, in_specs=in_specs, out_specs=out_specs, check_vma=False
    )
```

```python
import math

import jax
import jax.numpy as jnp
import numpy as np
from jax import lax
from jax.experimental import pallas as pl
from jax.experimental.pallas import tpu as pltpu
from jax.sharding import Mesh
from jax.sharding import PartitionSpec as P

AXES = ("z", "x", "yh", "core", "rep")
SIZES = (8, 4, 2, 2, 2)
GROUP = ("yh", "core")
PLANE = ("x", "yh", "core", "rep")
QUARTERS = 4
BLOCK = 6
EXTRA = 128
MEMBERS, ROWS = 32, 24
MESSAGE = MEMBERS * ROWS
FRAMES, CHANNELS, TAPS = 512, 384, 31
EDGE_H, EDGE_U, SPILL = 48, 32, 16
LEFT_H, LEFT_U = 32, 16
WIDE = FRAMES + LEFT_U + EDGE_U
LONG = FRAMES + SPILL
SHARE = EDGE_H + 2 * EDGE_U
HANDED = 128 + EDGE_H + 4 * EDGE_U
BACK = 128 + SPILL
SWAP = [(0, 1), (1, 0)]
BF = jnp.bfloat16
F32 = jnp.float32


def placement(side):
    out = np.zeros((CHANNELS, MESSAGE), np.float32)
    for zl in range(2):
        for member in range(MEMBERS):
            for r in range(BLOCK):
                row = (zl * MEMBERS + member) * BLOCK + r
                out[row, member * ROWS + 12 * side + zl * BLOCK + r] = 1
    return jnp.asarray(out, BF)


def lanes(tile):
    return slice(tile * 128, tile * 128 + 128)


def begin(pairs, sems):
    copies = [pltpu.make_async_copy(a, b, sems.at[i]) for i, (a, b) in enumerate(pairs)]
    for copy in copies:
        copy.start()
    return copies


def finish(copies):
    for copy in copies:
        copy.wait()


def spread(
    weights, durations, hidden, upstream, out, share, edge,
    got, lengths, block, v_share, v_edge, sems,
):
    yh, core = lax.axis_index("yh"), lax.axis_index("core")
    other = pl.ds(pl.multiple_of((1 - yh) * 768, 128), 768)
    last = (yh + core) // 2
    from_h = pl.ds(pl.multiple_of(last * (128 - EDGE_H), 16), EDGE_H)
    from_u = pl.ds(pl.multiple_of(last * (128 - EDGE_U), 16), EDGE_U)
    taken = begin(
        [
            (hidden.at[:, other], v_share.at[pl.ds(0, 128)]),
            (upstream.at[:, pl.ds(0, 768)], v_share.at[pl.ds(128, 128)]),
            (upstream.at[:, pl.ds(768, 768)], v_share.at[pl.ds(256, 128)]),
            (hidden.at[from_h], v_edge.at[pl.ds(0, EDGE_H)]),
            (upstream.at[from_u], v_edge.at[pl.ds(EDGE_H, EDGE_U)]),
        ],
        sems.at[pl.ds(9, 5)],
    )
    finish(begin([(weights, got), (durations, lengths)], sems))
    lane = lax.broadcasted_iota(jnp.int32, (1, 1536), 1)
    total = jnp.sum(lengths[...].astype(F32), axis=1, keepdims=True)
    note = jnp.where(lane == lax.axis_index("z"), jnp.broadcast_to(total, (1, 1536)), 0.0)
    rows = [got[...].astype(F32), note, jnp.zeros((1, 1536), F32)]
    block[...] = jnp.concatenate(rows, axis=0).astype(BF)
    sent = begin([(block, out.at[peer]) for peer in range(8)], sems)
    finish(taken)
    finish(begin([(v_share, share), (v_edge, edge)], sems.at[pl.ds(9, 2)]))
    finish(sent)


def lend(slot, out, v_out, sems):
    other = pl.ds(pl.multiple_of((1 - lax.axis_index("yh")) * 768, 128), 768)
    up = pl.ds(EDGE_H, EDGE_U)
    finish(
        begin(
            [
                (slot.at[pl.ds(0, EDGE_H), other], v_out.at[pl.ds(0, EDGE_H)]),
                (slot.at[up, pl.ds(0, 768)], v_out.at[pl.ds(EDGE_H, EDGE_U)]),
                (slot.at[up, pl.ds(768, 768)], v_out.at[pl.ds(EDGE_H + EDGE_U, EDGE_U)]),
            ],
            sems,
        )
    )
    finish(begin([(v_out, out)], sems))


def pack(gathered, plane, rows, got, block, sems):
    finish(begin([(gathered, got)], sems))
    note = jnp.zeros((8, EXTRA), F32)
    for z in range(8):
        block_z = got[z].astype(F32)
        at = ROWS * (z // 2) + BLOCK * (z % 2)
        rows[at : at + BLOCK, :768] = block_z[:BLOCK, :768]
        rows[at + 12 : at + 12 + BLOCK, :768] = block_z[:BLOCK, 768:]
        note += jnp.broadcast_to(block_z[BLOCK : BLOCK + 1, :EXTRA], (8, EXTRA))
    rows[:, 768:] = jnp.concatenate([note] * (ROWS // 2), axis=0)
    for q in range(4):
        block[q] = rows[ROWS * q : ROWS * q + ROWS].astype(BF)
    finish(begin([(block.at[(j // 2) % 4], plane.at[j]) for j in range(MEMBERS)], sems))


def relay(hidden, slot, across, lent, beside, v_beside, sems):
    yh, core = lax.axis_index("yh"), lax.axis_index("core")
    other = pl.ds(pl.multiple_of((yh * 2 + 1 - core) * CHANNELS, 128), CHANNELS)
    part = pl.ds(pl.multiple_of((1 - core) * CHANNELS, 128), CHANNELS)
    ups = 128 + EDGE_H
    edge = pl.ds(0, EDGE_H)
    moves = [
        (hidden.at[:, other], v_beside.at[0, pl.ds(0, 128)]),
        (slot.at[edge, other], v_beside.at[0, pl.ds(128, EDGE_H)]),
        (across.at[pl.ds(0, 128), part], v_beside.at[1, pl.ds(0, 128)]),
        (lent.at[edge, part], v_beside.at[1, pl.ds(128, EDGE_H)]),
    ]
    for i in range(4):
        cut = pl.ds((i % 2) * CHANNELS, CHANNELS)
        row = pl.ds(ups + EDGE_U * i, EDGE_U)
        wide = pl.ds(i * CHANNELS, CHANNELS)
        moves.append((slot.at[pl.ds(EDGE_H, EDGE_U), wide], v_beside.at[0, row]))
        moves.append((lent.at[pl.ds(EDGE_H + EDGE_U * (i // 2), EDGE_U), cut], v_beside.at[1, row]))
    finish(begin(moves, sems))
    finish(begin([(v_beside, beside)], sems))


def group_grads(upstream, across, beside, beyond, grads):
    yh, core = lax.axis_index("yh"), lax.axis_index("core")
    moves = [(upstream, grads.at[yh * 2 + core]), (beside, grads.at[yh * 2 + 1 - core])]
    for source, place in ((across, 2 - 2 * yh + core), (beyond, 3 - 2 * yh - core)):
        for i in range(2):
            rows, cut = pl.ds(128 + 128 * i, 128), pl.ds(768 * i, 768)
            moves.append((source.at[rows], grads.at[place, :, cut]))
    return moves


def convolve(
    own, slot, across, lent, beside, upstream, up_beside, beyond, kernel, low, high,
    slope, hidden, parts,
    grads, frames, weights, v_low, v_high, v_slope, v_hidden, v_parts, active, sems,
):
    yh, core = lax.axis_index("yh"), lax.axis_index("core")
    part = pl.ds(pl.multiple_of(core * CHANNELS, 128), CHANNELS)
    mine = pl.ds(pl.multiple_of((yh * 2 + core) * CHANNELS, 128), CHANNELS)
    block = pl.ds(0, 128 + EDGE_H)
    needed = begin(
        [
            (own.at[:, mine], frames.at[yh * 2 + core, pl.ds(0, 128)]),
            (slot.at[pl.ds(0, EDGE_H), mine], frames.at[yh * 2 + core, pl.ds(128, EDGE_H)]),
            (across.at[pl.ds(0, 128), part], frames.at[(1 - yh) * 2 + core, pl.ds(0, 128)]),
            (lent.at[pl.ds(0, EDGE_H), part], frames.at[(1 - yh) * 2 + core, pl.ds(128, EDGE_H)]),
            (beside.at[0, block], frames.at[yh * 2 + 1 - core]),
            (beside.at[1, block], frames.at[(1 - yh) * 2 + 1 - core]),
            (kernel, weights),
        ],
        sems,
    )
    later = begin(
        group_grads(upstream, across, up_beside, beyond, grads) + [(low, v_low), (high, v_high)],
        sems.at[pl.ds(8, 8)],
    )
    finish(needed)
    v_hidden[:LEFT_H] = frames[0, 128 + EDGE_H - LEFT_H :].astype(F32)
    for b in range(4):
        v_hidden[LEFT_H + 128 * b : LEFT_H + 128 * b + 128] = frames[b, :128].astype(F32)
    v_hidden[LEFT_H + FRAMES :] = frames[3, 128:].astype(F32)
    rows = 112
    for tile in range(CHANNELS // 128):

        def chunk(c, _, tile=tile):
            base = pl.multiple_of(c * rows, 8)
            total = jnp.zeros((rows, 128), F32)
            window = v_hidden[pl.ds(base, rows + 32), lanes(tile)]
            for b in range(8):
                slab = window[b : b + rows + 24]
                for a in range(4):
                    k = 8 * a + b - 1
                    if 0 <= k < TAPS:
                        total += weights[k : k + 1, lanes(tile)] * slab[8 * a : 8 * a + rows]
            sig = jax.nn.sigmoid(total)
            v_slope[pl.ds(base, rows), lanes(tile)] = sig * (1.0 + total * (1.0 - sig))
            active[pl.ds(base, rows), lanes(tile)] = total * sig
            return 0

        lax.fori_loop(0, WIDE // rows, chunk, 0)
    out = begin([(v_slope, slope), (v_hidden, hidden)], sems)
    finish(later)
    acts = active[LEFT_U : LEFT_U + FRAMES].astype(BF)
    product = jnp.zeros((MESSAGE, 768), F32)
    for side, spot in enumerate((v_low, v_high)):
        columns = jnp.dot(acts, spot[...], preferred_element_type=F32).astype(BF)
        product += lax.dot_general(
            columns,
            grads[:, :, 768 * side : 768 * side + 768].reshape(FRAMES, 768),
            (((0,), (0,)), ((), ())),
            preferred_element_type=F32,
        )
    for j in range(MEMBERS):
        v_parts[j] = product[ROWS * j : ROWS * j + ROWS].astype(BF)
    finish(begin([(v_parts, parts.at[:, :, pl.ds(0, 768)])], sems.at[pl.ds(2, 1)]))
    finish(out)


def backward(
    gathered, low, high, upstream, across, up_beside, beyond, slope, hidden, parts,
    grad_conv, projection, message,
    got, v_low, v_high, grads, v_slope, v_hidden, v_grad, v_grad_f, v_taps, sums, v_weights, sems,
):
    needed = begin(
        [(gathered.at[:, :, pl.ds(0, 768)], got), (low, v_low), (high, v_high)], sems
    )
    later = begin(
        group_grads(upstream, across, up_beside, beyond, grads), sems.at[pl.ds(5, 6)]
    )
    last = begin(
        [(slope.at[pl.ds(LEFT_U, FRAMES)], v_slope), (hidden, v_hidden)], sems.at[pl.ds(13, 2)]
    )
    finish(needed)
    rows = got[...].reshape(MESSAGE, 768)
    for side, spot in enumerate((v_low, v_high)):
        v_weights[:, 768 * side : 768 * side + 768] = jnp.dot(
            spot[...], rows, preferred_element_type=F32
        ).astype(BF)
    finish(later)
    value = lax.dot_general(
        grads[...].reshape(FRAMES, 1536),
        v_weights[...],
        (((1,), (1,)), ((), ())),
        preferred_element_type=F32,
    )
    finish(last)
    value = (value * v_slope[...]).astype(BF)
    v_grad[...] = value
    v_grad_f[...] = value.astype(F32)
    out = begin([(v_grad, grad_conv), (v_weights, projection)], sems)
    span = 128
    sums[...] = jnp.zeros_like(sums)
    for tile in range(CHANNELS // 128):

        def piece(c, _, tile=tile):
            base = pl.multiple_of(c * span, 8)
            terms = v_grad_f[pl.ds(base, span), lanes(tile)]
            window = v_hidden[pl.ds(base + LEFT_U, span + 32), lanes(tile)]
            for b in range(8):
                slab = window[b : b + span + 24]
                for a in range(4):
                    k = 8 * a + b - 1
                    if 0 <= k < TAPS:
                        sums[k, :, lanes(tile)] += jnp.sum(
                            (terms * slab[8 * a : 8 * a + span]).reshape(span // 8, 8, 128),
                            axis=0,
                        )
            return 0

        lax.fori_loop(0, FRAMES // span, piece, 0)
    for j in range(MEMBERS):
        rows = [
            jnp.sum(sums[j, :, lanes(tile)], axis=0, keepdims=True)
            for tile in range(CHANNELS // 128)
        ]
        rows = jnp.concatenate(rows, axis=0)
        high_part = rows.astype(BF).astype(F32)
        rows = [high_part, rows - high_part, jnp.zeros((ROWS - 6, 128), F32)]
        v_taps[j] = jnp.concatenate(rows, axis=0).astype(BF)
    finish(begin([(v_taps, message.at[:, :, pl.ds(768, EXTRA)])], sems.at[pl.ds(3, 1)]))
    finish(out)


def transposed(
    grad_conv, projection, slope, slot, lent, beside, kernel,
    kept, given, v_grad, v_weights, v_slope, ups, weights, wide, total_f, v_kept, v_given, sems,
):
    yh, core = lax.axis_index("yh"), lax.axis_index("core")
    far = 128 + EDGE_H
    edges = [(slot.at[pl.ds(EDGE_H, EDGE_U)], ups.at[yh * 2 + core])]
    for i in range(2):
        edges.append(
            (
                lent.at[pl.ds(EDGE_H + EDGE_U * i, EDGE_U)],
                ups.at[(1 - yh) * 2 + core, :, pl.ds(768 * i, 768)],
            )
        )
    for i in range(4):
        row, cut = pl.ds(far + EDGE_U * i, EDGE_U), pl.ds(CHANNELS * i, CHANNELS)
        edges.append((beside.at[0, row], ups.at[yh * 2 + 1 - core, :, cut]))
        edges.append((beside.at[1, row], ups.at[(1 - yh) * 2 + 1 - core, :, cut]))
    edges += [
        (projection, v_weights),
        (slope.at[pl.ds(0, LEFT_U)], v_slope.at[pl.ds(0, LEFT_U)]),
        (slope.at[pl.ds(LEFT_U + FRAMES, EDGE_U)], v_slope.at[pl.ds(LEFT_U, EDGE_U)]),
        (grad_conv, v_grad),
        (kernel, weights),
    ]
    finish(begin(edges, sems))
    rows = jnp.concatenate([ups[0, EDGE_U - LEFT_U :], ups[3]], axis=0)
    value = lax.dot_general(
        rows, v_weights[...], (((1,), (1,)), ((), ())), preferred_element_type=F32
    )
    value = (value * v_slope[...]).astype(BF).astype(F32)
    wide[:LEFT_U] = value[:LEFT_U]
    wide[LEFT_U : LEFT_U + FRAMES] = v_grad[...].astype(F32)
    wide[LEFT_U + FRAMES :] = value[LEFT_U:]
    rows = 88
    for tile in range(CHANNELS // 128):

        def chunk(c, _, tile=tile):
            base = pl.multiple_of(c * rows, 8)
            total = jnp.zeros((rows, 128), F32)
            window = wide[pl.ds(base, rows + 32), lanes(tile)]
            for b in range(8):
                slab = window[b : b + rows + 24]
                for a in range(4):
                    k = TAPS - 8 * a - b
                    if 0 <= k < TAPS:
                        total += weights[k : k + 1, lanes(tile)] * slab[8 * a : 8 * a + rows]
            total_f[pl.ds(base, rows), lanes(tile)] = total
            return 0

        lax.fori_loop(0, LONG // rows, chunk, 0)
    for row in range(2):
        for out, side in ((v_kept, core), (v_given, 1 - core)):
            begin_row = pl.multiple_of((row * 2 + side) * 128, 128)
            out[row] = total_f[pl.ds(begin_row, BACK)].astype(BF)
    finish(begin([(v_kept, kept), (v_given, given)], sems))


def settle(
    kept, got, far, gathered, lengths, frame_grad, gloss, frames, notes, v_lengths, v_gloss, sems
):
    yh, core = lax.axis_index("yh"), lax.axis_index("core")
    sources = [(kept.at[yh], yh, core), (got.at[yh], yh, 1 - core)]
    sources += [(far.at[0], 1 - yh, core), (far.at[1], 1 - yh, 1 - core)]
    moves = [(lengths, v_lengths), (gathered.at[:, pl.ds(0, 16), pl.ds(768, EXTRA)], notes)]
    for source, a, b in sources:
        cut = pl.ds(pl.multiple_of((a * 2 + b) * CHANNELS, 128), CHANNELS)
        moves.append((source, frames.at[:, cut]))
    finish(begin(moves, sems))
    out = begin([(frames.at[pl.ds(0, 128)], frame_grad)], sems)
    mine = yh * 2 + core
    place = lax.axis_index("z") * 4 + lax.axis_index("x")
    lane = lax.broadcasted_iota(jnp.int32, (8, EXTRA), 1)
    start = jnp.zeros((8, EXTRA), F32)
    for member in range(MEMBERS):
        block = lane * 16 + member // 2
        earlier = (block < place * 4 + mine) & (lane < 8) & (lax.axis_index("rep") == member % 2)
        start += jnp.where(earlier, notes[member, :8].astype(F32), 0.0)
    start = jnp.sum(start, axis=1, keepdims=True) - (place * FRAMES + mine * 128).astype(F32)
    gloss_id = lax.broadcasted_iota(jnp.int32, (8, EXTRA), 0)
    length = v_lengths[...]
    first = jnp.sum(jnp.where(lane < gloss_id, length, 0.0), axis=1, keepdims=True) + start
    last = first + jnp.sum(jnp.where(lane == gloss_id, length, 0.0), axis=1, keepdims=True)
    at = lax.broadcasted_iota(jnp.int32, (8, 128 + SPILL), 1).astype(F32)
    covers = jnp.where((at >= first) & (at < last), 1.0, 0.0).astype(BF)
    v_gloss[...] = jnp.dot(covers, frames[...], preferred_element_type=F32)
    finish(begin([(v_gloss, gloss)], sems.at[pl.ds(1, 1)]))
    finish(out)


def pack_z(parts, out, v_parts, v_out, sems):
    finish(begin([(parts, v_parts)], sems))
    sums = []
    for q in range(4):
        total = jnp.zeros((ROWS, 896), F32)
        for x in range(4):
            for rep in range(2):
                total += v_parts[(x * 4 + q) * 2 + rep].astype(F32)
        sums.append(total)
    taps = [total[:3, 768:] + total[3:6, 768:] for total in sums]
    taps = jnp.concatenate([t[j : j + 1] for t in taps for j in range(3)], axis=1)
    high = taps.astype(BF).astype(F32)
    for z in range(8):
        at = BLOCK * (z % 2)
        halves = [sums[z // 2][at + 12 * side : at + 12 * side + BLOCK, :768] for side in range(2)]
        rows = [jnp.concatenate(halves, axis=1), high, taps - high]
        v_out[z] = jnp.concatenate(rows, axis=0).astype(BF)
    finish(begin([(v_out, out)], sems))


def unpack_z(got, weights, taps, v_got, v_weights, v_taps, sems):
    finish(begin([(got, v_got)], sems))
    total = v_got[0].astype(F32)
    for z in range(1, 8):
        total += v_got[z].astype(F32)
    total = total * (1.0 / math.sqrt(2 * 16384))
    v_weights[...] = total[:BLOCK]
    for peer in range(MEMBERS):
        v_taps[peer] = total[6:7] + total[7:8]
    finish(begin([(v_taps, taps), (v_weights, weights)], sems))


def arrange(got, out, v_got, v_out, sems):
    finish(begin([(got, v_got)], sems))
    for k in range(TAPS):
        v_out[k : k + 1] = v_got[k]
    finish(begin([(v_out, out)], sems))


def call(kernel, outs, scratch, megabytes, *args, alias=None, flops=200_000_000):
    shapes = [jax.ShapeDtypeStruct(shape, dtype) for shape, dtype in outs]
    size = sum(math.prod(s.shape) * s.dtype.itemsize for s in list(args) + shapes)
    return pl.pallas_call(
        kernel,
        out_shape=shapes,
        in_specs=[pl.BlockSpec(memory_space=pltpu.HBM)] * len(args),
        out_specs=[pl.BlockSpec(memory_space=pltpu.HBM)] * len(shapes),
        scratch_shapes=[pltpu.VMEM(shape, dtype) for shape, dtype in scratch]
        + [pltpu.SemaphoreType.DMA((48,))],
        input_output_aliases=alias or {},
        compiler_params=pltpu.CompilerParams(vmem_limit_bytes=megabytes * 2**20),
        cost_estimate=pl.CostEstimate(
            flops=flops, bytes_accessed=size, transcendentals=0
        ),
    )(*args)


def body(hidden_in, upstream, out_weight, conv_kernel, durations):
    yh, core = lax.axis_index("yh"), lax.axis_index("core")
    quarter = yh * 2 + core
    hidden, grads = hidden_in[0], upstream[0]
    lengths = jnp.broadcast_to(
        jnp.pad(durations.astype(F32), ((0, 0), (0, EXTRA - durations.shape[1]))), (8, EXTRA)
    )

    rows, share, edge = call(
        spread,
        [((8, 8, 1536), BF), ((384, 768), BF), ((EDGE_H + EDGE_U, 1536), BF)],
        [
            ((BLOCK, 1536), BF), ((1, 8), jnp.int32), ((8, 1536), BF), ((384, 768), BF),
            ((EDGE_H + EDGE_U, 1536), BF),
        ],
        56,
        out_weight, durations, hidden, grads,
    )
    ends = [(4 * i + 3, 4 * i + 4) for i in range(31)]
    slot = lax.ppermute(edge, ("z", "x", "yh", "core"), ends + [(b, a) for a, b in ends])
    rows = lax.all_to_all(rows, "z", 0, 0, tiled=True)
    across = lax.ppermute(share, "yh", SWAP)
    up_beside = lax.ppermute(grads, "core", SWAP)
    beyond = lax.ppermute(across, "core", SWAP)
    [lent] = call(lend, [((SHARE, 768), BF)], [((SHARE, 768), BF)], 16, slot)
    lent = lax.ppermute(lent, "yh", SWAP)
    message = ((MEMBERS, ROWS, 768 + EXTRA), BF)
    [plane] = call(
        pack,
        [message],
        [((4 * ROWS, 768 + EXTRA), F32), ((8, 8, 1536), BF), ((4, ROWS, 768 + EXTRA), BF)],
        56,
        rows,
    )
    handed = ((2, HANDED, CHANNELS), BF)
    [beside] = call(relay, [handed], [handed], 16, hidden, slot, across, lent, flops=30_000_000_000)
    rows = lax.all_to_all(plane, PLANE, 0, 0, tiled=True)
    beside = lax.ppermute(beside, "core", SWAP)
    kernel_f = lax.dynamic_slice_in_dim(
        jnp.pad(conv_kernel, ((0, 1), (0, 0))), quarter * CHANNELS, CHANNELS, 1
    ).astype(F32)
    spot = ((CHANNELS, MESSAGE), BF)
    low, high = placement(0), placement(1)
    frames_f = ((FRAMES, CHANNELS), F32)
    wide_f = ((LEFT_H + FRAMES + EDGE_H, CHANNELS), F32)
    slope_f = ((WIDE, CHANNELS), F32)
    all_grads = ((4, 128, 1536), BF)
    sent = ((MEMBERS, ROWS, 768), BF)
    kernel_shape = ((TAPS + 1, CHANNELS), F32)
    slope, hidden_f, parts = call(
        convolve,
        [slope_f, wide_f, message],
        [
            all_grads, ((4, 128 + EDGE_H, CHANNELS), BF), kernel_shape, spot, spot, slope_f, wide_f,
            sent, slope_f,
        ],
        56,
        hidden, slot, across, lent, beside, grads, up_beside, beyond, kernel_f, low, high,
    )
    grad_conv, projection, parts = call(
        backward,
        [
            ((FRAMES, CHANNELS), BF), ((CHANNELS, 1536), BF), message,
        ],
        [
            sent, spot, spot, all_grads, frames_f, wide_f, ((FRAMES, CHANNELS), BF), frames_f,
            ((MEMBERS, ROWS, EXTRA), BF), ((TAPS + 1, 8, CHANNELS), F32),
            ((CHANNELS, 1536), BF),
        ],
        56,
        rows, low, high, grads, across, up_beside, beyond, slope, hidden_f, parts,
        alias={9: 2},
    )

    parts = lax.all_to_all(parts, PLANE, 0, 0, tiled=True)
    [parts] = call(
        pack_z,
        [((8, 8, 1536), BF)],
        [message, ((8, 8, 1536), BF)],
        16,
        parts,
    )
    parts = lax.all_to_all(parts, "z", 0, 0, tiled=True)
    weight_grad, taps_all = call(
        unpack_z,
        [((BLOCK, 1536), F32), ((32, 1, 1536), F32)],
        [((8, 8, 1536), BF), ((BLOCK, 1536), F32), ((32, 1, 1536), F32)],
        16,
        parts,
    )
    taps_all = lax.all_to_all(taps_all, PLANE, 0, 0, tiled=True)
    [kernel_grad] = call(
        arrange,
        [((TAPS, 1536), F32)],
        [((32, 1, 1536), F32), ((TAPS, 1536), F32)],
        16,
        taps_all,
    )

    back = ((2, BACK, CHANNELS), BF)
    kept, given = call(
        transposed,
        [back, back],
        [
            ((FRAMES, CHANNELS), BF), ((CHANNELS, 1536), BF), ((LEFT_U + EDGE_U, CHANNELS), F32),
            ((4, EDGE_U, 1536), BF), kernel_shape,
            slope_f, ((LONG, CHANNELS), F32), back, back,
        ],
        56,
        grad_conv, projection, slope, slot, lent, beside, kernel_f,
    )
    got = lax.ppermute(given, "core", SWAP)
    far = jnp.stack(
        [lax.dynamic_index_in_dim(part, 1 - yh, 0, False) for part in (kept, got)]
    )
    far = lax.ppermute(far, "yh", SWAP)
    frame_grad, gloss = call(
        settle,
        [((128, 1536), BF), ((8, 1536), F32)],
        [
            ((BACK, 1536), BF), ((MEMBERS, 16, EXTRA), BF), ((8, EXTRA), F32),
            ((8, 1536), F32),
        ],
        16,
        kept, got, far, rows, lengths,
    )
    return (frame_grad[None], gloss[None], weight_grad, kernel_grad)


def solution(mesh):
    fine = Mesh(mesh.devices.reshape(SIZES), AXES)
    seq = ("z", "x", "yh", "core")
    rows = P(seq + ("rep",), None)
    in_specs = (P("rep", seq, None), P("rep", seq, None), rows, P(), P("rep", seq))
    out_specs = (P("rep", seq, None), P("rep", seq, None), rows, P())
    return jax.shard_map(
        body, mesh=fine, in_specs=in_specs, out_specs=out_specs, check_vma=False
    )
```

```python
import math

import jax
import jax.numpy as jnp
import numpy as np
from jax import lax
from jax.experimental import pallas as pl
from jax.experimental.pallas import tpu as pltpu
from jax.sharding import Mesh
from jax.sharding import PartitionSpec as P

AXES = ("z", "x", "yh", "core", "rep")
SIZES = (8, 4, 2, 2, 2)
GROUP = ("yh", "core")
PLANE = ("x", "yh", "core", "rep")
QUARTERS = 4
BLOCK = 6
EXTRA = 128
MEMBERS, ROWS = 32, 24
MESSAGE = MEMBERS * ROWS
FRAMES, CHANNELS, TAPS = 512, 384, 31
EDGE_H, EDGE_U, SPILL = 48, 32, 16
LEFT_H, LEFT_U = 32, 16
WIDE = FRAMES + LEFT_U + EDGE_U
LONG = FRAMES + SPILL
SHARE = EDGE_H + 2 * EDGE_U
HANDED = EDGE_H + 4 * EDGE_U
BACK = 128 + SPILL
SWAP = [(0, 1), (1, 0)]
BF = jnp.bfloat16
F32 = jnp.float32


def placement(side):
    out = np.zeros((CHANNELS, MESSAGE), np.float32)
    for zl in range(2):
        for member in range(MEMBERS):
            for r in range(BLOCK):
                row = (zl * MEMBERS + member) * BLOCK + r
                out[row, member * ROWS + 12 * side + zl * BLOCK + r] = 1
    return jnp.asarray(out, BF)


def lanes(tile):
    return slice(tile * 128, tile * 128 + 128)


def begin(pairs, sems):
    copies = [pltpu.make_async_copy(a, b, sems.at[i]) for i, (a, b) in enumerate(pairs)]
    for copy in copies:
        copy.start()
    return copies


def finish(copies):
    for copy in copies:
        copy.wait()


def spread(
    weights, durations, hidden, upstream, out, share, edge,
    got, lengths, block, v_share, v_edge, sems,
):
    yh, core = lax.axis_index("yh"), lax.axis_index("core")
    other = pl.ds(pl.multiple_of((1 - yh) * 768, 128), 768)
    last = (yh + core) // 2
    from_h = pl.ds(pl.multiple_of(last * (128 - EDGE_H), 16), EDGE_H)
    from_u = pl.ds(pl.multiple_of(last * (128 - EDGE_U), 16), EDGE_U)
    taken = begin(
        [
            (hidden.at[:, other], v_share.at[pl.ds(0, 128)]),
            (upstream.at[:, pl.ds(0, 768)], v_share.at[pl.ds(128, 128)]),
            (upstream.at[:, pl.ds(768, 768)], v_share.at[pl.ds(256, 128)]),
            (hidden.at[from_h], v_edge.at[pl.ds(0, EDGE_H)]),
            (upstream.at[from_u], v_edge.at[pl.ds(EDGE_H, EDGE_U)]),
        ],
        sems.at[pl.ds(9, 5)],
    )
    finish(begin([(weights, got), (durations, lengths)], sems))
    lane = lax.broadcasted_iota(jnp.int32, (1, 1536), 1)
    total = jnp.sum(lengths[...].astype(F32), axis=1, keepdims=True)
    note = jnp.where(lane == lax.axis_index("z"), jnp.broadcast_to(total, (1, 1536)), 0.0)
    rows = [got[...].astype(F32), note, jnp.zeros((1, 1536), F32)]
    block[...] = jnp.concatenate(rows, axis=0).astype(BF)
    sent = begin([(block, out.at[peer]) for peer in range(8)], sems)
    finish(taken)
    finish(begin([(v_share, share), (v_edge, edge)], sems.at[pl.ds(9, 2)]))
    finish(sent)


def lend(slot, out, v_out, sems):
    other = pl.ds(pl.multiple_of((1 - lax.axis_index("yh")) * 768, 128), 768)
    up = pl.ds(EDGE_H, EDGE_U)
    finish(
        begin(
            [
                (slot.at[pl.ds(0, EDGE_H), other], v_out.at[pl.ds(0, EDGE_H)]),
                (slot.at[up, pl.ds(0, 768)], v_out.at[pl.ds(EDGE_H, EDGE_U)]),
                (slot.at[up, pl.ds(768, 768)], v_out.at[pl.ds(EDGE_H + EDGE_U, EDGE_U)]),
            ],
            sems,
        )
    )
    finish(begin([(v_out, out)], sems))


def pack(gathered, plane, rows, got, block, sems):
    finish(begin([(gathered, got)], sems))
    note = jnp.zeros((8, EXTRA), F32)
    for z in range(8):
        block_z = got[z].astype(F32)
        at = ROWS * (z // 2) + BLOCK * (z % 2)
        rows[at : at + BLOCK, :768] = block_z[:BLOCK, :768]
        rows[at + 12 : at + 12 + BLOCK, :768] = block_z[:BLOCK, 768:]
        note += jnp.broadcast_to(block_z[BLOCK : BLOCK + 1, :EXTRA], (8, EXTRA))
    rows[:, 768:] = jnp.concatenate([note] * (ROWS // 2), axis=0)
    sent = []
    for q in range(4):
        block[q] = rows[ROWS * q : ROWS * q + ROWS].astype(BF)
        members = [j for j in range(MEMBERS) if (j // 2) % 4 == q]
        sent += begin([(block.at[q], plane.at[j]) for j in members], sems.at[pl.ds(8 * q, 8)])
    finish(sent)


def relay(hidden, across, beside, v_beside, sems):
    yh, core = lax.axis_index("yh"), lax.axis_index("core")
    other = pl.ds(pl.multiple_of((yh * 2 + 1 - core) * CHANNELS, 128), CHANNELS)
    part = pl.ds(pl.multiple_of((1 - core) * CHANNELS, 128), CHANNELS)
    moves = [(hidden.at[:, other], v_beside.at[0]), (across.at[pl.ds(0, 128), part], v_beside.at[1])]
    finish(begin(moves, sems))
    finish(begin([(v_beside, beside)], sems))


def relay_edges(slot, lent, beside, v_beside, sems):
    yh, core = lax.axis_index("yh"), lax.axis_index("core")
    other = pl.ds(pl.multiple_of((yh * 2 + 1 - core) * CHANNELS, 128), CHANNELS)
    part = pl.ds(pl.multiple_of((1 - core) * CHANNELS, 128), CHANNELS)
    edge = pl.ds(0, EDGE_H)
    moves = [
        (slot.at[edge, other], v_beside.at[0, edge]),
        (lent.at[edge, part], v_beside.at[1, edge]),
    ]
    for i in range(4):
        cut = pl.ds((i % 2) * CHANNELS, CHANNELS)
        row = pl.ds(EDGE_H + EDGE_U * i, EDGE_U)
        wide = pl.ds(i * CHANNELS, CHANNELS)
        moves.append((slot.at[pl.ds(EDGE_H, EDGE_U), wide], v_beside.at[0, row]))
        moves.append((lent.at[pl.ds(EDGE_H + EDGE_U * (i // 2), EDGE_U), cut], v_beside.at[1, row]))
    finish(begin(moves, sems))
    finish(begin([(v_beside, beside)], sems))


def group_grads(upstream, across, beside, beyond, grads):
    yh, core = lax.axis_index("yh"), lax.axis_index("core")
    moves = [(upstream, grads.at[yh * 2 + core]), (beside, grads.at[yh * 2 + 1 - core])]
    for source, place in ((across, 2 - 2 * yh + core), (beyond, 3 - 2 * yh - core)):
        for i in range(2):
            rows, cut = pl.ds(128 + 128 * i, 128), pl.ds(768 * i, 768)
            moves.append((source.at[rows], grads.at[place, :, cut]))
    return moves


def convolve(
    own, slot, across, lent, beside, edges, upstream, up_beside, beyond, kernel, low, high,
    slope, hidden, parts,
    grads, frames, weights, v_low, v_high, v_slope, v_hidden, v_parts, active, sems,
):
    yh, core = lax.axis_index("yh"), lax.axis_index("core")
    part = pl.ds(pl.multiple_of(core * CHANNELS, 128), CHANNELS)
    mine = pl.ds(pl.multiple_of((yh * 2 + core) * CHANNELS, 128), CHANNELS)
    block, edge = pl.ds(0, 128), pl.ds(0, EDGE_H)
    needed = begin(
        [
            (own.at[:, mine], frames.at[yh * 2 + core, pl.ds(0, 128)]),
            (slot.at[pl.ds(0, EDGE_H), mine], frames.at[yh * 2 + core, pl.ds(128, EDGE_H)]),
            (across.at[pl.ds(0, 128), part], frames.at[(1 - yh) * 2 + core, pl.ds(0, 128)]),
            (lent.at[pl.ds(0, EDGE_H), part], frames.at[(1 - yh) * 2 + core, pl.ds(128, EDGE_H)]),
            (beside.at[0], frames.at[yh * 2 + 1 - core, block]),
            (beside.at[1], frames.at[(1 - yh) * 2 + 1 - core, block]),
            (edges.at[0, edge], frames.at[yh * 2 + 1 - core, pl.ds(128, EDGE_H)]),
            (edges.at[1, edge], frames.at[(1 - yh) * 2 + 1 - core, pl.ds(128, EDGE_H)]),
            (kernel, weights),
        ],
        sems,
    )
    later = begin(
        group_grads(upstream, across, up_beside, beyond, grads) + [(low, v_low), (high, v_high)],
        sems.at[pl.ds(10, 8)],
    )
    finish(needed)
    v_hidden[:LEFT_H] = frames[0, 128 + EDGE_H - LEFT_H :].astype(F32)
    for b in range(4):
        v_hidden[LEFT_H + 128 * b : LEFT_H + 128 * b + 128] = frames[b, :128].astype(F32)
    v_hidden[LEFT_H + FRAMES :] = frames[3, 128:].astype(F32)
    rows = 112
    for tile in range(CHANNELS // 128):

        def chunk(c, _, tile=tile):
            base = pl.multiple_of(c * rows, 8)
            total = jnp.zeros((rows, 128), F32)
            window = v_hidden[pl.ds(base, rows + 32), lanes(tile)]
            for b in range(8):
                slab = window[b : b + rows + 24]
                for a in range(4):
                    k = 8 * a + b - 1
                    if 0 <= k < TAPS:
                        total += weights[k : k + 1, lanes(tile)] * slab[8 * a : 8 * a + rows]
            sig = jax.nn.sigmoid(total)
            v_slope[pl.ds(base, rows), lanes(tile)] = sig * (1.0 + total * (1.0 - sig))
            active[pl.ds(base, rows), lanes(tile)] = total * sig
            return 0

        lax.fori_loop(0, WIDE // rows, chunk, 0)
    out = begin([(v_slope, slope), (v_hidden, hidden)], sems)
    finish(later)
    acts = active[LEFT_U : LEFT_U + FRAMES].astype(BF)
    product = jnp.zeros((MESSAGE, 768), F32)
    for side, spot in enumerate((v_low, v_high)):
        columns = jnp.dot(acts, spot[...], preferred_element_type=F32).astype(BF)
        product += lax.dot_general(
            columns,
            grads[:, :, 768 * side : 768 * side + 768].reshape(FRAMES, 768),
            (((0,), (0,)), ((), ())),
            preferred_element_type=F32,
        )
    for j in range(MEMBERS):
        v_parts[j] = product[ROWS * j : ROWS * j + ROWS].astype(BF)
    finish(begin([(v_parts, parts.at[:, :, pl.ds(0, 768)])], sems.at[pl.ds(2, 1)]))
    finish(out)


def backward(
    gathered, low, high, upstream, across, up_beside, beyond, slope, hidden, parts,
    grad_conv, projection, message,
    got, v_low, v_high, grads, v_slope, v_hidden, v_grad, v_grad_f, v_taps, sums, v_weights, sems,
):
    needed = begin(
        [(gathered.at[:, :, pl.ds(0, 768)], got), (low, v_low), (high, v_high)], sems
    )
    later = begin(
        group_grads(upstream, across, up_beside, beyond, grads), sems.at[pl.ds(5, 6)]
    )
    last = begin(
        [(slope.at[pl.ds(LEFT_U, FRAMES)], v_slope), (hidden, v_hidden)], sems.at[pl.ds(13, 2)]
    )
    finish(needed)
    rows = got[...].reshape(MESSAGE, 768)
    for side, spot in enumerate((v_low, v_high)):
        v_weights[:, 768 * side : 768 * side + 768] = jnp.dot(
            spot[...], rows, preferred_element_type=F32
        ).astype(BF)
    finish(later)
    value = lax.dot_general(
        grads[...].reshape(FRAMES, 1536),
        v_weights[...],
        (((1,), (1,)), ((), ())),
        preferred_element_type=F32,
    )
    finish(last)
    value = (value * v_slope[...]).astype(BF)
    v_grad[...] = value
    v_grad_f[...] = value.astype(F32)
    out = begin([(v_grad, grad_conv), (v_weights, projection)], sems)
    span = 128
    sums[...] = jnp.zeros_like(sums)
    for tile in range(CHANNELS // 128):

        def piece(c, _, tile=tile):
            base = pl.multiple_of(c * span, 8)
            terms = v_grad_f[pl.ds(base, span), lanes(tile)]
            window = v_hidden[pl.ds(base + LEFT_U, span + 32), lanes(tile)]
            for b in range(8):
                slab = window[b : b + span + 24]
                for a in range(4):
                    k = 8 * a + b - 1
                    if 0 <= k < TAPS:
                        sums[k, :, lanes(tile)] += jnp.sum(
                            (terms * slab[8 * a : 8 * a + span]).reshape(span // 8, 8, 128),
                            axis=0,
                        )
            return 0

        lax.fori_loop(0, FRAMES // span, piece, 0, unroll=True)
    for j in range(MEMBERS):
        rows = [
            jnp.sum(sums[j, :, lanes(tile)], axis=0, keepdims=True)
            for tile in range(CHANNELS // 128)
        ]
        rows = jnp.concatenate(rows, axis=0)
        high_part = rows.astype(BF).astype(F32)
        rows = [high_part, rows - high_part, jnp.zeros((ROWS - 6, 128), F32)]
        v_taps[j] = jnp.concatenate(rows, axis=0).astype(BF)
    finish(begin([(v_taps, message.at[:, :, pl.ds(768, EXTRA)])], sems.at[pl.ds(3, 1)]))
    finish(out)


def transposed(
    grad_conv, projection, slope, slot, lent, beside, kernel,
    kept, given, v_grad, v_weights, v_slope, ups, weights, wide, total_f, v_kept, v_given, sems,
):
    yh, core = lax.axis_index("yh"), lax.axis_index("core")
    edges = [(slot.at[pl.ds(EDGE_H, EDGE_U)], ups.at[yh * 2 + core])]
    for i in range(2):
        edges.append(
            (
                lent.at[pl.ds(EDGE_H + EDGE_U * i, EDGE_U)],
                ups.at[(1 - yh) * 2 + core, :, pl.ds(768 * i, 768)],
            )
        )
    for i in range(4):
        row, cut = pl.ds(EDGE_H + EDGE_U * i, EDGE_U), pl.ds(CHANNELS * i, CHANNELS)
        edges.append((beside.at[0, row], ups.at[yh * 2 + 1 - core, :, cut]))
        edges.append((beside.at[1, row], ups.at[(1 - yh) * 2 + 1 - core, :, cut]))
    edges += [
        (projection, v_weights),
        (slope.at[pl.ds(0, LEFT_U)], v_slope.at[pl.ds(0, LEFT_U)]),
        (slope.at[pl.ds(LEFT_U + FRAMES, EDGE_U)], v_slope.at[pl.ds(LEFT_U, EDGE_U)]),
        (grad_conv, v_grad),
        (kernel, weights),
    ]
    finish(begin(edges, sems))
    rows = jnp.concatenate([ups[0, EDGE_U - LEFT_U :], ups[3]], axis=0)
    value = lax.dot_general(
        rows, v_weights[...], (((1,), (1,)), ((), ())), preferred_element_type=F32
    )
    value = (value * v_slope[...]).astype(BF).astype(F32)
    wide[:LEFT_U] = value[:LEFT_U]
    wide[LEFT_U : LEFT_U + FRAMES] = v_grad[...].astype(F32)
    wide[LEFT_U + FRAMES :] = value[LEFT_U:]
    rows = 88
    for tile in range(CHANNELS // 128):

        def chunk(c, _, tile=tile):
            base = pl.multiple_of(c * rows, 8)
            total = jnp.zeros((rows, 128), F32)
            window = wide[pl.ds(base, rows + 32), lanes(tile)]
            for b in range(8):
                slab = window[b : b + rows + 24]
                for a in range(4):
                    k = TAPS - 8 * a - b
                    if 0 <= k < TAPS:
                        total += weights[k : k + 1, lanes(tile)] * slab[8 * a : 8 * a + rows]
            total_f[pl.ds(base, rows), lanes(tile)] = total
            return 0

        lax.fori_loop(0, LONG // rows, chunk, 0)
    for row in range(2):
        for out, side in ((v_kept, core), (v_given, 1 - core)):
            begin_row = pl.multiple_of((row * 2 + side) * 128, 128)
            out[row] = total_f[pl.ds(begin_row, BACK)].astype(BF)
    finish(begin([(v_kept, kept), (v_given, given)], sems))


def settle(
    kept, got, far, gathered, lengths, frame_grad, gloss, frames, notes, v_lengths, v_gloss, sems
):
    yh, core = lax.axis_index("yh"), lax.axis_index("core")
    sources = [(kept.at[yh], yh, core), (got.at[yh], yh, 1 - core)]
    sources += [(far.at[0], 1 - yh, core), (far.at[1], 1 - yh, 1 - core)]
    moves = [(lengths, v_lengths), (gathered.at[:, pl.ds(0, 16), pl.ds(768, EXTRA)], notes)]
    for source, a, b in sources:
        cut = pl.ds(pl.multiple_of((a * 2 + b) * CHANNELS, 128), CHANNELS)
        moves.append((source, frames.at[:, cut]))
    finish(begin(moves, sems))
    out = begin([(frames.at[pl.ds(0, 128)], frame_grad)], sems)
    mine = yh * 2 + core
    place = lax.axis_index("z") * 4 + lax.axis_index("x")
    lane = lax.broadcasted_iota(jnp.int32, (8, EXTRA), 1)
    start = jnp.zeros((8, EXTRA), F32)
    for member in range(MEMBERS):
        block = lane * 16 + member // 2
        earlier = (block < place * 4 + mine) & (lane < 8) & (lax.axis_index("rep") == member % 2)
        start += jnp.where(earlier, notes[member, :8].astype(F32), 0.0)
    start = jnp.sum(start, axis=1, keepdims=True) - (place * FRAMES + mine * 128).astype(F32)
    gloss_id = lax.broadcasted_iota(jnp.int32, (8, EXTRA), 0)
    length = v_lengths[...]
    first = jnp.sum(jnp.where(lane < gloss_id, length, 0.0), axis=1, keepdims=True) + start
    last = first + jnp.sum(jnp.where(lane == gloss_id, length, 0.0), axis=1, keepdims=True)
    at = lax.broadcasted_iota(jnp.int32, (8, 128 + SPILL), 1).astype(F32)
    covers = jnp.where((at >= first) & (at < last), 1.0, 0.0).astype(BF)
    v_gloss[...] = jnp.dot(covers, frames[...], preferred_element_type=F32)
    finish(begin([(v_gloss, gloss)], sems.at[pl.ds(1, 1)]))
    finish(out)


def pack_z(parts, out, sems):
    sums = []
    for q in range(4):
        total = jnp.zeros((ROWS, 896), F32)
        for x in range(4):
            for rep in range(2):
                total += parts[(x * 4 + q) * 2 + rep].astype(F32)
        sums.append(total)
    taps = [total[:3, 768:] + total[3:6, 768:] for total in sums]
    taps = jnp.concatenate([t[j : j + 1] for t in taps for j in range(3)], axis=1)
    high = taps.astype(BF).astype(F32)
    for z in range(8):
        at = BLOCK * (z % 2)
        halves = [sums[z // 2][at + 12 * side : at + 12 * side + BLOCK, :768] for side in range(2)]
        rows = [jnp.concatenate(halves, axis=1), high, taps - high]
        out[z] = jnp.concatenate(rows, axis=0).astype(BF)


def unpack_z(got, weights, taps, sems):
    total = got[0].astype(F32)
    for z in range(1, 8):
        total += got[z].astype(F32)
    total = total * (1.0 / math.sqrt(2 * 16384))
    weights[...] = total[:BLOCK]
    for peer in range(MEMBERS):
        taps[peer] = total[6:7] + total[7:8]


def arrange(got, out, v_out, sems):
    for k in range(TAPS):
        v_out[k : k + 1] = got[k]
    finish(begin([(v_out, out)], sems))


def call(
    kernel, outs, scratch, megabytes, *args, alias=None, flops=200_000_000, near=(), near_out=()
):
    def space(vmem):
        return pl.BlockSpec(memory_space=pltpu.VMEM if vmem else pltpu.HBM)

    shapes = [jax.ShapeDtypeStruct(shape, dtype) for shape, dtype in outs]
    size = sum(math.prod(s.shape) * s.dtype.itemsize for s in list(args) + shapes)
    return pl.pallas_call(
        kernel,
        out_shape=shapes,
        in_specs=[space(i in near) for i in range(len(args))],
        out_specs=[space(i in near_out) for i in range(len(shapes))],
        scratch_shapes=[pltpu.VMEM(shape, dtype) for shape, dtype in scratch]
        + [pltpu.SemaphoreType.DMA((48,))],
        input_output_aliases=alias or {},
        compiler_params=pltpu.CompilerParams(vmem_limit_bytes=megabytes * 2**20),
        cost_estimate=pl.CostEstimate(
            flops=flops, bytes_accessed=size, transcendentals=0
        ),
    )(*args)


def body(hidden_in, upstream, out_weight, conv_kernel, durations):
    yh, core = lax.axis_index("yh"), lax.axis_index("core")
    quarter = yh * 2 + core
    hidden, grads = hidden_in[0], upstream[0]
    lengths = jnp.broadcast_to(
        jnp.pad(durations.astype(F32), ((0, 0), (0, EXTRA - durations.shape[1]))), (8, EXTRA)
    )

    rows, share, edge = call(
        spread,
        [((8, 8, 1536), BF), ((384, 768), BF), ((EDGE_H + EDGE_U, 1536), BF)],
        [
            ((BLOCK, 1536), BF), ((1, 8), jnp.int32), ((8, 1536), BF), ((384, 768), BF),
            ((EDGE_H + EDGE_U, 1536), BF),
        ],
        56,
        out_weight, durations, hidden, grads,
    )
    ends = [(4 * i + 3, 4 * i + 4) for i in range(31)]
    slot = lax.ppermute(edge, ("z", "x", "yh", "core"), ends + [(b, a) for a, b in ends])
    rows = lax.all_to_all(rows, "z", 0, 0, tiled=True)
    across = lax.ppermute(share, "yh", SWAP)
    up_beside = lax.ppermute(grads, "core", SWAP)
    beyond = lax.ppermute(across, "core", SWAP)
    [lent] = call(lend, [((SHARE, 768), BF)], [((SHARE, 768), BF)], 16, slot)
    lent = lax.ppermute(lent, "yh", SWAP)
    message = ((MEMBERS, ROWS, 768 + EXTRA), BF)
    [plane] = call(
        pack,
        [message],
        [((4 * ROWS, 768 + EXTRA), F32), ((8, 8, 1536), BF), ((4, ROWS, 768 + EXTRA), BF)],
        56,
        rows,
    )
    handed = ((2, 128, CHANNELS), BF)
    [beside] = call(relay, [handed], [handed], 16, hidden, across, flops=3_000_000_000)
    handed = ((2, HANDED, CHANNELS), BF)
    [edges] = call(relay_edges, [handed], [handed], 16, slot, lent, flops=30_000_000_000)
    rows = lax.all_to_all(plane, PLANE, 0, 0, tiled=True)
    beside = lax.ppermute(beside, "core", SWAP)
    edges = lax.ppermute(edges, "core", SWAP)
    kernel_f = lax.dynamic_slice_in_dim(
        jnp.pad(conv_kernel, ((0, 1), (0, 0))), quarter * CHANNELS, CHANNELS, 1
    ).astype(F32)
    spot = ((CHANNELS, MESSAGE), BF)
    low, high = placement(0), placement(1)
    frames_f = ((FRAMES, CHANNELS), F32)
    wide_f = ((LEFT_H + FRAMES + EDGE_H, CHANNELS), F32)
    slope_f = ((WIDE, CHANNELS), F32)
    all_grads = ((4, 128, 1536), BF)
    sent = ((MEMBERS, ROWS, 768), BF)
    kernel_shape = ((TAPS + 1, CHANNELS), F32)
    slope, hidden_f, parts = call(
        convolve,
        [slope_f, wide_f, message],
        [
            all_grads, ((4, 128 + EDGE_H, CHANNELS), BF), kernel_shape, spot, spot, slope_f, wide_f,
            sent, slope_f,
        ],
        56,
        hidden, slot, across, lent, beside, edges, grads, up_beside, beyond, kernel_f, low, high,
    )
    grad_conv, projection, parts = call(
        backward,
        [
            ((FRAMES, CHANNELS), BF), ((CHANNELS, 1536), BF), message,
        ],
        [
            sent, spot, spot, all_grads, frames_f, wide_f, ((FRAMES, CHANNELS), BF), frames_f,
            ((MEMBERS, ROWS, EXTRA), BF), ((TAPS + 1, 8, CHANNELS), F32),
            ((CHANNELS, 1536), BF),
        ],
        56,
        rows, low, high, grads, across, up_beside, beyond, slope, hidden_f, parts,
        alias={9: 2},
    )

    parts = lax.all_to_all(parts, PLANE, 0, 0, tiled=True)
    [parts] = call(
        pack_z,
        [((8, 8, 1536), BF)],
        [],
        16,
        parts,
        near=(0,),
        near_out=(0,),
    )
    parts = lax.all_to_all(parts, "z", 0, 0, tiled=True)
    weight_grad, taps_all = call(
        unpack_z,
        [((BLOCK, 1536), F32), ((32, 1, 1536), F32)],
        [],
        16,
        parts,
        near=(0,),
        near_out=(0, 1),
    )
    taps_all = lax.all_to_all(taps_all, PLANE, 0, 0, tiled=True)
    [kernel_grad] = call(
        arrange,
        [((TAPS, 1536), F32)],
        [((TAPS, 1536), F32)],
        16,
        taps_all,
        near=(0,),
    )

    back = ((2, BACK, CHANNELS), BF)
    kept, given = call(
        transposed,
        [back, back],
        [
            ((FRAMES, CHANNELS), BF), ((CHANNELS, 1536), BF), ((LEFT_U + EDGE_U, CHANNELS), F32),
            ((4, EDGE_U, 1536), BF), kernel_shape,
            slope_f, ((LONG, CHANNELS), F32), back, back,
        ],
        56,
        grad_conv, projection, slope, slot, lent, edges, kernel_f,
    )
    got = lax.ppermute(given, "core", SWAP)
    far = jnp.stack(
        [lax.dynamic_index_in_dim(part, 1 - yh, 0, False) for part in (kept, got)]
    )
    far = lax.ppermute(far, "yh", SWAP)
    frame_grad, gloss = call(
        settle,
        [((128, 1536), BF), ((8, 1536), F32)],
        [
            ((BACK, 1536), BF), ((MEMBERS, 16, EXTRA), BF), ((8, EXTRA), F32),
            ((8, 1536), F32),
        ],
        16,
        kept, got, far, rows, lengths,
    )
    return (frame_grad[None], gloss[None], weight_grad, kernel_grad)


def solution(mesh):
    fine = Mesh(mesh.devices.reshape(SIZES), AXES)
    seq = ("z", "x", "yh", "core")
    rows = P(seq + ("rep",), None)
    in_specs = (P("rep", seq, None), P("rep", seq, None), rows, P(), P("rep", seq))
    out_specs = (P("rep", seq, None), P("rep", seq, None), rows, P())
    return jax.shard_map(
        body, mesh=fine, in_specs=in_specs, out_specs=out_specs, check_vma=False
    )
```

```python
import math

import jax
import jax.numpy as jnp
import numpy as np
from jax import lax
from jax.experimental import pallas as pl
from jax.experimental.pallas import tpu as pltpu
from jax.sharding import Mesh
from jax.sharding import PartitionSpec as P

AXES = ("z", "x", "yh", "core", "rep")
SIZES = (8, 4, 2, 2, 2)
GROUP = ("yh", "core")
PLANE = ("x", "yh", "core", "rep")
QUARTERS = 4
BLOCK = 6
EXTRA = 128
MEMBERS, ROWS, LANES = 32, 8, 2304
MESSAGE = MEMBERS * ROWS
FRAMES, CHANNELS, TAPS = 512, 384, 31
EDGE_H, EDGE_U, SPILL = 48, 32, 16
LEFT_H, LEFT_U = 32, 16
WIDE = FRAMES + LEFT_U + EDGE_U
LONG = FRAMES + SPILL
SHARE = EDGE_H + 2 * EDGE_U
HANDED = EDGE_H + 4 * EDGE_U
BACK = 128 + SPILL
SWAP = [(0, 1), (1, 0)]
BF = jnp.bfloat16
F32 = jnp.float32


def placement(part):
    out = np.zeros((CHANNELS, MESSAGE), np.float32)
    for zl in range(2):
        for member in range(MEMBERS):
            for r in range(BLOCK):
                row, i = (zl * MEMBERS + member) * BLOCK + r, zl * BLOCK + r
                if part == 0 and i < ROWS:
                    out[row, member * ROWS + i] = 1
                if part > 0 and i >= ROWS:
                    out[row, member * ROWS + 2 * (i - ROWS) + part - 1] = 1
    return jnp.asarray(out, BF)


def lanes(tile):
    return slice(tile * 128, tile * 128 + 128)


def begin(pairs, sems):
    copies = [pltpu.make_async_copy(a, b, sems.at[i]) for i, (a, b) in enumerate(pairs)]
    for copy in copies:
        copy.start()
    return copies


def finish(copies):
    for copy in copies:
        copy.wait()


def spread(
    weights, durations, hidden, upstream, out, share, edge,
    got, lengths, block, v_share, v_edge, sems,
):
    yh, core = lax.axis_index("yh"), lax.axis_index("core")
    other = pl.ds(pl.multiple_of((1 - yh) * 768, 128), 768)
    last = (yh + core) // 2
    from_h = pl.ds(pl.multiple_of(last * (128 - EDGE_H), 16), EDGE_H)
    from_u = pl.ds(pl.multiple_of(last * (128 - EDGE_U), 16), EDGE_U)
    taken = begin(
        [
            (hidden.at[:, other], v_share.at[pl.ds(0, 128)]),
            (upstream.at[:, pl.ds(0, 768)], v_share.at[pl.ds(128, 128)]),
            (upstream.at[:, pl.ds(768, 768)], v_share.at[pl.ds(256, 128)]),
            (hidden.at[from_h], v_edge.at[pl.ds(0, EDGE_H)]),
            (upstream.at[from_u], v_edge.at[pl.ds(EDGE_H, EDGE_U)]),
        ],
        sems.at[pl.ds(9, 5)],
    )
    finish(begin([(weights, got), (durations, lengths)], sems))
    lane = lax.broadcasted_iota(jnp.int32, (1, 1536), 1)
    total = jnp.sum(lengths[...].astype(F32), axis=1, keepdims=True)
    note = jnp.where(lane == lax.axis_index("z"), jnp.broadcast_to(total, (1, 1536)), 0.0)
    rows = [got[...].astype(F32), note, jnp.zeros((1, 1536), F32)]
    block[...] = jnp.concatenate(rows, axis=0).astype(BF)
    sent = begin([(block, out.at[peer]) for peer in range(8)], sems)
    finish(taken)
    finish(begin([(v_share, share), (v_edge, edge)], sems.at[pl.ds(9, 2)]))
    finish(sent)


def lend(slot, out, v_out, sems):
    other = pl.ds(pl.multiple_of((1 - lax.axis_index("yh")) * 768, 128), 768)
    up = pl.ds(EDGE_H, EDGE_U)
    finish(
        begin(
            [
                (slot.at[pl.ds(0, EDGE_H), other], v_out.at[pl.ds(0, EDGE_H)]),
                (slot.at[up, pl.ds(0, 768)], v_out.at[pl.ds(EDGE_H, EDGE_U)]),
                (slot.at[up, pl.ds(768, 768)], v_out.at[pl.ds(EDGE_H + EDGE_U, EDGE_U)]),
            ],
            sems,
        )
    )
    finish(begin([(v_out, out)], sems))


def pack(gathered, plane, note_out, rows, got, block, v_note, sems):
    finish(begin([(gathered, got)], sems))
    note = jnp.zeros((8, EXTRA), F32)
    for z in range(8):
        block_z = got[z].astype(F32)
        for r in range(BLOCK):
            i = BLOCK * (z % 2) + r
            at = ROWS * (z // 2)
            if i < ROWS:
                rows[at + i : at + i + 1, :1536] = block_z[r : r + 1]
            else:
                for h in range(2):
                    to = at + 2 * (i - ROWS) + h
                    rows[to : to + 1, 1536:] = block_z[r : r + 1, 768 * h : 768 * h + 768]
        note += jnp.broadcast_to(block_z[BLOCK : BLOCK + 1, :EXTRA], (8, EXTRA))
    v_note[...] = note
    sent = begin([(v_note, note_out)], sems.at[pl.ds(32, 1)])
    for q in range(4):
        block[q] = rows[ROWS * q : ROWS * q + ROWS].astype(BF)
        members = [j for j in range(MEMBERS) if (j // 2) % 4 == q]
        sent += begin([(block.at[q], plane.at[j]) for j in members], sems.at[pl.ds(8 * q, 8)])
    finish(sent)


def relay(hidden, across, beside, v_beside, sems):
    yh, core = lax.axis_index("yh"), lax.axis_index("core")
    other = pl.ds(pl.multiple_of((yh * 2 + 1 - core) * CHANNELS, 128), CHANNELS)
    part = pl.ds(pl.multiple_of((1 - core) * CHANNELS, 128), CHANNELS)
    moves = [(hidden.at[:, other], v_beside.at[0]), (across.at[pl.ds(0, 128), part], v_beside.at[1])]
    finish(begin(moves, sems))
    finish(begin([(v_beside, beside)], sems))


def relay_edges(slot, lent, beside, v_beside, sems):
    yh, core = lax.axis_index("yh"), lax.axis_index("core")
    other = pl.ds(pl.multiple_of((yh * 2 + 1 - core) * CHANNELS, 128), CHANNELS)
    part = pl.ds(pl.multiple_of((1 - core) * CHANNELS, 128), CHANNELS)
    edge = pl.ds(0, EDGE_H)
    moves = [
        (slot.at[edge, other], v_beside.at[0, edge]),
        (lent.at[edge, part], v_beside.at[1, edge]),
    ]
    for i in range(4):
        cut = pl.ds((i % 2) * CHANNELS, CHANNELS)
        row = pl.ds(EDGE_H + EDGE_U * i, EDGE_U)
        wide = pl.ds(i * CHANNELS, CHANNELS)
        moves.append((slot.at[pl.ds(EDGE_H, EDGE_U), wide], v_beside.at[0, row]))
        moves.append((lent.at[pl.ds(EDGE_H + EDGE_U * (i // 2), EDGE_U), cut], v_beside.at[1, row]))
    finish(begin(moves, sems))
    finish(begin([(v_beside, beside)], sems))


def group_grads(upstream, across, beside, beyond, grads):
    yh, core = lax.axis_index("yh"), lax.axis_index("core")
    moves = [(upstream, grads.at[yh * 2 + core]), (beside, grads.at[yh * 2 + 1 - core])]
    for source, place in ((across, 2 - 2 * yh + core), (beyond, 3 - 2 * yh - core)):
        for i in range(2):
            rows, cut = pl.ds(128 + 128 * i, 128), pl.ds(768 * i, 768)
            moves.append((source.at[rows], grads.at[place, :, cut]))
    return moves


def convolve(
    own, slot, across, lent, beside, edges, upstream, up_beside, beyond, kernel, whole, low, high,
    slope, hidden, parts,
    grads, frames, weights, v_whole, v_low, v_high, v_slope, v_hidden, v_parts, active, sems,
):
    yh, core = lax.axis_index("yh"), lax.axis_index("core")
    part = pl.ds(pl.multiple_of(core * CHANNELS, 128), CHANNELS)
    mine = pl.ds(pl.multiple_of((yh * 2 + core) * CHANNELS, 128), CHANNELS)
    block, edge = pl.ds(0, 128), pl.ds(0, EDGE_H)
    needed = begin(
        [
            (own.at[:, mine], frames.at[yh * 2 + core, pl.ds(0, 128)]),
            (slot.at[pl.ds(0, EDGE_H), mine], frames.at[yh * 2 + core, pl.ds(128, EDGE_H)]),
            (across.at[pl.ds(0, 128), part], frames.at[(1 - yh) * 2 + core, pl.ds(0, 128)]),
            (lent.at[pl.ds(0, EDGE_H), part], frames.at[(1 - yh) * 2 + core, pl.ds(128, EDGE_H)]),
            (beside.at[0], frames.at[yh * 2 + 1 - core, block]),
            (beside.at[1], frames.at[(1 - yh) * 2 + 1 - core, block]),
            (edges.at[0, edge], frames.at[yh * 2 + 1 - core, pl.ds(128, EDGE_H)]),
            (edges.at[1, edge], frames.at[(1 - yh) * 2 + 1 - core, pl.ds(128, EDGE_H)]),
            (kernel, weights),
        ],
        sems,
    )
    later = begin(
        group_grads(upstream, across, up_beside, beyond, grads) + [(whole, v_whole), (low, v_low), (high, v_high)],
        sems.at[pl.ds(10, 9)],
    )
    finish(needed)
    v_hidden[:LEFT_H] = frames[0, 128 + EDGE_H - LEFT_H :].astype(F32)
    for b in range(4):
        v_hidden[LEFT_H + 128 * b : LEFT_H + 128 * b + 128] = frames[b, :128].astype(F32)
    v_hidden[LEFT_H + FRAMES :] = frames[3, 128:].astype(F32)
    rows = 112
    for tile in range(CHANNELS // 128):

        def chunk(c, _, tile=tile):
            base = pl.multiple_of(c * rows, 8)
            total = jnp.zeros((rows, 128), F32)
            window = v_hidden[pl.ds(base, rows + 32), lanes(tile)]
            for b in range(8):
                slab = window[b : b + rows + 24]
                for a in range(4):
                    k = 8 * a + b - 1
                    if 0 <= k < TAPS:
                        total += weights[k : k + 1, lanes(tile)] * slab[8 * a : 8 * a + rows]
            sig = jax.nn.sigmoid(total)
            v_slope[pl.ds(base, rows), lanes(tile)] = sig * (1.0 + total * (1.0 - sig))
            active[pl.ds(base, rows), lanes(tile)] = total * sig
            return 0

        lax.fori_loop(0, WIDE // rows, chunk, 0)
    out = begin([(v_slope, slope), (v_hidden, hidden)], sems)
    finish(later)
    acts = active[LEFT_U : LEFT_U + FRAMES].astype(BF)
    def outer(spot, cut):
        columns = jnp.dot(acts, spot[...], preferred_element_type=F32).astype(BF)
        return lax.dot_general(
            columns,
            grads[:, :, cut].reshape(FRAMES, -1),
            (((0,), (0,)), ((), ())),
            preferred_element_type=F32,
        )

    product = outer(v_whole, slice(0, 1536))
    halves = outer(v_low, slice(0, 768)) + outer(v_high, slice(768, 1536))
    for j in range(MEMBERS):
        v_parts[j, :, :1536] = product[ROWS * j : ROWS * j + ROWS].astype(BF)
        v_parts[j, :, 1536:] = halves[ROWS * j : ROWS * j + ROWS].astype(BF)
    finish(begin([(v_parts, parts.at[:, :, pl.ds(0, LANES)])], sems.at[pl.ds(2, 1)]))
    finish(out)


def backward(
    gathered, notes, whole, low, high, upstream, across, up_beside, beyond, slope, hidden, parts,
    grad_conv, projection, message,
    got, v_note, v_whole, v_low, v_high, grads, v_slope, v_hidden, v_grad, v_grad_f, v_taps, sums, v_weights, sems,
):
    needed = begin(
        [(gathered, got), (whole, v_whole), (low, v_low), (high, v_high), (notes, v_note)], sems
    )
    later = begin(
        group_grads(upstream, across, up_beside, beyond, grads), sems.at[pl.ds(5, 6)]
    )
    last = begin(
        [(slope.at[pl.ds(LEFT_U, FRAMES)], v_slope), (hidden, v_hidden)], sems.at[pl.ds(13, 2)]
    )
    finish(needed)
    rows = got[:, :, :1536].reshape(MESSAGE, 1536)
    halves = got[:, :, 1536:].reshape(MESSAGE, 768)
    for side, spot in enumerate((v_low, v_high)):
        cut = slice(768 * side, 768 * side + 768)
        value = jnp.dot(v_whole[...], rows[:, cut], preferred_element_type=F32)
        value += jnp.dot(spot[...], halves, preferred_element_type=F32)
        v_weights[:, cut] = value.astype(BF)
    finish(later)
    value = lax.dot_general(
        grads[...].reshape(FRAMES, 1536),
        v_weights[...],
        (((1,), (1,)), ((), ())),
        preferred_element_type=F32,
    )
    finish(last)
    value = (value * v_slope[...]).astype(BF)
    v_grad[...] = value
    v_grad_f[...] = value.astype(F32)
    out = begin([(v_grad, grad_conv), (v_weights, projection)], sems)
    span = 128
    sums[...] = jnp.zeros_like(sums)
    for tile in range(CHANNELS // 128):

        def piece(c, _, tile=tile):
            base = pl.multiple_of(c * span, 8)
            terms = v_grad_f[pl.ds(base, span), lanes(tile)]
            window = v_hidden[pl.ds(base + LEFT_U, span + 32), lanes(tile)]
            for b in range(8):
                slab = window[b : b + span + 24]
                for a in range(4):
                    k = 8 * a + b - 1
                    if 0 <= k < TAPS:
                        sums[k, :, lanes(tile)] += jnp.sum(
                            (terms * slab[8 * a : 8 * a + span]).reshape(span // 8, 8, 128),
                            axis=0,
                        )
            return 0

        lax.fori_loop(0, FRAMES // span, piece, 0, unroll=True)
    for j in range(MEMBERS):
        rows = [
            jnp.sum(sums[j, :, lanes(tile)], axis=0, keepdims=True)
            for tile in range(CHANNELS // 128)
        ]
        rows = jnp.concatenate(rows, axis=0)
        high_part = rows.astype(BF).astype(F32)
        rows = [high_part, rows - high_part, v_note[:1], jnp.zeros((ROWS - 7, 128), F32)]
        v_taps[j] = jnp.concatenate(rows, axis=0).astype(BF)
    finish(begin([(v_taps, message.at[:, :, pl.ds(LANES, EXTRA)])], sems.at[pl.ds(3, 1)]))
    finish(out)


def transposed(
    grad_conv, projection, slope, slot, lent, beside, kernel,
    kept, given, v_grad, v_weights, v_slope, ups, weights, wide, total_f, v_kept, v_given, sems,
):
    yh, core = lax.axis_index("yh"), lax.axis_index("core")
    edges = [(slot.at[pl.ds(EDGE_H, EDGE_U)], ups.at[yh * 2 + core])]
    for i in range(2):
        edges.append(
            (
                lent.at[pl.ds(EDGE_H + EDGE_U * i, EDGE_U)],
                ups.at[(1 - yh) * 2 + core, :, pl.ds(768 * i, 768)],
            )
        )
    for i in range(4):
        row, cut = pl.ds(EDGE_H + EDGE_U * i, EDGE_U), pl.ds(CHANNELS * i, CHANNELS)
        edges.append((beside.at[0, row], ups.at[yh * 2 + 1 - core, :, cut]))
        edges.append((beside.at[1, row], ups.at[(1 - yh) * 2 + 1 - core, :, cut]))
    edges += [
        (projection, v_weights),
        (slope.at[pl.ds(0, LEFT_U)], v_slope.at[pl.ds(0, LEFT_U)]),
        (slope.at[pl.ds(LEFT_U + FRAMES, EDGE_U)], v_slope.at[pl.ds(LEFT_U, EDGE_U)]),
        (grad_conv, v_grad),
        (kernel, weights),
    ]
    finish(begin(edges, sems))
    rows = jnp.concatenate([ups[0, EDGE_U - LEFT_U :], ups[3]], axis=0)
    value = lax.dot_general(
        rows, v_weights[...], (((1,), (1,)), ((), ())), preferred_element_type=F32
    )
    value = (value * v_slope[...]).astype(BF).astype(F32)
    wide[:LEFT_U] = value[:LEFT_U]
    wide[LEFT_U : LEFT_U + FRAMES] = v_grad[...].astype(F32)
    wide[LEFT_U + FRAMES :] = value[LEFT_U:]
    rows = 88
    for tile in range(CHANNELS // 128):

        def chunk(c, _, tile=tile):
            base = pl.multiple_of(c * rows, 8)
            total = jnp.zeros((rows, 128), F32)
            window = wide[pl.ds(base, rows + 32), lanes(tile)]
            for b in range(8):
                slab = window[b : b + rows + 24]
                for a in range(4):
                    k = TAPS - 8 * a - b
                    if 0 <= k < TAPS:
                        total += weights[k : k + 1, lanes(tile)] * slab[8 * a : 8 * a + rows]
            total_f[pl.ds(base, rows), lanes(tile)] = total
            return 0

        lax.fori_loop(0, LONG // rows, chunk, 0)
    for row in range(2):
        for out, side in ((v_kept, core), (v_given, 1 - core)):
            begin_row = pl.multiple_of((row * 2 + side) * 128, 128)
            out[row] = total_f[pl.ds(begin_row, BACK)].astype(BF)
    finish(begin([(v_kept, kept), (v_given, given)], sems))


def settle(
    kept, got, far, gathered, lengths, frame_grad, gloss, frames, notes, v_lengths, v_gloss, sems
):
    yh, core = lax.axis_index("yh"), lax.axis_index("core")
    sources = [(kept.at[yh], yh, core), (got.at[yh], yh, 1 - core)]
    sources += [(far.at[0], 1 - yh, core), (far.at[1], 1 - yh, 1 - core)]
    moves = [(lengths, v_lengths), (gathered.at[:, :, pl.ds(LANES, EXTRA)], notes)]
    for source, a, b in sources:
        cut = pl.ds(pl.multiple_of((a * 2 + b) * CHANNELS, 128), CHANNELS)
        moves.append((source, frames.at[:, cut]))
    finish(begin(moves, sems))
    out = begin([(frames.at[pl.ds(0, 128)], frame_grad)], sems)
    mine = yh * 2 + core
    place = lax.axis_index("z") * 4 + lax.axis_index("x")
    lane = lax.broadcasted_iota(jnp.int32, (8, EXTRA), 1)
    start = jnp.zeros((8, EXTRA), F32)
    for member in range(MEMBERS):
        block = lane * 16 + member // 2
        earlier = (block < place * 4 + mine) & (lane < 8) & (lax.axis_index("rep") == member % 2)
        start += jnp.where(earlier, notes[member, 6:7].astype(F32), 0.0)
    start = jnp.sum(start, axis=1, keepdims=True) - (place * FRAMES + mine * 128).astype(F32)
    gloss_id = lax.broadcasted_iota(jnp.int32, (8, EXTRA), 0)
    length = v_lengths[...]
    first = jnp.sum(jnp.where(lane < gloss_id, length, 0.0), axis=1, keepdims=True) + start
    last = first + jnp.sum(jnp.where(lane == gloss_id, length, 0.0), axis=1, keepdims=True)
    at = lax.broadcasted_iota(jnp.int32, (8, 128 + SPILL), 1).astype(F32)
    covers = jnp.where((at >= first) & (at < last), 1.0, 0.0).astype(BF)
    v_gloss[...] = jnp.dot(covers, frames[...], preferred_element_type=F32)
    finish(begin([(v_gloss, gloss)], sems.at[pl.ds(1, 1)]))
    finish(out)


def pack_z(parts, out, sems):
    sums = []
    for q in range(4):
        total = jnp.zeros((ROWS, LANES + EXTRA), F32)
        for x in range(4):
            for rep in range(2):
                total += parts[(x * 4 + q) * 2 + rep].astype(F32)
        sums.append(total)
    taps = [total[:3, LANES:] + total[3:6, LANES:] for total in sums]
    taps = jnp.concatenate([t[j : j + 1] for t in taps for j in range(3)], axis=1)
    high = taps.astype(BF).astype(F32)
    for z in range(8):
        total = sums[z // 2]
        rows = [total[:BLOCK, :1536]]
        if z % 2:
            rows = [total[BLOCK:, :1536]]
            for i in range(0, ROWS, 2):
                halves = [total[i + h : i + h + 1, 1536:LANES] for h in range(2)]
                rows.append(jnp.concatenate(halves, axis=1))
        rows += [high, taps - high]
        out[z] = jnp.concatenate(rows, axis=0).astype(BF)


def unpack_z(got, weights, taps, sems):
    total = got[0].astype(F32)
    for z in range(1, 8):
        total += got[z].astype(F32)
    total = total * (1.0 / math.sqrt(2 * 16384))
    weights[...] = total[:BLOCK]
    for peer in range(MEMBERS):
        taps[peer] = total[6:7] + total[7:8]


def arrange(got, out, v_out, sems):
    for k in range(TAPS):
        v_out[k : k + 1] = got[k]
    finish(begin([(v_out, out)], sems))


def call(
    kernel, outs, scratch, megabytes, *args, alias=None, flops=200_000_000, near=(), near_out=()
):
    def space(vmem):
        return pl.BlockSpec(memory_space=pltpu.VMEM if vmem else pltpu.HBM)

    shapes = [jax.ShapeDtypeStruct(shape, dtype) for shape, dtype in outs]
    size = sum(math.prod(s.shape) * s.dtype.itemsize for s in list(args) + shapes)
    return pl.pallas_call(
        kernel,
        out_shape=shapes,
        in_specs=[space(i in near) for i in range(len(args))],
        out_specs=[space(i in near_out) for i in range(len(shapes))],
        scratch_shapes=[pltpu.VMEM(shape, dtype) for shape, dtype in scratch]
        + [pltpu.SemaphoreType.DMA((48,))],
        input_output_aliases=alias or {},
        compiler_params=pltpu.CompilerParams(vmem_limit_bytes=megabytes * 2**20),
        cost_estimate=pl.CostEstimate(
            flops=flops, bytes_accessed=size, transcendentals=0
        ),
    )(*args)


def body(hidden_in, upstream, out_weight, conv_kernel, durations):
    yh, core = lax.axis_index("yh"), lax.axis_index("core")
    quarter = yh * 2 + core
    hidden, grads = hidden_in[0], upstream[0]
    lengths = jnp.broadcast_to(
        jnp.pad(durations.astype(F32), ((0, 0), (0, EXTRA - durations.shape[1]))), (8, EXTRA)
    )

    rows, share, edge = call(
        spread,
        [((8, 8, 1536), BF), ((384, 768), BF), ((EDGE_H + EDGE_U, 1536), BF)],
        [
            ((BLOCK, 1536), BF), ((1, 8), jnp.int32), ((8, 1536), BF), ((384, 768), BF),
            ((EDGE_H + EDGE_U, 1536), BF),
        ],
        56,
        out_weight, durations, hidden, grads,
    )
    ends = [(4 * i + 3, 4 * i + 4) for i in range(31)]
    slot = lax.ppermute(edge, ("z", "x", "yh", "core"), ends + [(b, a) for a, b in ends])
    rows = lax.all_to_all(rows, "z", 0, 0, tiled=True)
    across = lax.ppermute(share, "yh", SWAP)
    up_beside = lax.ppermute(grads, "core", SWAP)
    beyond = lax.ppermute(across, "core", SWAP)
    [lent] = call(lend, [((SHARE, 768), BF)], [((SHARE, 768), BF)], 16, slot)
    lent = lax.ppermute(lent, GROUP, [(0, 2), (3, 1)])
    message = ((MEMBERS, ROWS, LANES + EXTRA), BF)
    note = ((8, EXTRA), F32)
    plane, notes = call(
        pack,
        [((MEMBERS, ROWS, LANES), BF), note],
        [((4 * ROWS, LANES), F32), ((8, 8, 1536), BF), ((4, ROWS, LANES), BF), note],
        56,
        rows,
    )
    handed = ((2, 128, CHANNELS), BF)
    [beside] = call(relay, [handed], [handed], 16, hidden, across, flops=3_000_000_000)
    handed = ((2, HANDED, CHANNELS), BF)
    [edges] = call(relay_edges, [handed], [handed], 16, slot, lent, flops=30_000_000_000)
    rows = lax.all_to_all(plane, PLANE, 0, 0, tiled=True)
    beside = lax.ppermute(beside, "core", SWAP)
    edges = lax.ppermute(edges, "core", SWAP)
    kernel_f = lax.dynamic_slice_in_dim(
        jnp.pad(conv_kernel, ((0, 1), (0, 0))), quarter * CHANNELS, CHANNELS, 1
    ).astype(F32)
    spot = ((CHANNELS, MESSAGE), BF)
    spots = [placement(part) for part in range(3)]
    frames_f = ((FRAMES, CHANNELS), F32)
    wide_f = ((LEFT_H + FRAMES + EDGE_H, CHANNELS), F32)
    slope_f = ((WIDE, CHANNELS), F32)
    all_grads = ((4, 128, 1536), BF)
    sent = ((MEMBERS, ROWS, LANES), BF)
    kernel_shape = ((TAPS + 1, CHANNELS), F32)
    slope, hidden_f, parts = call(
        convolve,
        [slope_f, wide_f, message],
        [
            all_grads, ((4, 128 + EDGE_H, CHANNELS), BF), kernel_shape, spot, spot, spot, slope_f, wide_f,
            sent, slope_f,
        ],
        56,
        hidden, slot, across, lent, beside, edges, grads, up_beside, beyond, kernel_f, *spots,
    )
    grad_conv, projection, parts = call(
        backward,
        [
            ((FRAMES, CHANNELS), BF), ((CHANNELS, 1536), BF), message,
        ],
        [
            sent, note, spot, spot, spot, all_grads, frames_f, wide_f, ((FRAMES, CHANNELS), BF), frames_f,
            ((MEMBERS, ROWS, EXTRA), BF), ((TAPS + 1, 8, CHANNELS), F32),
            ((CHANNELS, 1536), BF),
        ],
        56,
        rows, notes, *spots, grads, across, up_beside, beyond, slope, hidden_f, parts,
        alias={11: 2},
    )

    summed = parts = lax.all_to_all(parts, PLANE, 0, 0, tiled=True)
    [parts] = call(
        pack_z,
        [((8, 8, 1536), BF)],
        [],
        16,
        parts,
        near=(0,),
        near_out=(0,),
    )
    parts = lax.all_to_all(parts, "z", 0, 0, tiled=True)
    weight_grad, taps_all = call(
        unpack_z,
        [((BLOCK, 1536), F32), ((32, 1, 1536), F32)],
        [],
        16,
        parts,
        near=(0,),
        near_out=(0, 1),
    )
    taps_all = lax.all_to_all(taps_all, PLANE, 0, 0, tiled=True)
    [kernel_grad] = call(
        arrange,
        [((TAPS, 1536), F32)],
        [((TAPS, 1536), F32)],
        16,
        taps_all,
        near=(0,),
    )

    back = ((2, BACK, CHANNELS), BF)
    kept, given = call(
        transposed,
        [back, back],
        [
            ((FRAMES, CHANNELS), BF), ((CHANNELS, 1536), BF), ((LEFT_U + EDGE_U, CHANNELS), F32),
            ((4, EDGE_U, 1536), BF), kernel_shape,
            slope_f, ((LONG, CHANNELS), F32), back, back,
        ],
        56,
        grad_conv, projection, slope, slot, lent, edges, kernel_f,
    )
    got = lax.ppermute(given, "core", SWAP)
    far = jnp.stack(
        [lax.dynamic_index_in_dim(part, 1 - yh, 0, False) for part in (kept, got)]
    )
    far = lax.ppermute(far, "yh", SWAP)
    frame_grad, gloss = call(
        settle,
        [((128, 1536), BF), ((8, 1536), F32)],
        [
            ((BACK, 1536), BF), ((MEMBERS, ROWS, EXTRA), BF), ((8, EXTRA), F32),
            ((8, 1536), F32),
        ],
        16,
        kept, got, far, summed, lengths,
    )
    return (frame_grad[None], gloss[None], weight_grad, kernel_grad)


def solution(mesh):
    fine = Mesh(mesh.devices.reshape(SIZES), AXES)
    seq = ("z", "x", "yh", "core")
    rows = P(seq + ("rep",), None)
    in_specs = (P("rep", seq, None), P("rep", seq, None), rows, P(), P("rep", seq))
    out_specs = (P("rep", seq, None), P("rep", seq, None), rows, P())
    return jax.shard_map(
        body, mesh=fine, in_specs=in_specs, out_specs=out_specs, check_vma=False
    )
```

```python
import math

import jax
import jax.numpy as jnp
import numpy as np
from jax import lax
from jax.experimental import pallas as pl
from jax.experimental.pallas import tpu as pltpu
from jax.sharding import Mesh
from jax.sharding import PartitionSpec as P

AXES = ("z", "x", "yh", "core", "rep")
SIZES = (8, 4, 2, 2, 2)
GROUP = ("yh", "core")
PLANE = ("x", "yh", "core", "rep")
QUARTERS = 4
BLOCK = 6
EXTRA = 128
MEMBERS, ROWS, LANES = 32, 8, 2304
MESSAGE = MEMBERS * ROWS
FRAMES, CHANNELS, TAPS = 512, 384, 31
EDGE_H, EDGE_U, SPILL = 48, 32, 16
LEFT_H, LEFT_U = 32, 16
WIDE = FRAMES + LEFT_U + EDGE_U
LONG = FRAMES + SPILL
SHARE = EDGE_H + 2 * EDGE_U
HANDED = EDGE_H + 4 * EDGE_U
BACK = 128 + SPILL
SWAP = [(0, 1), (1, 0)]
BF = jnp.bfloat16
F32 = jnp.float32


def placement(part):
    out = np.zeros((CHANNELS, MESSAGE), np.float32)
    for zl in range(2):
        for member in range(MEMBERS):
            for r in range(BLOCK):
                row, i = (zl * MEMBERS + member) * BLOCK + r, zl * BLOCK + r
                if part == 0 and i < ROWS:
                    out[row, member * ROWS + i] = 1
                if part > 0 and i >= ROWS:
                    out[row, member * ROWS + 2 * (i - ROWS) + part - 1] = 1
    return jnp.asarray(out, BF)


def lanes(tile):
    return slice(tile * 128, tile * 128 + 128)


def begin(pairs, sems):
    copies = [pltpu.make_async_copy(a, b, sems.at[i]) for i, (a, b) in enumerate(pairs)]
    for copy in copies:
        copy.start()
    return copies


def finish(copies):
    for copy in copies:
        copy.wait()


def spread(
    weights, durations, hidden, upstream, out, share, edge,
    got, lengths, block, v_share, v_edge, sems,
):
    yh, core = lax.axis_index("yh"), lax.axis_index("core")
    other = pl.ds(pl.multiple_of((1 - yh) * 768, 128), 768)
    last = (yh + core) // 2
    from_h = pl.ds(pl.multiple_of(last * (128 - EDGE_H), 16), EDGE_H)
    from_u = pl.ds(pl.multiple_of(last * (128 - EDGE_U), 16), EDGE_U)
    taken = begin(
        [
            (hidden.at[:, other], v_share.at[pl.ds(0, 128)]),
            (upstream.at[:, pl.ds(0, 768)], v_share.at[pl.ds(128, 128)]),
            (upstream.at[:, pl.ds(768, 768)], v_share.at[pl.ds(256, 128)]),
            (hidden.at[from_h], v_edge.at[pl.ds(0, EDGE_H)]),
            (upstream.at[from_u], v_edge.at[pl.ds(EDGE_H, EDGE_U)]),
        ],
        sems.at[pl.ds(9, 5)],
    )
    finish(begin([(weights, got), (durations, lengths)], sems))
    lane = lax.broadcasted_iota(jnp.int32, (8, EXTRA), 1)
    total = jnp.sum(lengths[...].astype(F32), axis=1, keepdims=True)
    note = jnp.where(lane == lax.axis_index("z"), jnp.broadcast_to(total, (8, EXTRA)), 0.0)
    rows = got[...].astype(F32)
    rest = [
        jnp.concatenate([rows[3 * i + j : 3 * i + j + 1, 1152:] for j in range(3)], axis=1)
        for i in range(2)
    ]
    rows = jnp.concatenate([rows[:, :1152]] + rest, axis=0)
    block[...] = jnp.concatenate([rows, note], axis=1).astype(BF)
    sent = begin([(block, out.at[peer]) for peer in range(8)], sems)
    finish(taken)
    finish(begin([(v_share, share), (v_edge, edge)], sems.at[pl.ds(9, 2)]))
    finish(sent)


def lend(slot, out, v_out, sems):
    other = pl.ds(pl.multiple_of((1 - lax.axis_index("yh")) * 768, 128), 768)
    up = pl.ds(EDGE_H, EDGE_U)
    finish(
        begin(
            [
                (slot.at[pl.ds(0, EDGE_H), other], v_out.at[pl.ds(0, EDGE_H)]),
                (slot.at[up, pl.ds(0, 768)], v_out.at[pl.ds(EDGE_H, EDGE_U)]),
                (slot.at[up, pl.ds(768, 768)], v_out.at[pl.ds(EDGE_H + EDGE_U, EDGE_U)]),
            ],
            sems,
        )
    )
    finish(begin([(v_out, out)], sems))


def pack(gathered, plane, note_out, rows, got, block, v_note, sems):
    finish(begin([(gathered, got)], sems))
    note = jnp.zeros((8, EXTRA), F32)
    for z in range(8):
        block_z = got[z].astype(F32)
        rest = [block_z[6 + r // 3, 384 * (r % 3) : 384 * (r % 3) + 384] for r in range(BLOCK)]
        block_z, spare = (
            jnp.concatenate([block_z[:BLOCK, :1152], jnp.stack(rest)], axis=1),
            block_z[:, 1152:],
        )
        for r in range(BLOCK):
            i = BLOCK * (z % 2) + r
            at = ROWS * (z // 2)
            if i < ROWS:
                rows[at + i : at + i + 1, :1536] = block_z[r : r + 1]
            else:
                for h in range(2):
                    to = at + 2 * (i - ROWS) + h
                    rows[to : to + 1, 1536:] = block_z[r : r + 1, 768 * h : 768 * h + 768]
        note += spare
    v_note[...] = note
    sent = begin([(v_note, note_out)], sems.at[pl.ds(32, 1)])
    for q in range(4):
        block[q] = rows[ROWS * q : ROWS * q + ROWS].astype(BF)
        members = [j for j in range(MEMBERS) if (j // 2) % 4 == q]
        sent += begin([(block.at[q], plane.at[j]) for j in members], sems.at[pl.ds(8 * q, 8)])
    finish(sent)


def relay(hidden, across, beside, v_beside, sems):
    yh, core = lax.axis_index("yh"), lax.axis_index("core")
    other = pl.ds(pl.multiple_of((yh * 2 + 1 - core) * CHANNELS, 128), CHANNELS)
    part = pl.ds(pl.multiple_of((1 - core) * CHANNELS, 128), CHANNELS)
    moves = [(hidden.at[:, other], v_beside.at[0]), (across.at[pl.ds(0, 128), part], v_beside.at[1])]
    finish(begin(moves, sems))
    finish(begin([(v_beside, beside)], sems))


def relay_edges(slot, lent, beside, v_beside, sems):
    yh, core = lax.axis_index("yh"), lax.axis_index("core")
    other = pl.ds(pl.multiple_of((yh * 2 + 1 - core) * CHANNELS, 128), CHANNELS)
    part = pl.ds(pl.multiple_of((1 - core) * CHANNELS, 128), CHANNELS)
    edge = pl.ds(0, EDGE_H)
    moves = [
        (slot.at[edge, other], v_beside.at[0, edge]),
        (lent.at[edge, part], v_beside.at[1, edge]),
    ]
    for i in range(4):
        cut = pl.ds((i % 2) * CHANNELS, CHANNELS)
        row = pl.ds(EDGE_H + EDGE_U * i, EDGE_U)
        wide = pl.ds(i * CHANNELS, CHANNELS)
        moves.append((slot.at[pl.ds(EDGE_H, EDGE_U), wide], v_beside.at[0, row]))
        moves.append((lent.at[pl.ds(EDGE_H + EDGE_U * (i // 2), EDGE_U), cut], v_beside.at[1, row]))
    finish(begin(moves, sems))
    finish(begin([(v_beside, beside)], sems))


def group_grads(upstream, across, beside, beyond, grads):
    yh, core = lax.axis_index("yh"), lax.axis_index("core")
    moves = [(upstream, grads.at[yh * 2 + core]), (beside, grads.at[yh * 2 + 1 - core])]
    for source, place in ((across, 2 - 2 * yh + core), (beyond, 3 - 2 * yh - core)):
        for i in range(2):
            rows, cut = pl.ds(128 + 128 * i, 128), pl.ds(768 * i, 768)
            moves.append((source.at[rows], grads.at[place, :, cut]))
    return moves


def convolve(
    own, slot, across, lent, beside, edges, upstream, up_beside, beyond, kernel, whole, low, high,
    slope, hidden, parts,
    grads, frames, weights, v_whole, v_low, v_high, v_slope, v_hidden, v_parts, active, sems,
):
    yh, core = lax.axis_index("yh"), lax.axis_index("core")
    part = pl.ds(pl.multiple_of(core * CHANNELS, 128), CHANNELS)
    mine = pl.ds(pl.multiple_of((yh * 2 + core) * CHANNELS, 128), CHANNELS)
    block, edge = pl.ds(0, 128), pl.ds(0, EDGE_H)
    needed = begin(
        [
            (own.at[:, mine], frames.at[yh * 2 + core, pl.ds(0, 128)]),
            (slot.at[pl.ds(0, EDGE_H), mine], frames.at[yh * 2 + core, pl.ds(128, EDGE_H)]),
            (across.at[pl.ds(0, 128), part], frames.at[(1 - yh) * 2 + core, pl.ds(0, 128)]),
            (lent.at[pl.ds(0, EDGE_H), part], frames.at[(1 - yh) * 2 + core, pl.ds(128, EDGE_H)]),
            (beside.at[0], frames.at[yh * 2 + 1 - core, block]),
            (beside.at[1], frames.at[(1 - yh) * 2 + 1 - core, block]),
            (edges.at[0, edge], frames.at[yh * 2 + 1 - core, pl.ds(128, EDGE_H)]),
            (edges.at[1, edge], frames.at[(1 - yh) * 2 + 1 - core, pl.ds(128, EDGE_H)]),
            (kernel, weights),
        ],
        sems,
    )
    later = begin(
        group_grads(upstream, across, up_beside, beyond, grads) + [(whole, v_whole), (low, v_low), (high, v_high)],
        sems.at[pl.ds(10, 9)],
    )
    finish(needed)
    v_hidden[:LEFT_H] = frames[0, 128 + EDGE_H - LEFT_H :].astype(F32)
    for b in range(4):
        v_hidden[LEFT_H + 128 * b : LEFT_H + 128 * b + 128] = frames[b, :128].astype(F32)
    v_hidden[LEFT_H + FRAMES :] = frames[3, 128:].astype(F32)
    rows = 112
    for tile in range(CHANNELS // 128):

        def chunk(c, _, tile=tile):
            base = pl.multiple_of(c * rows, 8)
            total = jnp.zeros((rows, 128), F32)
            window = v_hidden[pl.ds(base, rows + 32), lanes(tile)]
            for b in range(8):
                slab = window[b : b + rows + 24]
                for a in range(4):
                    k = 8 * a + b - 1
                    if 0 <= k < TAPS:
                        total += weights[k : k + 1, lanes(tile)] * slab[8 * a : 8 * a + rows]
            sig = jax.nn.sigmoid(total)
            v_slope[pl.ds(base, rows), lanes(tile)] = sig * (1.0 + total * (1.0 - sig))
            active[pl.ds(base, rows), lanes(tile)] = total * sig
            return 0

        lax.fori_loop(0, WIDE // rows, chunk, 0, unroll=True)
    out = begin([(v_slope, slope), (v_hidden, hidden)], sems)
    finish(later)
    acts = active[LEFT_U : LEFT_U + FRAMES].astype(BF)
    def outer(spot, cut):
        columns = jnp.dot(acts, spot[...], preferred_element_type=F32).astype(BF)
        return lax.dot_general(
            columns,
            grads[:, :, cut].reshape(FRAMES, -1),
            (((0,), (0,)), ((), ())),
            preferred_element_type=F32,
        )

    product = outer(v_whole, slice(0, 1536))
    for j in range(MEMBERS):
        v_parts[j, :, :1536] = product[ROWS * j : ROWS * j + ROWS].astype(BF)
    cut = pl.ds(0, 1536)
    out += begin([(v_parts.at[:, :, cut], parts.at[:, :, cut])], sems.at[pl.ds(2, 1)])
    halves = outer(v_low, slice(0, 768)) + outer(v_high, slice(768, 1536))
    for j in range(MEMBERS):
        v_parts[j, :, 1536:] = halves[ROWS * j : ROWS * j + ROWS].astype(BF)
    cut = pl.ds(1536, LANES - 1536)
    out += begin([(v_parts.at[:, :, cut], parts.at[:, :, cut])], sems.at[pl.ds(3, 1)])
    finish(out)


def backward(
    gathered, notes, whole, low, high, upstream, across, up_beside, beyond, slope, hidden, parts,
    grad_conv, projection, message,
    got, v_note, v_whole, v_low, v_high, grads, v_slope, v_hidden, v_grad, v_grad_f, v_taps, sums, v_weights, sems,
):
    needed = begin(
        [(gathered, got), (whole, v_whole), (low, v_low), (high, v_high), (notes, v_note)], sems
    )
    later = begin(
        group_grads(upstream, across, up_beside, beyond, grads), sems.at[pl.ds(5, 6)]
    )
    last = begin(
        [(slope.at[pl.ds(LEFT_U, FRAMES)], v_slope), (hidden, v_hidden)], sems.at[pl.ds(13, 2)]
    )
    finish(needed)
    rows = got[:, :, :1536].reshape(MESSAGE, 1536)
    halves = got[:, :, 1536:].reshape(MESSAGE, 768)
    for side, spot in enumerate((v_low, v_high)):
        cut = slice(768 * side, 768 * side + 768)
        value = jnp.dot(v_whole[...], rows[:, cut], preferred_element_type=F32)
        value += jnp.dot(spot[...], halves, preferred_element_type=F32)
        v_weights[:, cut] = value.astype(BF)
    finish(later)
    value = lax.dot_general(
        grads[...].reshape(FRAMES, 1536),
        v_weights[...],
        (((1,), (1,)), ((), ())),
        preferred_element_type=F32,
    )
    finish(last)
    value = (value * v_slope[...]).astype(BF)
    v_grad[...] = value
    v_grad_f[...] = value.astype(F32)
    out = begin([(v_grad, grad_conv), (v_weights, projection)], sems)
    span = 128
    sums[...] = jnp.zeros_like(sums)
    for tile in range(CHANNELS // 128):

        def piece(c, _, tile=tile):
            base = pl.multiple_of(c * span, 8)
            terms = v_grad_f[pl.ds(base, span), lanes(tile)]
            window = v_hidden[pl.ds(base + LEFT_U, span + 32), lanes(tile)]
            for b in range(8):
                slab = window[b : b + span + 24]
                for a in range(4):
                    k = 8 * a + b - 1
                    if 0 <= k < TAPS:
                        sums[k, :, lanes(tile)] += jnp.sum(
                            (terms * slab[8 * a : 8 * a + span]).reshape(span // 8, 8, 128),
                            axis=0,
                        )
            return 0

        lax.fori_loop(0, FRAMES // span, piece, 0, unroll=True)
    for j in range(MEMBERS):
        rows = [
            jnp.sum(sums[j, :, lanes(tile)], axis=0, keepdims=True)
            for tile in range(CHANNELS // 128)
        ]
        rows = jnp.concatenate(rows, axis=0)
        high_part = rows.astype(BF).astype(F32)
        rows = [high_part, rows - high_part, v_note[:1], jnp.zeros((ROWS - 7, 128), F32)]
        v_taps[j] = jnp.concatenate(rows, axis=0).astype(BF)
    finish(begin([(v_taps, message.at[:, :, pl.ds(LANES, EXTRA)])], sems.at[pl.ds(3, 1)]))
    finish(out)


def transposed(
    grad_conv, projection, slope, slot, lent, beside, kernel,
    kept, given, v_grad, v_weights, v_slope, ups, weights, wide, total_f, v_kept, v_given, sems,
):
    yh, core = lax.axis_index("yh"), lax.axis_index("core")
    edges = [(slot.at[pl.ds(EDGE_H, EDGE_U)], ups.at[yh * 2 + core])]
    for i in range(2):
        edges.append(
            (
                lent.at[pl.ds(EDGE_H + EDGE_U * i, EDGE_U)],
                ups.at[(1 - yh) * 2 + core, :, pl.ds(768 * i, 768)],
            )
        )
    for i in range(4):
        row, cut = pl.ds(EDGE_H + EDGE_U * i, EDGE_U), pl.ds(CHANNELS * i, CHANNELS)
        edges.append((beside.at[0, row], ups.at[yh * 2 + 1 - core, :, cut]))
        edges.append((beside.at[1, row], ups.at[(1 - yh) * 2 + 1 - core, :, cut]))
    edges += [
        (projection, v_weights),
        (slope.at[pl.ds(0, LEFT_U)], v_slope.at[pl.ds(0, LEFT_U)]),
        (slope.at[pl.ds(LEFT_U + FRAMES, EDGE_U)], v_slope.at[pl.ds(LEFT_U, EDGE_U)]),
        (grad_conv, v_grad),
        (kernel, weights),
    ]
    finish(begin(edges, sems))
    rows = jnp.concatenate([ups[0, EDGE_U - LEFT_U :], ups[3]], axis=0)
    value = lax.dot_general(
        rows, v_weights[...], (((1,), (1,)), ((), ())), preferred_element_type=F32
    )
    value = (value * v_slope[...]).astype(BF).astype(F32)
    wide[:LEFT_U] = value[:LEFT_U]
    wide[LEFT_U : LEFT_U + FRAMES] = v_grad[...].astype(F32)
    wide[LEFT_U + FRAMES :] = value[LEFT_U:]
    rows = 88
    for tile in range(CHANNELS // 128):

        def chunk(c, _, tile=tile):
            base = pl.multiple_of(c * rows, 8)
            total = jnp.zeros((rows, 128), F32)
            window = wide[pl.ds(base, rows + 32), lanes(tile)]
            for b in range(8):
                slab = window[b : b + rows + 24]
                for a in range(4):
                    k = TAPS - 8 * a - b
                    if 0 <= k < TAPS:
                        total += weights[k : k + 1, lanes(tile)] * slab[8 * a : 8 * a + rows]
            total_f[pl.ds(base, rows), lanes(tile)] = total
            return 0

        lax.fori_loop(0, LONG // rows, chunk, 0)
    for row in range(2):
        for out, side in ((v_kept, core), (v_given, 1 - core)):
            begin_row = pl.multiple_of((row * 2 + side) * 128, 128)
            out[row] = total_f[pl.ds(begin_row, BACK)].astype(BF)
    finish(begin([(v_kept, kept), (v_given, given)], sems))


def settle(
    kept, got, far, gathered, lengths, frame_grad, gloss, frames, notes, v_lengths, v_gloss, sems
):
    yh, core = lax.axis_index("yh"), lax.axis_index("core")
    sources = [(kept.at[yh], yh, core), (got.at[yh], yh, 1 - core)]
    sources += [(far.at[0], 1 - yh, core), (far.at[1], 1 - yh, 1 - core)]
    moves = [(lengths, v_lengths), (gathered.at[:, :, pl.ds(LANES, EXTRA)], notes)]
    for source, a, b in sources:
        cut = pl.ds(pl.multiple_of((a * 2 + b) * CHANNELS, 128), CHANNELS)
        moves.append((source, frames.at[:, cut]))
    finish(begin(moves, sems))
    out = begin([(frames.at[pl.ds(0, 128)], frame_grad)], sems)
    mine = yh * 2 + core
    place = lax.axis_index("z") * 4 + lax.axis_index("x")
    lane = lax.broadcasted_iota(jnp.int32, (8, EXTRA), 1)
    start = jnp.zeros((8, EXTRA), F32)
    for member in range(MEMBERS):
        block = lane * 16 + member // 2
        earlier = (block < place * 4 + mine) & (lane < 8) & (lax.axis_index("rep") == member % 2)
        start += jnp.where(earlier, notes[member, 6:7].astype(F32), 0.0)
    start = jnp.sum(start, axis=1, keepdims=True) - (place * FRAMES + mine * 128).astype(F32)
    gloss_id = lax.broadcasted_iota(jnp.int32, (8, EXTRA), 0)
    length = v_lengths[...]
    first = jnp.sum(jnp.where(lane < gloss_id, length, 0.0), axis=1, keepdims=True) + start
    last = first + jnp.sum(jnp.where(lane == gloss_id, length, 0.0), axis=1, keepdims=True)
    at = lax.broadcasted_iota(jnp.int32, (8, 128 + SPILL), 1).astype(F32)
    covers = jnp.where((at >= first) & (at < last), 1.0, 0.0).astype(BF)
    v_gloss[...] = jnp.dot(covers, frames[...], preferred_element_type=F32)
    finish(begin([(v_gloss, gloss)], sems.at[pl.ds(1, 1)]))
    finish(out)


def pack_z(parts, out, sems):
    sums = []
    for q in range(4):
        total = jnp.zeros((ROWS, LANES + EXTRA), F32)
        for x in range(4):
            for rep in range(2):
                total += parts[(x * 4 + q) * 2 + rep].astype(F32)
        sums.append(total)
    taps = [total[:3, LANES:] + total[3:6, LANES:] for total in sums]
    taps = jnp.concatenate([t[j : j + 1] for t in taps for j in range(3)], axis=1)
    high = taps.astype(BF).astype(F32)
    for z in range(8):
        total = sums[z // 2]
        rows = [total[:BLOCK, :1536]]
        if z % 2:
            rows = [total[BLOCK:, :1536]]
            for i in range(0, ROWS, 2):
                halves = [total[i + h : i + h + 1, 1536:LANES] for h in range(2)]
                rows.append(jnp.concatenate(halves, axis=1))
        rows += [high, taps - high]
        out[z] = jnp.concatenate(rows, axis=0).astype(BF)


def unpack_z(got, weights, taps, sems):
    total = got[0].astype(F32)
    for z in range(1, 8):
        total += got[z].astype(F32)
    total = total * (1.0 / math.sqrt(2 * 16384))
    weights[...] = total[:BLOCK]
    for peer in range(MEMBERS):
        taps[peer] = total[6:7] + total[7:8]


def arrange(got, out, v_out, sems):
    for k in range(TAPS):
        v_out[k : k + 1] = got[k]
    finish(begin([(v_out, out)], sems))


def call(
    kernel, outs, scratch, megabytes, *args, alias=None, flops=200_000_000, near=(), near_out=()
):
    def space(vmem):
        return pl.BlockSpec(memory_space=pltpu.VMEM if vmem else pltpu.HBM)

    shapes = [jax.ShapeDtypeStruct(shape, dtype) for shape, dtype in outs]
    size = sum(math.prod(s.shape) * s.dtype.itemsize for s in list(args) + shapes)
    return pl.pallas_call(
        kernel,
        out_shape=shapes,
        in_specs=[space(i in near) for i in range(len(args))],
        out_specs=[space(i in near_out) for i in range(len(shapes))],
        scratch_shapes=[pltpu.VMEM(shape, dtype) for shape, dtype in scratch]
        + [pltpu.SemaphoreType.DMA((48,))],
        input_output_aliases=alias or {},
        compiler_params=pltpu.CompilerParams(vmem_limit_bytes=megabytes * 2**20),
        cost_estimate=pl.CostEstimate(
            flops=flops, bytes_accessed=size, transcendentals=0
        ),
    )(*args)


def body(hidden_in, upstream, out_weight, conv_kernel, durations):
    yh, core = lax.axis_index("yh"), lax.axis_index("core")
    quarter = yh * 2 + core
    hidden, grads = hidden_in[0], upstream[0]
    lengths = jnp.broadcast_to(
        jnp.pad(durations.astype(F32), ((0, 0), (0, EXTRA - durations.shape[1]))), (8, EXTRA)
    )

    rows, share, edge = call(
        spread,
        [((8, 8, 1280), BF), ((384, 768), BF), ((EDGE_H + EDGE_U, 1536), BF)],
        [
            ((BLOCK, 1536), BF), ((1, 8), jnp.int32), ((8, 1280), BF), ((384, 768), BF),
            ((EDGE_H + EDGE_U, 1536), BF),
        ],
        56,
        out_weight, durations, hidden, grads,
    )
    ends = [(4 * i + 3, 4 * i + 4) for i in range(31)]
    slot = lax.ppermute(edge, ("z", "x", "yh", "core"), ends + [(b, a) for a, b in ends])
    rows = lax.all_to_all(rows, "z", 0, 0, tiled=True)
    across = lax.ppermute(share, "yh", SWAP)
    up_beside = lax.ppermute(grads, "core", SWAP)
    beyond = lax.ppermute(across, "core", SWAP)
    [lent] = call(lend, [((SHARE, 768), BF)], [((SHARE, 768), BF)], 16, slot)
    lent = lax.ppermute(lent, GROUP, [(0, 2), (3, 1)])
    message = ((MEMBERS, ROWS, LANES + EXTRA), BF)
    note = ((8, EXTRA), F32)
    plane, notes = call(
        pack,
        [((MEMBERS, ROWS, LANES), BF), note],
        [((4 * ROWS, LANES), F32), ((8, 8, 1280), BF), ((4, ROWS, LANES), BF), note],
        56,
        rows,
    )
    handed = ((2, 128, CHANNELS), BF)
    [beside] = call(relay, [handed], [handed], 16, hidden, across, flops=3_000_000_000)
    handed = ((2, HANDED, CHANNELS), BF)
    [edges] = call(relay_edges, [handed], [handed], 16, slot, lent, flops=30_000_000_000)
    rows = lax.all_to_all(plane, PLANE, 0, 0, tiled=True)
    beside = lax.ppermute(beside, "core", SWAP)
    edges = lax.ppermute(edges, "core", SWAP)
    kernel_f = lax.dynamic_slice_in_dim(
        jnp.pad(conv_kernel, ((0, 1), (0, 0))), quarter * CHANNELS, CHANNELS, 1
    ).astype(F32)
    spot = ((CHANNELS, MESSAGE), BF)
    spots = [placement(part) for part in range(3)]
    frames_f = ((FRAMES, CHANNELS), F32)
    wide_f = ((LEFT_H + FRAMES + EDGE_H, CHANNELS), F32)
    slope_f = ((WIDE, CHANNELS), F32)
    all_grads = ((4, 128, 1536), BF)
    sent = ((MEMBERS, ROWS, LANES), BF)
    kernel_shape = ((TAPS + 1, CHANNELS), F32)
    slope, hidden_f, parts = call(
        convolve,
        [slope_f, wide_f, message],
        [
            all_grads, ((4, 128 + EDGE_H, CHANNELS), BF), kernel_shape, spot, spot, spot, slope_f, wide_f,
            sent, slope_f,
        ],
        56,
        hidden, slot, across, lent, beside, edges, grads, up_beside, beyond, kernel_f, *spots,
    )
    grad_conv, projection, parts = call(
        backward,
        [
            ((FRAMES, CHANNELS), BF), ((CHANNELS, 1536), BF), message,
        ],
        [
            sent, note, spot, spot, spot, all_grads, frames_f, wide_f, ((FRAMES, CHANNELS), BF), frames_f,
            ((MEMBERS, ROWS, EXTRA), BF), ((TAPS + 1, 8, CHANNELS), F32),
            ((CHANNELS, 1536), BF),
        ],
        56,
        rows, notes, *spots, grads, across, up_beside, beyond, slope, hidden_f, parts,
        alias={11: 2},
    )

    summed = parts = lax.all_to_all(parts, PLANE, 0, 0, tiled=True)
    [parts] = call(
        pack_z,
        [((8, 8, 1536), BF)],
        [],
        16,
        parts,
        near=(0,),
        near_out=(0,),
    )
    parts = lax.all_to_all(parts, "z", 0, 0, tiled=True)
    weight_grad, taps_all = call(
        unpack_z,
        [((BLOCK, 1536), F32), ((32, 1, 1536), F32)],
        [],
        16,
        parts,
        near=(0,),
        near_out=(0, 1),
    )
    taps_all = lax.all_to_all(taps_all, PLANE, 0, 0, tiled=True)
    [kernel_grad] = call(
        arrange,
        [((TAPS, 1536), F32)],
        [((TAPS, 1536), F32)],
        16,
        taps_all,
        near=(0,),
    )

    back = ((2, BACK, CHANNELS), BF)
    kept, given = call(
        transposed,
        [back, back],
        [
            ((FRAMES, CHANNELS), BF), ((CHANNELS, 1536), BF), ((LEFT_U + EDGE_U, CHANNELS), F32),
            ((4, EDGE_U, 1536), BF), kernel_shape,
            slope_f, ((LONG, CHANNELS), F32), back, back,
        ],
        56,
        grad_conv, projection, slope, slot, lent, edges, kernel_f,
    )
    got = lax.ppermute(given, "core", SWAP)
    far = jnp.stack(
        [lax.dynamic_index_in_dim(part, 1 - yh, 0, False) for part in (kept, got)]
    )
    far = lax.ppermute(far, "yh", SWAP)
    frame_grad, gloss = call(
        settle,
        [((128, 1536), BF), ((8, 1536), F32)],
        [
            ((BACK, 1536), BF), ((MEMBERS, ROWS, EXTRA), BF), ((8, EXTRA), F32),
            ((8, 1536), F32),
        ],
        16,
        kept, got, far, summed, lengths,
    )
    return (frame_grad[None], gloss[None], weight_grad, kernel_grad)


def solution(mesh):
    fine = Mesh(mesh.devices.reshape(SIZES), AXES)
    seq = ("z", "x", "yh", "core")
    rows = P(seq + ("rep",), None)
    in_specs = (P("rep", seq, None), P("rep", seq, None), rows, P(), P("rep", seq))
    out_specs = (P("rep", seq, None), P("rep", seq, None), rows, P())
    return jax.shard_map(
        body, mesh=fine, in_specs=in_specs, out_specs=out_specs, check_vma=False
    )
```

```python
import math

import jax
import jax.numpy as jnp
import numpy as np
from jax import lax
from jax.experimental import pallas as pl
from jax.experimental.pallas import tpu as pltpu
from jax.sharding import Mesh
from jax.sharding import PartitionSpec as P

AXES = ("z", "x", "yh", "core", "rep")
SIZES = (8, 4, 2, 2, 2)
GROUP = ("yh", "core")
PLANE = ("x", "yh", "core", "rep")
QUARTERS = 4
BLOCK = 6
EXTRA = 128
MEMBERS, ROWS, LANES = 32, 8, 2304
MESSAGE = MEMBERS * ROWS
FRAMES, CHANNELS, TAPS = 512, 384, 31
EDGE_H, EDGE_U, SPILL = 48, 32, 16
LEFT_H, LEFT_U = 32, 16
WIDE = FRAMES + LEFT_U + EDGE_U
LONG = FRAMES + SPILL
SHARE = EDGE_H + 2 * EDGE_U
HANDED = EDGE_H + 4 * EDGE_U
BACK = 128 + SPILL
SWAP = [(0, 1), (1, 0)]
BF = jnp.bfloat16
F32 = jnp.float32


def placement(part):
    out = np.zeros((CHANNELS, MESSAGE), np.float32)
    for zl in range(2):
        for member in range(MEMBERS):
            for r in range(BLOCK):
                row, i = (zl * MEMBERS + member) * BLOCK + r, zl * BLOCK + r
                if part == 0 and i < ROWS:
                    out[row, member * ROWS + i] = 1
                if part > 0 and i >= ROWS:
                    out[row, member * ROWS + 2 * (i - ROWS) + part - 1] = 1
    return jnp.asarray(out, BF)


def lanes(tile):
    return slice(tile * 128, tile * 128 + 128)


def begin(pairs, sems):
    copies = [pltpu.make_async_copy(a, b, sems.at[i]) for i, (a, b) in enumerate(pairs)]
    for copy in copies:
        copy.start()
    return copies


def finish(copies):
    for copy in copies:
        copy.wait()


def spread(
    weights, durations, hidden, upstream, out, share, edge,
    got, lengths, block, v_share, v_edge, sems,
):
    yh, core = lax.axis_index("yh"), lax.axis_index("core")
    other = pl.ds(pl.multiple_of((1 - yh) * 768, 128), 768)
    last = (yh + core) // 2
    from_h = pl.ds(pl.multiple_of(last * (128 - EDGE_H), 16), EDGE_H)
    from_u = pl.ds(pl.multiple_of(last * (128 - EDGE_U), 16), EDGE_U)
    taken = begin(
        [
            (hidden.at[:, other], v_share.at[pl.ds(0, 128)]),
            (upstream.at[:, pl.ds(0, 768)], v_share.at[pl.ds(128, 128)]),
            (upstream.at[:, pl.ds(768, 768)], v_share.at[pl.ds(256, 128)]),
            (hidden.at[from_h], v_edge.at[pl.ds(0, EDGE_H)]),
            (upstream.at[from_u], v_edge.at[pl.ds(EDGE_H, EDGE_U)]),
        ],
        sems.at[pl.ds(9, 5)],
    )
    finish(begin([(weights, got), (durations, lengths)], sems))
    lane = lax.broadcasted_iota(jnp.int32, (8, EXTRA), 1)
    total = jnp.sum(lengths[...].astype(F32), axis=1, keepdims=True)
    note = jnp.where(lane == lax.axis_index("z"), jnp.broadcast_to(total, (8, EXTRA)), 0.0)
    rows = got[...].astype(F32)
    rest = [
        jnp.concatenate([rows[3 * i + j : 3 * i + j + 1, 1152:] for j in range(3)], axis=1)
        for i in range(2)
    ]
    rows = jnp.concatenate([rows[:, :1152]] + rest, axis=0)
    block[...] = jnp.concatenate([rows, note], axis=1).astype(BF)
    sent = begin([(block, out.at[peer]) for peer in range(8)], sems)
    finish(taken)
    finish(begin([(v_share, share), (v_edge, edge)], sems.at[pl.ds(9, 2)]))
    finish(sent)


def lend(slot, out, v_out, sems):
    other = pl.ds(pl.multiple_of((1 - lax.axis_index("yh")) * 768, 128), 768)
    up = pl.ds(EDGE_H, EDGE_U)
    finish(
        begin(
            [
                (slot.at[pl.ds(0, EDGE_H), other], v_out.at[pl.ds(0, EDGE_H)]),
                (slot.at[up, pl.ds(0, 768)], v_out.at[pl.ds(EDGE_H, EDGE_U)]),
                (slot.at[up, pl.ds(768, 768)], v_out.at[pl.ds(EDGE_H + EDGE_U, EDGE_U)]),
            ],
            sems,
        )
    )
    finish(begin([(v_out, out)], sems))


def pack(got, plane, note_out, rows, block, v_note, sems):
    note = jnp.zeros((8, EXTRA), F32)
    for z in range(8):
        block_z = got[z].astype(F32)
        rest = [block_z[6 + r // 3, 384 * (r % 3) : 384 * (r % 3) + 384] for r in range(BLOCK)]
        block_z, spare = (
            jnp.concatenate([block_z[:BLOCK, :1152], jnp.stack(rest)], axis=1),
            block_z[:, 1152:],
        )
        for r in range(BLOCK):
            i = BLOCK * (z % 2) + r
            at = ROWS * (z // 2)
            if i < ROWS:
                rows[at + i : at + i + 1, :1536] = block_z[r : r + 1]
            else:
                for h in range(2):
                    to = at + 2 * (i - ROWS) + h
                    rows[to : to + 1, 1536:] = block_z[r : r + 1, 768 * h : 768 * h + 768]
        note += spare
    v_note[...] = note
    sent = begin([(v_note, note_out)], sems.at[pl.ds(32, 1)])
    for q in range(4):
        block[q] = rows[ROWS * q : ROWS * q + ROWS].astype(BF)
        members = [j for j in range(MEMBERS) if (j // 2) % 4 == q]
        sent += begin([(block.at[q], plane.at[j]) for j in members], sems.at[pl.ds(8 * q, 8)])
    finish(sent)


def relay(hidden, across, beside, v_beside, sems):
    yh, core = lax.axis_index("yh"), lax.axis_index("core")
    other = pl.ds(pl.multiple_of((yh * 2 + 1 - core) * CHANNELS, 128), CHANNELS)
    part = pl.ds(pl.multiple_of((1 - core) * CHANNELS, 128), CHANNELS)
    moves = [(hidden.at[:, other], v_beside.at[0]), (across.at[pl.ds(0, 128), part], v_beside.at[1])]
    finish(begin(moves, sems))
    finish(begin([(v_beside, beside)], sems))


def relay_edges(slot, lent, beside, v_beside, sems):
    yh, core = lax.axis_index("yh"), lax.axis_index("core")
    other = pl.ds(pl.multiple_of((yh * 2 + 1 - core) * CHANNELS, 128), CHANNELS)
    part = pl.ds(pl.multiple_of((1 - core) * CHANNELS, 128), CHANNELS)
    edge = pl.ds(0, EDGE_H)
    moves = [
        (slot.at[edge, other], v_beside.at[0, edge]),
        (lent.at[edge, part], v_beside.at[1, edge]),
    ]
    for i in range(4):
        cut = pl.ds((i % 2) * CHANNELS, CHANNELS)
        row = pl.ds(EDGE_H + EDGE_U * i, EDGE_U)
        wide = pl.ds(i * CHANNELS, CHANNELS)
        moves.append((slot.at[pl.ds(EDGE_H, EDGE_U), wide], v_beside.at[0, row]))
        moves.append((lent.at[pl.ds(EDGE_H + EDGE_U * (i // 2), EDGE_U), cut], v_beside.at[1, row]))
    finish(begin(moves, sems))
    finish(begin([(v_beside, beside)], sems))


def group_grads(upstream, across, beside, beyond, grads):
    yh, core = lax.axis_index("yh"), lax.axis_index("core")
    moves = [(upstream, grads.at[yh * 2 + core]), (beside, grads.at[yh * 2 + 1 - core])]
    for source, place in ((across, 2 - 2 * yh + core), (beyond, 3 - 2 * yh - core)):
        for i in range(2):
            rows, cut = pl.ds(128 + 128 * i, 128), pl.ds(768 * i, 768)
            moves.append((source.at[rows], grads.at[place, :, cut]))
    return moves


def convolve(
    own, slot, across, lent, beside, edges, upstream, up_beside, beyond, kernel, whole, low, high,
    slope, hidden, parts,
    grads, frames, weights, v_whole, v_low, v_high, v_slope, v_hidden, v_parts, active, sems,
):
    yh, core = lax.axis_index("yh"), lax.axis_index("core")
    part = pl.ds(pl.multiple_of(core * CHANNELS, 128), CHANNELS)
    mine = pl.ds(pl.multiple_of((yh * 2 + core) * CHANNELS, 128), CHANNELS)
    block, edge = pl.ds(0, 128), pl.ds(0, EDGE_H)
    needed = begin(
        [
            (own.at[:, mine], frames.at[yh * 2 + core, pl.ds(0, 128)]),
            (slot.at[pl.ds(0, EDGE_H), mine], frames.at[yh * 2 + core, pl.ds(128, EDGE_H)]),
            (across.at[pl.ds(0, 128), part], frames.at[(1 - yh) * 2 + core, pl.ds(0, 128)]),
            (lent.at[pl.ds(0, EDGE_H), part], frames.at[(1 - yh) * 2 + core, pl.ds(128, EDGE_H)]),
            (beside.at[0], frames.at[yh * 2 + 1 - core, block]),
            (beside.at[1], frames.at[(1 - yh) * 2 + 1 - core, block]),
            (edges.at[0, edge], frames.at[yh * 2 + 1 - core, pl.ds(128, EDGE_H)]),
            (edges.at[1, edge], frames.at[(1 - yh) * 2 + 1 - core, pl.ds(128, EDGE_H)]),
            (kernel, weights),
        ],
        sems,
    )
    later = begin(
        group_grads(upstream, across, up_beside, beyond, grads) + [(whole, v_whole), (low, v_low), (high, v_high)],
        sems.at[pl.ds(10, 9)],
    )
    finish(needed)
    v_hidden[:LEFT_H] = frames[0, 128 + EDGE_H - LEFT_H :].astype(F32)
    for b in range(4):
        v_hidden[LEFT_H + 128 * b : LEFT_H + 128 * b + 128] = frames[b, :128].astype(F32)
    v_hidden[LEFT_H + FRAMES :] = frames[3, 128:].astype(F32)
    rows = 112
    for tile in range(CHANNELS // 128):

        def chunk(c, _, tile=tile):
            base = pl.multiple_of(c * rows, 8)
            total = jnp.zeros((rows, 128), F32)
            window = v_hidden[pl.ds(base, rows + 32), lanes(tile)]
            for b in range(8):
                slab = window[b : b + rows + 24]
                for a in range(4):
                    k = 8 * a + b - 1
                    if 0 <= k < TAPS:
                        total += weights[k : k + 1, lanes(tile)] * slab[8 * a : 8 * a + rows]
            sig = jax.nn.sigmoid(total)
            v_slope[pl.ds(base, rows), lanes(tile)] = sig * (1.0 + total * (1.0 - sig))
            active[pl.ds(base, rows), lanes(tile)] = total * sig
            return 0

        lax.fori_loop(0, WIDE // rows, chunk, 0, unroll=True)
    out = begin([(v_slope, slope), (v_hidden, hidden)], sems)
    finish(later)
    acts = active[LEFT_U : LEFT_U + FRAMES].astype(BF)
    def outer(spot, cut):
        columns = jnp.dot(acts, spot[...], preferred_element_type=F32).astype(BF)
        return lax.dot_general(
            columns,
            grads[:, :, cut].reshape(FRAMES, -1),
            (((0,), (0,)), ((), ())),
            preferred_element_type=F32,
        )

    product = outer(v_whole, slice(0, 1536))
    for j in range(MEMBERS):
        v_parts[j, :, :1536] = product[ROWS * j : ROWS * j + ROWS].astype(BF)
    cut = pl.ds(0, 1536)
    out += begin([(v_parts.at[:, :, cut], parts.at[:, :, cut])], sems.at[pl.ds(2, 1)])
    halves = outer(v_low, slice(0, 768)) + outer(v_high, slice(768, 1536))
    for j in range(MEMBERS):
        v_parts[j, :, 1536:] = halves[ROWS * j : ROWS * j + ROWS].astype(BF)
    cut = pl.ds(1536, LANES - 1536)
    out += begin([(v_parts.at[:, :, cut], parts.at[:, :, cut])], sems.at[pl.ds(3, 1)])
    finish(out)


def backward(
    gathered, notes, whole, low, high, upstream, across, up_beside, beyond, slope, hidden, parts,
    grad_conv, projection, message,
    got, v_note, v_whole, v_low, v_high, grads, v_slope, v_hidden, v_grad, v_grad_f, v_taps, sums, v_weights, sems,
):
    needed = begin(
        [(gathered, got), (whole, v_whole), (low, v_low), (high, v_high), (notes, v_note)], sems
    )
    later = begin(
        group_grads(upstream, across, up_beside, beyond, grads), sems.at[pl.ds(5, 6)]
    )
    last = begin(
        [(slope.at[pl.ds(LEFT_U, FRAMES)], v_slope), (hidden, v_hidden)], sems.at[pl.ds(13, 2)]
    )
    finish(needed)
    rows = got[:, :, :1536].reshape(MESSAGE, 1536)
    halves = got[:, :, 1536:].reshape(MESSAGE, 768)
    for side, spot in enumerate((v_low, v_high)):
        cut = slice(768 * side, 768 * side + 768)
        value = jnp.dot(v_whole[...], rows[:, cut], preferred_element_type=F32)
        value += jnp.dot(spot[...], halves, preferred_element_type=F32)
        v_weights[:, cut] = value.astype(BF)
    finish(later)
    value = lax.dot_general(
        grads[...].reshape(FRAMES, 1536),
        v_weights[...],
        (((1,), (1,)), ((), ())),
        preferred_element_type=F32,
    )
    finish(last)
    value = (value * v_slope[...]).astype(BF)
    v_grad[...] = value
    v_grad_f[...] = value.astype(F32)
    out = begin([(v_grad, grad_conv), (v_weights, projection)], sems)
    span = 128
    sums[...] = jnp.zeros_like(sums)
    for tile in range(CHANNELS // 128):

        def piece(c, _, tile=tile):
            base = pl.multiple_of(c * span, 8)
            terms = v_grad_f[pl.ds(base, span), lanes(tile)]
            window = v_hidden[pl.ds(base + LEFT_U, span + 32), lanes(tile)]
            for b in range(8):
                slab = window[b : b + span + 24]
                for a in range(4):
                    k = 8 * a + b - 1
                    if 0 <= k < TAPS:
                        sums[k, :, lanes(tile)] += jnp.sum(
                            (terms * slab[8 * a : 8 * a + span]).reshape(span // 8, 8, 128),
                            axis=0,
                        )
            return 0

        lax.fori_loop(0, FRAMES // span, piece, 0, unroll=True)
    for j in range(MEMBERS):
        rows = [
            jnp.sum(sums[j, :, lanes(tile)], axis=0, keepdims=True)
            for tile in range(CHANNELS // 128)
        ]
        rows = jnp.concatenate(rows, axis=0)
        high_part = rows.astype(BF).astype(F32)
        rows = [high_part, rows - high_part, v_note[:1], jnp.zeros((ROWS - 7, 128), F32)]
        v_taps[j] = jnp.concatenate(rows, axis=0).astype(BF)
    finish(begin([(v_taps, message.at[:, :, pl.ds(LANES, EXTRA)])], sems.at[pl.ds(3, 1)]))
    finish(out)


def transposed(
    grad_conv, projection, slope, slot, lent, beside, kernel,
    kept, given, v_grad, v_weights, v_slope, ups, weights, wide, total_f, v_kept, v_given, sems,
):
    yh, core = lax.axis_index("yh"), lax.axis_index("core")
    edges = [(slot.at[pl.ds(EDGE_H, EDGE_U)], ups.at[yh * 2 + core])]
    for i in range(2):
        edges.append(
            (
                lent.at[pl.ds(EDGE_H + EDGE_U * i, EDGE_U)],
                ups.at[(1 - yh) * 2 + core, :, pl.ds(768 * i, 768)],
            )
        )
    for i in range(4):
        row, cut = pl.ds(EDGE_H + EDGE_U * i, EDGE_U), pl.ds(CHANNELS * i, CHANNELS)
        edges.append((beside.at[0, row], ups.at[yh * 2 + 1 - core, :, cut]))
        edges.append((beside.at[1, row], ups.at[(1 - yh) * 2 + 1 - core, :, cut]))
    edges += [
        (projection, v_weights),
        (slope.at[pl.ds(0, LEFT_U)], v_slope.at[pl.ds(0, LEFT_U)]),
        (slope.at[pl.ds(LEFT_U + FRAMES, EDGE_U)], v_slope.at[pl.ds(LEFT_U, EDGE_U)]),
        (grad_conv, v_grad),
        (kernel, weights),
    ]
    finish(begin(edges, sems))
    rows = jnp.concatenate([ups[0, EDGE_U - LEFT_U :], ups[3]], axis=0)
    value = lax.dot_general(
        rows, v_weights[...], (((1,), (1,)), ((), ())), preferred_element_type=F32
    )
    value = (value * v_slope[...]).astype(BF).astype(F32)
    wide[:LEFT_U] = value[:LEFT_U]
    wide[LEFT_U : LEFT_U + FRAMES] = v_grad[...].astype(F32)
    wide[LEFT_U + FRAMES :] = value[LEFT_U:]
    rows = 88
    for tile in range(CHANNELS // 128):

        def chunk(c, _, tile=tile):
            base = pl.multiple_of(c * rows, 8)
            total = jnp.zeros((rows, 128), F32)
            window = wide[pl.ds(base, rows + 32), lanes(tile)]
            for b in range(8):
                slab = window[b : b + rows + 24]
                for a in range(4):
                    k = TAPS - 8 * a - b
                    if 0 <= k < TAPS:
                        total += weights[k : k + 1, lanes(tile)] * slab[8 * a : 8 * a + rows]
            total_f[pl.ds(base, rows), lanes(tile)] = total
            return 0

        lax.fori_loop(0, LONG // rows, chunk, 0)
    for row in range(2):
        for out, side in ((v_kept, core), (v_given, 1 - core)):
            begin_row = pl.multiple_of((row * 2 + side) * 128, 128)
            out[row] = total_f[pl.ds(begin_row, BACK)].astype(BF)
    finish(begin([(v_kept, kept), (v_given, given)], sems))


def settle(
    kept, got, far, gathered, lengths, frame_grad, gloss, frames, notes, v_lengths, v_gloss, sems
):
    yh, core = lax.axis_index("yh"), lax.axis_index("core")
    sources = [(kept.at[yh], yh, core), (got.at[yh], yh, 1 - core)]
    sources += [(far.at[0], 1 - yh, core), (far.at[1], 1 - yh, 1 - core)]
    moves = [(lengths, v_lengths), (gathered.at[:, :, pl.ds(LANES, EXTRA)], notes)]
    for source, a, b in sources:
        cut = pl.ds(pl.multiple_of((a * 2 + b) * CHANNELS, 128), CHANNELS)
        moves.append((source, frames.at[:, cut]))
    finish(begin(moves, sems))
    out = begin([(frames.at[pl.ds(0, 128)], frame_grad)], sems)
    mine = yh * 2 + core
    place = lax.axis_index("z") * 4 + lax.axis_index("x")
    lane = lax.broadcasted_iota(jnp.int32, (8, EXTRA), 1)
    start = jnp.zeros((8, EXTRA), F32)
    for member in range(MEMBERS):
        block = lane * 16 + member // 2
        earlier = (block < place * 4 + mine) & (lane < 8) & (lax.axis_index("rep") == member % 2)
        start += jnp.where(earlier, notes[member, 6:7].astype(F32), 0.0)
    start = jnp.sum(start, axis=1, keepdims=True) - (place * FRAMES + mine * 128).astype(F32)
    gloss_id = lax.broadcasted_iota(jnp.int32, (8, EXTRA), 0)
    length = v_lengths[...]
    first = jnp.sum(jnp.where(lane < gloss_id, length, 0.0), axis=1, keepdims=True) + start
    last = first + jnp.sum(jnp.where(lane == gloss_id, length, 0.0), axis=1, keepdims=True)
    at = lax.broadcasted_iota(jnp.int32, (8, 128 + SPILL), 1).astype(F32)
    covers = jnp.where((at >= first) & (at < last), 1.0, 0.0).astype(BF)
    v_gloss[...] = jnp.dot(covers, frames[...], preferred_element_type=F32)
    finish(begin([(v_gloss, gloss)], sems.at[pl.ds(1, 1)]))
    finish(out)


def pack_z(parts, out, sems):
    sums = []
    for q in range(4):
        total = jnp.zeros((ROWS, LANES + EXTRA), F32)
        for x in range(4):
            for rep in range(2):
                total += parts[(x * 4 + q) * 2 + rep].astype(F32)
        sums.append(total)
    taps = [total[:3, LANES:] + total[3:6, LANES:] for total in sums]
    taps = jnp.concatenate([t[j : j + 1] for t in taps for j in range(3)], axis=1)
    high = taps.astype(BF).astype(F32)
    for z in range(8):
        total = sums[z // 2]
        rows = [total[:BLOCK, :1536]]
        if z % 2:
            rows = [total[BLOCK:, :1536]]
            for i in range(0, ROWS, 2):
                halves = [total[i + h : i + h + 1, 1536:LANES] for h in range(2)]
                rows.append(jnp.concatenate(halves, axis=1))
        rows += [high, taps - high]
        out[z] = jnp.concatenate(rows, axis=0).astype(BF)


def unpack_z(got, weights, taps, sems):
    total = got[0].astype(F32)
    for z in range(1, 8):
        total += got[z].astype(F32)
    total = total * (1.0 / math.sqrt(2 * 16384))
    weights[...] = total[:BLOCK]
    for peer in range(MEMBERS):
        taps[peer] = total[6:7] + total[7:8]


def arrange(got, out, v_out, sems):
    for k in range(TAPS):
        v_out[k : k + 1] = got[k]
    finish(begin([(v_out, out)], sems))


def call(
    kernel, outs, scratch, megabytes, *args, alias=None, flops=200_000_000, near=(), near_out=()
):
    def space(vmem):
        return pl.BlockSpec(memory_space=pltpu.VMEM if vmem else pltpu.HBM)

    shapes = [jax.ShapeDtypeStruct(shape, dtype) for shape, dtype in outs]
    size = sum(math.prod(s.shape) * s.dtype.itemsize for s in list(args) + shapes)
    return pl.pallas_call(
        kernel,
        out_shape=shapes,
        in_specs=[space(i in near) for i in range(len(args))],
        out_specs=[space(i in near_out) for i in range(len(shapes))],
        scratch_shapes=[pltpu.VMEM(shape, dtype) for shape, dtype in scratch]
        + [pltpu.SemaphoreType.DMA((48,))],
        input_output_aliases=alias or {},
        compiler_params=pltpu.CompilerParams(vmem_limit_bytes=megabytes * 2**20),
        cost_estimate=pl.CostEstimate(
            flops=flops, bytes_accessed=size, transcendentals=0
        ),
    )(*args)


def body(hidden_in, upstream, out_weight, conv_kernel, durations):
    yh, core = lax.axis_index("yh"), lax.axis_index("core")
    quarter = yh * 2 + core
    hidden, grads = hidden_in[0], upstream[0]
    lengths = jnp.broadcast_to(
        jnp.pad(durations.astype(F32), ((0, 0), (0, EXTRA - durations.shape[1]))), (8, EXTRA)
    )

    rows, share, edge = call(
        spread,
        [((8, 8, 1280), BF), ((384, 768), BF), ((EDGE_H + EDGE_U, 1536), BF)],
        [
            ((BLOCK, 1536), BF), ((1, 8), jnp.int32), ((8, 1280), BF), ((384, 768), BF),
            ((EDGE_H + EDGE_U, 1536), BF),
        ],
        56,
        out_weight, durations, hidden, grads,
    )
    ends = [(4 * i + 3, 4 * i + 4) for i in range(31)]
    slot = lax.ppermute(edge, ("z", "x", "yh", "core"), ends + [(b, a) for a, b in ends])
    rows = lax.all_to_all(rows, "z", 0, 0, tiled=True)
    across = lax.ppermute(share, "yh", SWAP)
    up_beside = lax.ppermute(grads, "core", SWAP)
    beyond = lax.ppermute(across, "core", SWAP)
    [lent] = call(lend, [((SHARE, 768), BF)], [((SHARE, 768), BF)], 16, slot)
    lent = lax.ppermute(lent, GROUP, [(0, 2), (3, 1)])
    message = ((MEMBERS, ROWS, LANES + EXTRA), BF)
    note = ((8, EXTRA), F32)
    plane, notes = call(
        pack,
        [((MEMBERS, ROWS, LANES), BF), note],
        [((4 * ROWS, LANES), F32), ((4, ROWS, LANES), BF), note],
        16,
        rows,
        near=(0,),
    )
    handed = ((2, 128, CHANNELS), BF)
    [beside] = call(relay, [handed], [handed], 16, hidden, across, flops=3_000_000_000)
    handed = ((2, HANDED, CHANNELS), BF)
    [edges] = call(relay_edges, [handed], [handed], 16, slot, lent, flops=30_000_000_000)
    rows = lax.all_to_all(plane, PLANE, 0, 0, tiled=True)
    beside = lax.ppermute(beside, "core", SWAP)
    edges = lax.ppermute(edges, "core", SWAP)
    kernel_f = lax.dynamic_slice_in_dim(
        jnp.pad(conv_kernel, ((0, 1), (0, 0))), quarter * CHANNELS, CHANNELS, 1
    ).astype(F32)
    spot = ((CHANNELS, MESSAGE), BF)
    spots = [placement(part) for part in range(3)]
    frames_f = ((FRAMES, CHANNELS), F32)
    wide_f = ((LEFT_H + FRAMES + EDGE_H, CHANNELS), F32)
    slope_f = ((WIDE, CHANNELS), F32)
    all_grads = ((4, 128, 1536), BF)
    sent = ((MEMBERS, ROWS, LANES), BF)
    kernel_shape = ((TAPS + 1, CHANNELS), F32)
    slope, hidden_f, parts = call(
        convolve,
        [slope_f, wide_f, message],
        [
            all_grads, ((4, 128 + EDGE_H, CHANNELS), BF), kernel_shape, spot, spot, spot, slope_f, wide_f,
            sent, slope_f,
        ],
        56,
        hidden, slot, across, lent, beside, edges, grads, up_beside, beyond, kernel_f, *spots,
    )
    grad_conv, projection, parts = call(
        backward,
        [
            ((FRAMES, CHANNELS), BF), ((CHANNELS, 1536), BF), message,
        ],
        [
            sent, note, spot, spot, spot, all_grads, frames_f, wide_f, ((FRAMES, CHANNELS), BF), frames_f,
            ((MEMBERS, ROWS, EXTRA), BF), ((TAPS + 1, 8, CHANNELS), F32),
            ((CHANNELS, 1536), BF),
        ],
        56,
        rows, notes, *spots, grads, across, up_beside, beyond, slope, hidden_f, parts,
        alias={11: 2},
    )

    summed = parts = lax.all_to_all(parts, PLANE, 0, 0, tiled=True)
    [parts] = call(
        pack_z,
        [((8, 8, 1536), BF)],
        [],
        16,
        parts,
        near=(0,),
        near_out=(0,),
    )
    parts = lax.all_to_all(parts, "z", 0, 0, tiled=True)
    weight_grad, taps_all = call(
        unpack_z,
        [((BLOCK, 1536), F32), ((32, 1, 1536), F32)],
        [],
        16,
        parts,
        near=(0,),
        near_out=(0, 1),
    )
    taps_all = lax.all_to_all(taps_all, PLANE, 0, 0, tiled=True)
    [kernel_grad] = call(
        arrange,
        [((TAPS, 1536), F32)],
        [((TAPS, 1536), F32)],
        16,
        taps_all,
        near=(0,),
    )

    back = ((2, BACK, CHANNELS), BF)
    kept, given = call(
        transposed,
        [back, back],
        [
            ((FRAMES, CHANNELS), BF), ((CHANNELS, 1536), BF), ((LEFT_U + EDGE_U, CHANNELS), F32),
            ((4, EDGE_U, 1536), BF), kernel_shape,
            slope_f, ((LONG, CHANNELS), F32), back, back,
        ],
        56,
        grad_conv, projection, slope, slot, lent, edges, kernel_f,
    )
    got = lax.ppermute(given, "core", SWAP)
    far = jnp.stack(
        [lax.dynamic_index_in_dim(part, 1 - yh, 0, False) for part in (kept, got)]
    )
    far = lax.ppermute(far, "yh", SWAP)
    frame_grad, gloss = call(
        settle,
        [((128, 1536), BF), ((8, 1536), F32)],
        [
            ((BACK, 1536), BF), ((MEMBERS, ROWS, EXTRA), BF), ((8, EXTRA), F32),
            ((8, 1536), F32),
        ],
        16,
        kept, got, far, summed, lengths,
    )
    return (frame_grad[None], gloss[None], weight_grad, kernel_grad)


def solution(mesh):
    fine = Mesh(mesh.devices.reshape(SIZES), AXES)
    seq = ("z", "x", "yh", "core")
    rows = P(seq + ("rep",), None)
    in_specs = (P("rep", seq, None), P("rep", seq, None), rows, P(), P("rep", seq))
    out_specs = (P("rep", seq, None), P("rep", seq, None), rows, P())
    return jax.shard_map(
        body, mesh=fine, in_specs=in_specs, out_specs=out_specs, check_vma=False
    )
```

```python
import math

import jax
import jax.numpy as jnp
import numpy as np
from jax import lax
from jax.experimental import pallas as pl
from jax.experimental.pallas import tpu as pltpu
from jax.sharding import Mesh
from jax.sharding import PartitionSpec as P

AXES = ("z", "x", "yh", "core", "rep")
SIZES = (8, 4, 2, 2, 2)
GROUP = ("yh", "core")
PLANE = ("x", "yh", "core", "rep")
QUARTERS = 4
BLOCK = 6
EXTRA = 128
MEMBERS, ROWS, LANES = 32, 8, 2304
MESSAGE = MEMBERS * ROWS
FRAMES, CHANNELS, TAPS = 512, 384, 31
EDGE_H, EDGE_U, SPILL = 48, 32, 16
LEFT_H, LEFT_U = 32, 16
WIDE = FRAMES + LEFT_U + EDGE_U
LONG = FRAMES + SPILL
SHARE = EDGE_H + 2 * EDGE_U
HANDED = EDGE_H + 4 * EDGE_U
BACK = 128 + SPILL
SWAP = [(0, 1), (1, 0)]
BF = jnp.bfloat16
F32 = jnp.float32


def placement(part):
    out = np.zeros((CHANNELS, MESSAGE), np.float32)
    for zl in range(2):
        for member in range(MEMBERS):
            for r in range(BLOCK):
                row, i = (zl * MEMBERS + member) * BLOCK + r, zl * BLOCK + r
                if part == 0 and i < ROWS:
                    out[row, member * ROWS + i] = 1
                if part > 0 and i >= ROWS:
                    out[row, member * ROWS + 2 * (i - ROWS) + part - 1] = 1
    return jnp.asarray(out, BF)


def lanes(tile):
    return slice(tile * 128, tile * 128 + 128)


def begin(pairs, sems):
    copies = [pltpu.make_async_copy(a, b, sems.at[i]) for i, (a, b) in enumerate(pairs)]
    for copy in copies:
        copy.start()
    return copies


def finish(copies):
    for copy in copies:
        copy.wait()


def spread(
    weights, durations, hidden, upstream, out, share, edge,
    got, lengths, block, v_share, v_edge, sems,
):
    yh, core = lax.axis_index("yh"), lax.axis_index("core")
    other = pl.ds(pl.multiple_of((1 - yh) * 768, 128), 768)
    last = (yh + core) // 2
    from_h = pl.ds(pl.multiple_of(last * (128 - EDGE_H), 16), EDGE_H)
    from_u = pl.ds(pl.multiple_of(last * (128 - EDGE_U), 16), EDGE_U)
    taken = begin(
        [
            (hidden.at[:, other], v_share.at[pl.ds(0, 128)]),
            (upstream.at[:, pl.ds(0, 768)], v_share.at[pl.ds(128, 128)]),
            (upstream.at[:, pl.ds(768, 768)], v_share.at[pl.ds(256, 128)]),
            (hidden.at[from_h], v_edge.at[pl.ds(0, EDGE_H)]),
            (upstream.at[from_u], v_edge.at[pl.ds(EDGE_H, EDGE_U)]),
        ],
        sems.at[pl.ds(9, 5)],
    )
    finish(begin([(weights, got), (durations, lengths)], sems))
    lane = lax.broadcasted_iota(jnp.int32, (8, EXTRA), 1)
    total = jnp.sum(lengths[...].astype(F32), axis=1, keepdims=True)
    note = jnp.where(lane == lax.axis_index("z"), jnp.broadcast_to(total, (8, EXTRA)), 0.0)
    rows = got[...].astype(F32)
    rest = [
        jnp.concatenate([rows[3 * i + j : 3 * i + j + 1, 1152:] for j in range(3)], axis=1)
        for i in range(2)
    ]
    rows = jnp.concatenate([rows[:, :1152]] + rest, axis=0)
    block[...] = jnp.concatenate([rows, note], axis=1).astype(BF)
    sent = begin([(block, out.at[peer]) for peer in range(8)], sems)
    finish(taken)
    finish(begin([(v_share, share), (v_edge, edge)], sems.at[pl.ds(9, 2)]))
    finish(sent)


def lend(slot, out, v_out, sems):
    other = pl.ds(pl.multiple_of((1 - lax.axis_index("yh")) * 768, 128), 768)
    up = pl.ds(EDGE_H, EDGE_U)
    finish(
        begin(
            [
                (slot.at[pl.ds(0, EDGE_H), other], v_out.at[pl.ds(0, EDGE_H)]),
                (slot.at[up, pl.ds(0, 768)], v_out.at[pl.ds(EDGE_H, EDGE_U)]),
                (slot.at[up, pl.ds(768, 768)], v_out.at[pl.ds(EDGE_H + EDGE_U, EDGE_U)]),
            ],
            sems,
        )
    )
    finish(begin([(v_out, out)], sems))


def pack(got, plane, note_out, rows, block, v_note, sems):
    note = jnp.zeros((8, EXTRA), F32)
    for z in range(8):
        block_z = got[z].astype(F32)
        rest = [block_z[6 + r // 3, 384 * (r % 3) : 384 * (r % 3) + 384] for r in range(BLOCK)]
        block_z, spare = (
            jnp.concatenate([block_z[:BLOCK, :1152], jnp.stack(rest)], axis=1),
            block_z[:, 1152:],
        )
        for r in range(BLOCK):
            i = BLOCK * (z % 2) + r
            at = ROWS * (z // 2)
            if i < ROWS:
                rows[at + i : at + i + 1, :1536] = block_z[r : r + 1]
            else:
                for h in range(2):
                    to = at + 2 * (i - ROWS) + h
                    rows[to : to + 1, 1536:] = block_z[r : r + 1, 768 * h : 768 * h + 768]
        note += spare
    v_note[...] = note
    sent = begin([(v_note, note_out)], sems.at[pl.ds(32, 1)])
    for q in range(4):
        block[q] = rows[ROWS * q : ROWS * q + ROWS].astype(BF)
        members = [j for j in range(MEMBERS) if (j // 2) % 4 == q]
        sent += begin([(block.at[q], plane.at[j]) for j in members], sems.at[pl.ds(8 * q, 8)])
    finish(sent)


def relay(hidden, across, beside, v_beside, sems):
    yh, core = lax.axis_index("yh"), lax.axis_index("core")
    other = pl.ds(pl.multiple_of((yh * 2 + 1 - core) * CHANNELS, 128), CHANNELS)
    part = pl.ds(pl.multiple_of((1 - core) * CHANNELS, 128), CHANNELS)
    moves = [(hidden.at[:, other], v_beside.at[0]), (across.at[pl.ds(0, 128), part], v_beside.at[1])]
    finish(begin(moves, sems))
    finish(begin([(v_beside, beside)], sems))


def relay_edges(slot, lent, beside, v_beside, sems):
    yh, core = lax.axis_index("yh"), lax.axis_index("core")
    other = pl.ds(pl.multiple_of((yh * 2 + 1 - core) * CHANNELS, 128), CHANNELS)
    part = pl.ds(pl.multiple_of((1 - core) * CHANNELS, 128), CHANNELS)
    edge = pl.ds(0, EDGE_H)
    moves = [
        (slot.at[edge, other], v_beside.at[0, edge]),
        (lent.at[edge, part], v_beside.at[1, edge]),
    ]
    for i in range(4):
        cut = pl.ds((i % 2) * CHANNELS, CHANNELS)
        row = pl.ds(EDGE_H + EDGE_U * i, EDGE_U)
        wide = pl.ds(i * CHANNELS, CHANNELS)
        moves.append((slot.at[pl.ds(EDGE_H, EDGE_U), wide], v_beside.at[0, row]))
        moves.append((lent.at[pl.ds(EDGE_H + EDGE_U * (i // 2), EDGE_U), cut], v_beside.at[1, row]))
    finish(begin(moves, sems))
    finish(begin([(v_beside, beside)], sems))


def group_grads(upstream, across, beside, beyond, grads):
    yh, core = lax.axis_index("yh"), lax.axis_index("core")
    moves = [(upstream, grads.at[yh * 2 + core]), (beside, grads.at[yh * 2 + 1 - core])]
    for source, place in ((across, 2 - 2 * yh + core), (beyond, 3 - 2 * yh - core)):
        for i in range(2):
            rows, cut = pl.ds(128 + 128 * i, 128), pl.ds(768 * i, 768)
            moves.append((source.at[rows], grads.at[place, :, cut]))
    return moves


def convolve(
    own, slot, across, lent, beside, edges, upstream, up_beside, beyond, kernel, whole, low, high,
    slope, hidden, parts,
    grads, frames, weights, v_whole, v_low, v_high, v_slope, v_hidden, v_parts, active, sems,
):
    yh, core = lax.axis_index("yh"), lax.axis_index("core")
    part = pl.ds(pl.multiple_of(core * CHANNELS, 128), CHANNELS)
    mine = pl.ds(pl.multiple_of((yh * 2 + core) * CHANNELS, 128), CHANNELS)
    block, edge = pl.ds(0, 128), pl.ds(0, EDGE_H)
    needed = begin(
        [
            (own.at[:, mine], frames.at[yh * 2 + core, pl.ds(0, 128)]),
            (slot.at[pl.ds(0, EDGE_H), mine], frames.at[yh * 2 + core, pl.ds(128, EDGE_H)]),
            (across.at[pl.ds(0, 128), part], frames.at[(1 - yh) * 2 + core, pl.ds(0, 128)]),
            (lent.at[pl.ds(0, EDGE_H), part], frames.at[(1 - yh) * 2 + core, pl.ds(128, EDGE_H)]),
            (beside.at[0], frames.at[yh * 2 + 1 - core, block]),
            (beside.at[1], frames.at[(1 - yh) * 2 + 1 - core, block]),
            (edges.at[0, edge], frames.at[yh * 2 + 1 - core, pl.ds(128, EDGE_H)]),
            (edges.at[1, edge], frames.at[(1 - yh) * 2 + 1 - core, pl.ds(128, EDGE_H)]),
            (kernel, weights),
        ],
        sems,
    )
    later = begin(
        group_grads(upstream, across, up_beside, beyond, grads) + [(whole, v_whole), (low, v_low), (high, v_high)],
        sems.at[pl.ds(10, 9)],
    )
    finish(needed)
    v_hidden[:LEFT_H] = frames[0, 128 + EDGE_H - LEFT_H :].astype(F32)
    for b in range(4):
        v_hidden[LEFT_H + 128 * b : LEFT_H + 128 * b + 128] = frames[b, :128].astype(F32)
    v_hidden[LEFT_H + FRAMES :] = frames[3, 128:].astype(F32)
    rows = 112
    for tile in range(CHANNELS // 128):

        def chunk(c, _, tile=tile):
            base = pl.multiple_of(c * rows, 8)
            total = jnp.zeros((rows, 128), F32)
            window = v_hidden[pl.ds(base, rows + 32), lanes(tile)]
            for b in range(8):
                slab = window[b : b + rows + 24]
                for a in range(4):
                    k = 8 * a + b - 1
                    if 0 <= k < TAPS:
                        total += weights[k : k + 1, lanes(tile)] * slab[8 * a : 8 * a + rows]
            sig = jax.nn.sigmoid(total)
            v_slope[pl.ds(base, rows), lanes(tile)] = sig * (1.0 + total * (1.0 - sig))
            active[pl.ds(base, rows), lanes(tile)] = total * sig
            return 0

        lax.fori_loop(0, WIDE // rows, chunk, 0, unroll=True)
    out = begin([(v_slope, slope), (v_hidden, hidden)], sems)
    finish(later)
    acts = active[LEFT_U : LEFT_U + FRAMES].astype(BF)
    def outer(spot, cut):
        columns = jnp.dot(acts, spot[...], preferred_element_type=F32).astype(BF)
        return lax.dot_general(
            columns,
            grads[:, :, cut].reshape(FRAMES, -1),
            (((0,), (0,)), ((), ())),
            preferred_element_type=F32,
        )

    product = outer(v_whole, slice(0, 1536))
    for j in range(MEMBERS):
        v_parts[j, :, :1536] = product[ROWS * j : ROWS * j + ROWS].astype(BF)
    cut = pl.ds(0, 1536)
    out += begin([(v_parts.at[:, :, cut], parts.at[:, :, cut])], sems.at[pl.ds(2, 1)])
    halves = outer(v_low, slice(0, 768)) + outer(v_high, slice(768, 1536))
    for j in range(MEMBERS):
        v_parts[j, :, 1536:] = halves[ROWS * j : ROWS * j + ROWS].astype(BF)
    cut = pl.ds(1536, LANES - 1536)
    out += begin([(v_parts.at[:, :, cut], parts.at[:, :, cut])], sems.at[pl.ds(3, 1)])
    finish(out)


def backward(
    gathered, notes, whole, low, high, upstream, across, up_beside, beyond, slope, hidden, parts,
    grad_conv, projection, message,
    got, v_note, v_whole, v_low, v_high, grads, v_slope, v_hidden, v_grad, v_grad_f, v_taps, sums, v_weights, sems,
):
    needed = begin(
        [(gathered, got), (whole, v_whole), (low, v_low), (high, v_high), (notes, v_note)], sems
    )
    finish(needed)
    later = begin(
        group_grads(upstream, across, up_beside, beyond, grads), sems.at[pl.ds(5, 6)]
    )
    last = begin(
        [(slope.at[pl.ds(LEFT_U, FRAMES)], v_slope), (hidden, v_hidden)], sems.at[pl.ds(13, 2)]
    )
    rows = got[:, :, :1536].reshape(MESSAGE, 1536)
    halves = got[:, :, 1536:].reshape(MESSAGE, 768)
    for side, spot in enumerate((v_low, v_high)):
        cut = slice(768 * side, 768 * side + 768)
        value = jnp.dot(v_whole[...], rows[:, cut], preferred_element_type=F32)
        value += jnp.dot(spot[...], halves, preferred_element_type=F32)
        v_weights[:, cut] = value.astype(BF)
    finish(later)
    value = lax.dot_general(
        grads[...].reshape(FRAMES, 1536),
        v_weights[...],
        (((1,), (1,)), ((), ())),
        preferred_element_type=F32,
    )
    finish(last)
    value = (value * v_slope[...]).astype(BF)
    v_grad[...] = value
    v_grad_f[...] = value.astype(F32)
    out = begin([(v_grad, grad_conv), (v_weights, projection)], sems)
    span = 128
    sums[...] = jnp.zeros_like(sums)
    for tile in range(CHANNELS // 128):

        def piece(c, _, tile=tile):
            base = pl.multiple_of(c * span, 8)
            terms = v_grad_f[pl.ds(base, span), lanes(tile)]
            window = v_hidden[pl.ds(base + LEFT_U, span + 32), lanes(tile)]
            for b in range(8):
                slab = window[b : b + span + 24]
                for a in range(4):
                    k = 8 * a + b - 1
                    if 0 <= k < TAPS:
                        sums[k, :, lanes(tile)] += jnp.sum(
                            (terms * slab[8 * a : 8 * a + span]).reshape(span // 8, 8, 128),
                            axis=0,
                        )
            return 0

        lax.fori_loop(0, FRAMES // span, piece, 0, unroll=True)
    for j in range(MEMBERS):
        rows = [
            jnp.sum(sums[j, :, lanes(tile)], axis=0, keepdims=True)
            for tile in range(CHANNELS // 128)
        ]
        rows = jnp.concatenate(rows, axis=0)
        high_part = rows.astype(BF).astype(F32)
        rows = [high_part, rows - high_part, v_note[:1], jnp.zeros((ROWS - 7, 128), F32)]
        v_taps[j] = jnp.concatenate(rows, axis=0).astype(BF)
    finish(begin([(v_taps, message.at[:, :, pl.ds(LANES, EXTRA)])], sems.at[pl.ds(3, 1)]))
    finish(out)


def transposed(
    grad_conv, projection, slope, slot, lent, beside, kernel,
    kept, given, v_grad, v_weights, v_slope, ups, weights, wide, total_f, v_kept, v_given, sems,
):
    yh, core = lax.axis_index("yh"), lax.axis_index("core")
    edges = [(slot.at[pl.ds(EDGE_H, EDGE_U)], ups.at[yh * 2 + core])]
    for i in range(2):
        edges.append(
            (
                lent.at[pl.ds(EDGE_H + EDGE_U * i, EDGE_U)],
                ups.at[(1 - yh) * 2 + core, :, pl.ds(768 * i, 768)],
            )
        )
    for i in range(4):
        row, cut = pl.ds(EDGE_H + EDGE_U * i, EDGE_U), pl.ds(CHANNELS * i, CHANNELS)
        edges.append((beside.at[0, row], ups.at[yh * 2 + 1 - core, :, cut]))
        edges.append((beside.at[1, row], ups.at[(1 - yh) * 2 + 1 - core, :, cut]))
    edges += [
        (projection, v_weights),
        (slope.at[pl.ds(0, LEFT_U)], v_slope.at[pl.ds(0, LEFT_U)]),
        (slope.at[pl.ds(LEFT_U + FRAMES, EDGE_U)], v_slope.at[pl.ds(LEFT_U, EDGE_U)]),
        (grad_conv, v_grad),
        (kernel, weights),
    ]
    finish(begin(edges, sems))
    rows = jnp.concatenate([ups[0, EDGE_U - LEFT_U :], ups[3]], axis=0)
    value = lax.dot_general(
        rows, v_weights[...], (((1,), (1,)), ((), ())), preferred_element_type=F32
    )
    value = (value * v_slope[...]).astype(BF).astype(F32)
    wide[:LEFT_U] = value[:LEFT_U]
    wide[LEFT_U : LEFT_U + FRAMES] = v_grad[...].astype(F32)
    wide[LEFT_U + FRAMES :] = value[LEFT_U:]
    rows = 88
    for tile in range(CHANNELS // 128):

        def chunk(c, _, tile=tile):
            base = pl.multiple_of(c * rows, 8)
            total = jnp.zeros((rows, 128), F32)
            window = wide[pl.ds(base, rows + 32), lanes(tile)]
            for b in range(8):
                slab = window[b : b + rows + 24]
                for a in range(4):
                    k = TAPS - 8 * a - b
                    if 0 <= k < TAPS:
                        total += weights[k : k + 1, lanes(tile)] * slab[8 * a : 8 * a + rows]
            total_f[pl.ds(base, rows), lanes(tile)] = total
            return 0

        lax.fori_loop(0, LONG // rows, chunk, 0)
    for row in range(2):
        for out, side in ((v_kept, core), (v_given, 1 - core)):
            begin_row = pl.multiple_of((row * 2 + side) * 128, 128)
            out[row] = total_f[pl.ds(begin_row, BACK)].astype(BF)
    finish(begin([(v_kept, kept), (v_given, given)], sems))


def settle(
    kept, got, far, gathered, lengths, frame_grad, gloss, frames, notes, v_lengths, v_gloss, sems
):
    yh, core = lax.axis_index("yh"), lax.axis_index("core")
    sources = [(kept.at[yh], yh, core), (got.at[yh], yh, 1 - core)]
    sources += [(far.at[0], 1 - yh, core), (far.at[1], 1 - yh, 1 - core)]
    moves = [(lengths, v_lengths), (gathered.at[:, :, pl.ds(LANES, EXTRA)], notes)]
    for source, a, b in sources:
        cut = pl.ds(pl.multiple_of((a * 2 + b) * CHANNELS, 128), CHANNELS)
        moves.append((source, frames.at[:, cut]))
    finish(begin(moves, sems))
    out = begin([(frames.at[pl.ds(0, 128)], frame_grad)], sems)
    mine = yh * 2 + core
    place = lax.axis_index("z") * 4 + lax.axis_index("x")
    lane = lax.broadcasted_iota(jnp.int32, (8, EXTRA), 1)
    start = jnp.zeros((8, EXTRA), F32)
    for member in range(MEMBERS):
        block = lane * 16 + member // 2
        earlier = (block < place * 4 + mine) & (lane < 8) & (lax.axis_index("rep") == member % 2)
        start += jnp.where(earlier, notes[member, 6:7].astype(F32), 0.0)
    start = jnp.sum(start, axis=1, keepdims=True) - (place * FRAMES + mine * 128).astype(F32)
    gloss_id = lax.broadcasted_iota(jnp.int32, (8, EXTRA), 0)
    length = v_lengths[...]
    first = jnp.sum(jnp.where(lane < gloss_id, length, 0.0), axis=1, keepdims=True) + start
    last = first + jnp.sum(jnp.where(lane == gloss_id, length, 0.0), axis=1, keepdims=True)
    at = lax.broadcasted_iota(jnp.int32, (8, 128 + SPILL), 1).astype(F32)
    covers = jnp.where((at >= first) & (at < last), 1.0, 0.0).astype(BF)
    v_gloss[...] = jnp.dot(covers, frames[...], preferred_element_type=F32)
    finish(begin([(v_gloss, gloss)], sems.at[pl.ds(1, 1)]))
    finish(out)


def pack_z(parts, out, sems):
    sums = []
    for q in range(4):
        total = jnp.zeros((ROWS, LANES + EXTRA), F32)
        for x in range(4):
            for rep in range(2):
                total += parts[(x * 4 + q) * 2 + rep].astype(F32)
        sums.append(total)
    taps = [total[:3, LANES:] + total[3:6, LANES:] for total in sums]
    taps = jnp.concatenate([t[j : j + 1] for t in taps for j in range(3)], axis=1)
    high = taps.astype(BF).astype(F32)
    for z in range(8):
        total = sums[z // 2]
        rows = [total[:BLOCK, :1536]]
        if z % 2:
            rows = [total[BLOCK:, :1536]]
            for i in range(0, ROWS, 2):
                halves = [total[i + h : i + h + 1, 1536:LANES] for h in range(2)]
                rows.append(jnp.concatenate(halves, axis=1))
        rows += [high, taps - high]
        out[z] = jnp.concatenate(rows, axis=0).astype(BF)


def unpack_z(got, weights, taps, sems):
    total = got[0].astype(F32)
    for z in range(1, 8):
        total += got[z].astype(F32)
    total = total * (1.0 / math.sqrt(2 * 16384))
    weights[...] = total[:BLOCK]
    for peer in range(MEMBERS):
        taps[peer] = total[6:7] + total[7:8]


def arrange(got, out, v_out, sems):
    for k in range(TAPS):
        v_out[k : k + 1] = got[k]
    finish(begin([(v_out, out)], sems))


def call(
    kernel, outs, scratch, megabytes, *args, alias=None, flops=200_000_000, near=(), near_out=()
):
    def space(vmem):
        return pl.BlockSpec(memory_space=pltpu.VMEM if vmem else pltpu.HBM)

    shapes = [jax.ShapeDtypeStruct(shape, dtype) for shape, dtype in outs]
    size = sum(math.prod(s.shape) * s.dtype.itemsize for s in list(args) + shapes)
    return pl.pallas_call(
        kernel,
        out_shape=shapes,
        in_specs=[space(i in near) for i in range(len(args))],
        out_specs=[space(i in near_out) for i in range(len(shapes))],
        scratch_shapes=[pltpu.VMEM(shape, dtype) for shape, dtype in scratch]
        + [pltpu.SemaphoreType.DMA((48,))],
        input_output_aliases=alias or {},
        compiler_params=pltpu.CompilerParams(vmem_limit_bytes=megabytes * 2**20),
        cost_estimate=pl.CostEstimate(
            flops=flops, bytes_accessed=size, transcendentals=0
        ),
    )(*args)


def body(hidden_in, upstream, out_weight, conv_kernel, durations):
    yh, core = lax.axis_index("yh"), lax.axis_index("core")
    quarter = yh * 2 + core
    hidden, grads = hidden_in[0], upstream[0]
    lengths = jnp.broadcast_to(
        jnp.pad(durations.astype(F32), ((0, 0), (0, EXTRA - durations.shape[1]))), (8, EXTRA)
    )

    rows, share, edge = call(
        spread,
        [((8, 8, 1280), BF), ((384, 768), BF), ((EDGE_H + EDGE_U, 1536), BF)],
        [
            ((BLOCK, 1536), BF), ((1, 8), jnp.int32), ((8, 1280), BF), ((384, 768), BF),
            ((EDGE_H + EDGE_U, 1536), BF),
        ],
        56,
        out_weight, durations, hidden, grads,
    )
    ends = [(4 * i + 3, 4 * i + 4) for i in range(31)]
    slot = lax.ppermute(edge, ("z", "x", "yh", "core"), ends + [(b, a) for a, b in ends])
    rows = lax.all_to_all(rows, "z", 0, 0, tiled=True)
    across = lax.ppermute(share, "yh", SWAP)
    up_beside = lax.ppermute(grads, "core", SWAP)
    beyond = lax.ppermute(across, "core", SWAP)
    [lent] = call(lend, [((SHARE, 768), BF)], [((SHARE, 768), BF)], 16, slot)
    lent = lax.ppermute(lent, GROUP, [(0, 2), (3, 1)])
    message = ((MEMBERS, ROWS, LANES + EXTRA), BF)
    note = ((8, EXTRA), F32)
    plane, notes = call(
        pack,
        [((MEMBERS, ROWS, LANES), BF), note],
        [((4 * ROWS, LANES), F32), ((4, ROWS, LANES), BF), note],
        16,
        rows,
        near=(0,),
    )
    handed = ((2, 128, CHANNELS), BF)
    [beside] = call(relay, [handed], [handed], 16, hidden, across, flops=3_000_000_000)
    handed = ((2, HANDED, CHANNELS), BF)
    [edges] = call(relay_edges, [handed], [handed], 16, slot, lent, flops=30_000_000_000)
    rows = lax.all_to_all(plane, PLANE, 0, 0, tiled=True)
    beside = lax.ppermute(beside, "core", SWAP)
    edges = lax.ppermute(edges, "core", SWAP)
    kernel_f = lax.dynamic_slice_in_dim(
        jnp.pad(conv_kernel, ((0, 1), (0, 0))), quarter * CHANNELS, CHANNELS, 1
    ).astype(F32)
    spot = ((CHANNELS, MESSAGE), BF)
    spots = [placement(part) for part in range(3)]
    frames_f = ((FRAMES, CHANNELS), F32)
    wide_f = ((LEFT_H + FRAMES + EDGE_H, CHANNELS), F32)
    slope_f = ((WIDE, CHANNELS), F32)
    all_grads = ((4, 128, 1536), BF)
    sent = ((MEMBERS, ROWS, LANES), BF)
    kernel_shape = ((TAPS + 1, CHANNELS), F32)
    slope, hidden_f, parts = call(
        convolve,
        [slope_f, wide_f, message],
        [
            all_grads, ((4, 128 + EDGE_H, CHANNELS), BF), kernel_shape, spot, spot, spot, slope_f, wide_f,
            sent, slope_f,
        ],
        56,
        hidden, slot, across, lent, beside, edges, grads, up_beside, beyond, kernel_f, *spots,
    )
    grad_conv, projection, parts = call(
        backward,
        [
            ((FRAMES, CHANNELS), BF), ((CHANNELS, 1536), BF), message,
        ],
        [
            sent, note, spot, spot, spot, all_grads, frames_f, wide_f, ((FRAMES, CHANNELS), BF), frames_f,
            ((MEMBERS, ROWS, EXTRA), BF), ((TAPS + 1, 8, CHANNELS), F32),
            ((CHANNELS, 1536), BF),
        ],
        56,
        rows, notes, *spots, grads, across, up_beside, beyond, slope, hidden_f, parts,
        alias={11: 2},
    )

    summed = parts = lax.all_to_all(parts, PLANE, 0, 0, tiled=True)
    [parts] = call(
        pack_z,
        [((8, 8, 1536), BF)],
        [],
        16,
        parts,
        near=(0,),
        near_out=(0,),
    )
    parts = lax.all_to_all(parts, "z", 0, 0, tiled=True)
    weight_grad, taps_all = call(
        unpack_z,
        [((BLOCK, 1536), F32), ((32, 1, 1536), F32)],
        [],
        16,
        parts,
        near=(0,),
        near_out=(0, 1),
    )
    taps_all = lax.all_to_all(taps_all, PLANE, 0, 0, tiled=True)
    [kernel_grad] = call(
        arrange,
        [((TAPS, 1536), F32)],
        [((TAPS, 1536), F32)],
        16,
        taps_all,
        near=(0,),
    )

    back = ((2, BACK, CHANNELS), BF)
    kept, given = call(
        transposed,
        [back, back],
        [
            ((FRAMES, CHANNELS), BF), ((CHANNELS, 1536), BF), ((LEFT_U + EDGE_U, CHANNELS), F32),
            ((4, EDGE_U, 1536), BF), kernel_shape,
            slope_f, ((LONG, CHANNELS), F32), back, back,
        ],
        56,
        grad_conv, projection, slope, slot, lent, edges, kernel_f,
    )
    got = lax.ppermute(given, "core", SWAP)
    far = jnp.stack(
        [lax.dynamic_index_in_dim(part, 1 - yh, 0, False) for part in (kept, got)]
    )
    far = lax.ppermute(far, "yh", SWAP)
    frame_grad, gloss = call(
        settle,
        [((128, 1536), BF), ((8, 1536), F32)],
        [
            ((BACK, 1536), BF), ((MEMBERS, ROWS, EXTRA), BF), ((8, EXTRA), F32),
            ((8, 1536), F32),
        ],
        16,
        kept, got, far, summed, lengths,
    )
    return (frame_grad[None], gloss[None], weight_grad, kernel_grad)


def solution(mesh):
    fine = Mesh(mesh.devices.reshape(SIZES), AXES)
    seq = ("z", "x", "yh", "core")
    rows = P(seq + ("rep",), None)
    in_specs = (P("rep", seq, None), P("rep", seq, None), rows, P(), P("rep", seq))
    out_specs = (P("rep", seq, None), P("rep", seq, None), rows, P())
    return jax.shard_map(
        body, mesh=fine, in_specs=in_specs, out_specs=out_specs, check_vma=False
    )
```
